32 devices in a mesh: fsdp: 4 (over y, x), seq: 8 (over z, core).
Axes of the slice: x: 2, y: 2, z: 4, core: 2. Of those that a mesh axis runs over, the one named last changes fastest.
Arguments:
- tokens: bfloat16 [4, 1024, 1600], P('fsdp', 'seq'), may hold values from -6 to 6
- segment_ids: int32 [4, 1024], P('fsdp', 'seq'), may hold values from 0 to 7, never falling along the last dimension, each value on 1 to 512 neighbouring positions
- cotangent: bfloat16 [4, 1024, 1600], P('fsdp', 'seq'), may hold values from -6 to 6
- qkv_weight: bfloat16 [1600, 4800], P('fsdp', 'seq'), may hold values from -0.15625 to 0.15625
- attn_out_weight: bfloat16 [1600, 1600], P('fsdp', 'seq'), may hold values from -1.25 to 1.25
- fc_weight: bfloat16 [1600, 6400], P(None, ('fsdp', 'seq')), may hold values from -0.15625 to 0.15625
- proj_weight: bfloat16 [6400, 1600], P(('fsdp', 'seq')), may hold values from -0.078125 to 0.078125
- vectors: bfloat16 [8, 1600], P('fsdp', 'seq'), may hold values from -1.5 to 1.5
- fc_bias: bfloat16 [6400], P(('fsdp', 'seq')), may hold values from -2 to 2
Outputs:
- output: float32 [4, 1024, 1600], P('fsdp', 'seq')
- input_grad: float32 [4, 1024, 1600], P('fsdp', 'seq')
- grad_qkv: float32 [1600, 4800], P('fsdp', 'seq')
- grad_attn_out: float32 [1600, 1600], P('fsdp', 'seq')
- grad_fc: float32 [1600, 6400], P(None, ('fsdp', 'seq'))
- grad_proj: float32 [6400, 1600], P(('fsdp', 'seq'))
- grad_vectors: float32 [8, 1600], P('fsdp', 'seq')
- grad_fc_bias: float32 [6400], P(('fsdp', 'seq'))
The draws below stay inside these ranges and needn't reach their ends.
Inputs may be any that keep to these rules, and one draw needn't show every extreme that they name: `segment_ids`: along each sequence the ids never fall, and each document holds at most 512 tokens.
All inputs are finite; a program needn't handle non-finite values.
Results may differ from the reference program's by a relative error of at most 0.019.
Values may be sent and summed in bfloat16 or wider, within the bound.
A program may use at most 384 MiB of HBM per device.

```python
import math
import jax
import jax.numpy as jnp
import numpy as np
from jax import lax

D = 1600
HEADS = 25
HEAD_DIM = 64
FF = 6400
DOCS = 8
SEQ_LEN = 1024
GROUPS = 4
DOC_MOST = 512


def draw_vectors(key, part):
    gain_key, shift_key = jax.random.split(jax.random.fold_in(key, 11))
    gains = jnp.clip(1.0 + 0.15 * jax.random.normal(gain_key, (8, D), jnp.float32), 0.5, 1.5)
    shifts = jnp.clip(0.5 * jax.random.normal(shift_key, (8, D), jnp.float32), -1.5, 1.5)
    row_index = lax.broadcasted_iota(jnp.int32, (8, D), 0)
    gain_rows = (row_index == 0) | (row_index == 5)
    return jnp.where(gain_rows, gains, shifts).astype(jnp.bfloat16)


def shard_levels(rng, shape, cuts, low, largest):
    def one(axis_at, blocks):
        steps = jax.random.uniform(jax.random.fold_in(jax.random.fold_in(rng, 6), axis_at), (blocks,), jnp.float32, low / len(cuts), largest / len(cuts))
        return jnp.repeat(jnp.exp(steps), shape[axis_at] // blocks).reshape((-1,) + (1,) * (len(shape) - axis_at - 1))

    level = one(*cuts[0])
    for cut in cuts[1:]:
        level = level * one(*cut)
    return level


def profile(count, total, reach, slope):
    weights = [(1 << 20) // math.isqrt(standing ** slope) + 1 for standing in range(2, count + 1)]
    rest, given = total - reach - (count - 1), [1] * (count - 1)
    while rest > 0:
        free = [i for i in range(count - 1) if given[i] < reach]
        pool, left = sum([weights[i] for i in free]), rest
        for i in free:
            addition = min(reach - given[i], max(1, left * weights[i] // pool), rest)
            given[i] = given[i] + addition
            rest = rest - addition
    return np.array([reach] + given)


def uneven(key, amount, total, reach, slope):
    if amount == 2:
        one = jax.random.randint(key, (), max(1, total - reach), min(reach, total - 1) + 1)
        return jnp.stack([one, total - one])
    tallies = jnp.asarray(profile(amount, total, reach, slope), jnp.int32)
    pairs = (amount - 1) // 2
    donor, sink = tallies[1:1 + 2 * pairs:2], tallies[2:2 + 2 * pairs:2]
    slack = jnp.minimum(donor - 1, reach - sink)
    moved = jax.random.randint(jax.random.fold_in(key, 1), (pairs,), 0, 1 << 20) % (slack + 1)
    tallies = tallies.at[1:1 + 2 * pairs:2].set(donor - moved).at[2:2 + 2 * pairs:2].set(sink + moved)
    return tallies[jax.random.permutation(jax.random.fold_in(key, 2), amount)]


def normal_values(key, extent, scale, reach, pieces=(), held_as=jnp.bfloat16):
    values = scale * jax.random.normal(key, extent, jnp.float32)
    if pieces:
        values = values * shard_levels(key, extent, pieces, -0.22, 0.18)
    return jnp.clip(values, -reach, reach).astype(held_as)


def setup_inputs(seed: int = 0) -> dict:
    keys = jax.random.split(jax.random.key(seed), 10)
    tokens = normal_values(keys[0], (GROUPS, SEQ_LEN, D), 1.0, 6.0, ((0, 4), (1, 8)))
    segment_ids = jax.vmap(lambda own: jnp.searchsorted(jnp.cumsum(uneven(own, DOCS, SEQ_LEN, DOC_MOST, 1)), jnp.arange(SEQ_LEN), side="right"))(jax.random.split(keys[1], GROUPS)).reshape((GROUPS, SEQ_LEN)).astype(jnp.int32)
    cotangent = normal_values(keys[2], (GROUPS, SEQ_LEN, D), 1.0, 6.0, ((0, 4), (1, 8)))
    qkv_weight = normal_values(keys[3], (D, 3 * D), D ** -0.5, 0.15625, ((0, 4), (1, 8)))
    attn_out_weight = normal_values(keys[4], (D, D), (max(16 * D // SEQ_LEN, 1)) ** -0.5, 1.25, ((0, 4), (1, 8)))
    fc_weight = normal_values(keys[5], (D, FF), D ** -0.5, 0.15625, ((1, 32),))
    proj_weight = normal_values(keys[6], (FF, D), FF ** -0.5, 0.078125, ((0, 32),))
    vectors = draw_vectors(jax.random.fold_in(keys[9], 71), 0)
    fc_bias = normal_values(keys[8], (FF,), 0.5, 2.0, ((0, 32),))
    return {"tokens": tokens, "segment_ids": segment_ids, "cotangent": cotangent, "qkv_weight": qkv_weight, "attn_out_weight": attn_out_weight, "fc_weight": fc_weight, "proj_weight": proj_weight, "vectors": vectors, "fc_bias": fc_bias}


norm_eps = 1e-05
tanh_coeff = math.sqrt(2.0 / math.pi)
cubic_coeff = 0.044715
masked_score = -1e+30

def layer_norm(values, gain, shift):
    centred = values - lax.optimization_barrier(jnp.mean(values, axis=-1, keepdims=True))
    inverse = lax.rsqrt(lax.optimization_barrier(jnp.mean(centred * centred, axis=-1, keepdims=True)) + norm_eps)
    normed = centred * inverse
    return (normed, inverse, normed * gain + shift)

def norm_back(grad_out, normed, inverse, gain):
    scaled = grad_out * gain
    grad_in = inverse * (scaled - lax.optimization_barrier(jnp.mean(scaled, axis=-1, keepdims=True)) - normed * lax.optimization_barrier(jnp.mean(scaled * normed, axis=-1, keepdims=True)))
    return (grad_in, lax.optimization_barrier(jnp.sum(grad_out * normed, axis=0)), lax.optimization_barrier(jnp.sum(grad_out, axis=0)))

def gelu_parts(preact):
    inner = tanh_coeff * (preact + cubic_coeff * preact * preact * preact)
    tangent = jnp.tanh(inner)
    gelu_value = 0.5 * preact * (1.0 + tangent)
    gelu_slope = 0.5 * (1.0 + tangent) + 0.5 * preact * (1.0 - tangent * tangent) * tanh_coeff * (1.0 + 3.0 * cubic_coeff * preact * preact)
    return (gelu_value, gelu_slope)

def reference(tokens, segment_ids, cotangent, qkv_weight, attn_out_weight, fc_weight, proj_weight, vectors, fc_bias):
    vector_rows = vectors.astype(jnp.float32)
    fc_shift = fc_bias.astype(jnp.float32)
    width = qkv_weight.shape[0]
    score_scale = HEAD_DIM ** (-0.5)

    def one_sequence(totals, sequence_items):
        inputs_bf, seq_ids, grad_out_bf = sequence_items
        length = inputs_bf.shape[0]
        inputs = inputs_bf.astype(jnp.float32)
        positions = lax.iota(jnp.int32, length)
        allowed = (positions[None, :] <= positions[:, None]) & (seq_ids[None, :] == seq_ids[:, None])
        normed1, inverse1, shifted1 = layer_norm(inputs, vector_rows[0], vector_rows[1])
        hidden1 = shifted1.astype(jnp.bfloat16)
        projected = jnp.dot(hidden1, qkv_weight, preferred_element_type=jnp.float32)
        queries = (projected[:, :width] + vector_rows[2]).astype(jnp.bfloat16)
        keys_all = projected[:, width:2 * width].astype(jnp.bfloat16)
        values_all = (projected[:, 2 * width:] + vector_rows[3]).astype(jnp.bfloat16)

        def split_heads(matrix):
            return matrix.reshape(length, HEADS, HEAD_DIM).transpose(1, 0, 2)
        query_heads = split_heads(queries)
        key_heads = split_heads(keys_all)
        value_heads = split_heads(values_all)

        def head_forward(head_items):
            query_head, key_head, value_head = head_items
            scores = jnp.dot(query_head, key_head.T, preferred_element_type=jnp.float32) * score_scale
            masked = jnp.where(allowed, scores, masked_score)
            top_score = lax.optimization_barrier(jnp.max(masked, axis=1, keepdims=True))
            total = lax.optimization_barrier(jnp.sum(jnp.where(allowed, jnp.exp(masked - top_score), 0.0), axis=1, keepdims=True))
            log_total = top_score + jnp.log(total)
            probs = jnp.where(allowed, jnp.exp(scores - log_total), 0.0).astype(jnp.bfloat16)
            head_out = jnp.dot(probs, value_head, preferred_element_type=jnp.float32).astype(jnp.bfloat16)
            return (head_out, log_total[:, 0])
        attn_heads, log_totals = lax.map(head_forward, (query_heads, key_heads, value_heads))
        attn_bf = attn_heads.transpose(1, 0, 2).reshape(length, width)
        resid = inputs + jnp.dot(attn_bf, attn_out_weight, preferred_element_type=jnp.float32) + vector_rows[4]
        normed2, inverse2, shifted2 = layer_norm(resid, vector_rows[5], vector_rows[6])
        hidden2 = shifted2.astype(jnp.bfloat16)
        preact = jnp.dot(hidden2, fc_weight, preferred_element_type=jnp.float32) + fc_shift
        gelu_value, gelu_slope = gelu_parts(preact)
        act_bf = gelu_value.astype(jnp.bfloat16)
        result = resid + jnp.dot(act_bf, proj_weight, preferred_element_type=jnp.float32) + vector_rows[7]
        grad_out = grad_out_bf.astype(jnp.float32)
        grad_proj = jnp.dot(act_bf.T, grad_out_bf, preferred_element_type=jnp.float32)
        grad_act = jnp.dot(grad_out_bf, proj_weight.T, preferred_element_type=jnp.float32)
        grad_pre = grad_act * gelu_slope
        grad_pre_bf = grad_pre.astype(jnp.bfloat16)
        grad_fc = jnp.dot(hidden2.T, grad_pre_bf, preferred_element_type=jnp.float32)
        grad_hidden2 = jnp.dot(grad_pre_bf, fc_weight.T, preferred_element_type=jnp.float32)
        grad_resid_norm, gain2_grad, shift2_grad = norm_back(grad_hidden2, normed2, inverse2, vector_rows[5])
        grad_resid = grad_out + grad_resid_norm
        grad_resid_bf = grad_resid.astype(jnp.bfloat16)
        grad_attn_out = jnp.dot(attn_bf.T, grad_resid_bf, preferred_element_type=jnp.float32)
        grad_attn_bf = jnp.dot(grad_resid_bf, attn_out_weight.T, preferred_element_type=jnp.float32).astype(jnp.bfloat16)
        grad_heads = split_heads(grad_attn_bf)

        def head_backward(head_items):
            query_head, key_head, value_head, out_head, grad_head, log_total = head_items
            scores = jnp.dot(query_head, key_head.T, preferred_element_type=jnp.float32) * score_scale
            probs = jnp.where(allowed, jnp.exp(scores - log_total[:, None]), 0.0)
            probs_bf = probs.astype(jnp.bfloat16)
            value_grad = jnp.dot(probs_bf.T, grad_head, preferred_element_type=jnp.float32)
            prob_grad = jnp.dot(grad_head, value_head.T, preferred_element_type=jnp.float32)
            delta = lax.optimization_barrier(jnp.sum(grad_head.astype(jnp.float32) * out_head.astype(jnp.float32), axis=1, keepdims=True))
            score_grad = (probs * (prob_grad - delta)).astype(jnp.bfloat16)
            query_grad = score_scale * jnp.dot(score_grad, key_head, preferred_element_type=jnp.float32)
            key_grad = score_scale * jnp.dot(score_grad.T, query_head, preferred_element_type=jnp.float32)
            return (query_grad, key_grad, value_grad)
        query_grads, key_grads, value_grads = lax.map(head_backward, (query_heads, key_heads, value_heads, attn_heads, grad_heads, log_totals))

        def merge_heads(stacked):
            return stacked.transpose(1, 0, 2).reshape(length, width)
        query_grad = merge_heads(query_grads)
        key_grad = merge_heads(key_grads)
        value_grad = merge_heads(value_grads)
        grad_qkv_bf = jnp.concatenate([query_grad, key_grad, value_grad], axis=1).astype(jnp.bfloat16)
        grad_qkv = jnp.dot(hidden1.T, grad_qkv_bf, preferred_element_type=jnp.float32)
        grad_hidden1 = jnp.dot(grad_qkv_bf, qkv_weight.T, preferred_element_type=jnp.float32)
        grad_input_norm, gain1_grad, shift1_grad = norm_back(grad_hidden1, normed1, inverse1, vector_rows[0])
        input_grad = grad_resid + grad_input_norm
        vector_grad = jnp.stack([gain1_grad, shift1_grad, lax.optimization_barrier(jnp.sum(query_grad, axis=0)), lax.optimization_barrier(jnp.sum(value_grad, axis=0)), lax.optimization_barrier(jnp.sum(grad_resid, axis=0)), gain2_grad, shift2_grad, lax.optimization_barrier(jnp.sum(grad_out, axis=0))])
        terms = (grad_qkv, grad_attn_out, grad_fc, grad_proj, vector_grad, lax.optimization_barrier(jnp.sum(grad_pre, axis=0)))
        totals = jax.tree.map(lambda left, right: left + right, totals, terms)
        return (totals, (result, input_grad))
    initial = (jnp.zeros(qkv_weight.shape, jnp.float32), jnp.zeros(attn_out_weight.shape, jnp.float32), jnp.zeros(fc_weight.shape, jnp.float32), jnp.zeros(proj_weight.shape, jnp.float32), jnp.zeros(vectors.shape, jnp.float32), jnp.zeros(fc_bias.shape, jnp.float32))
    totals, outputs = lax.scan(one_sequence, initial, (tokens, segment_ids, cotangent))
    return (outputs[0], outputs[1], totals[0], totals[1], totals[2], totals[3], totals[4], totals[5])
```

```python
import math

import jax
import jax.numpy as jnp
from jax import lax
from jax.experimental import pallas as pl
from jax.experimental.pallas import tpu as pltpu
from jax.sharding import PartitionSpec as P

HEADS = 25
HEAD_DIM = 64


norm_eps = 1e-05
tanh_coeff = math.sqrt(2.0 / math.pi)
cubic_coeff = 0.044715
masked_score = -1e30


def layer_norm(values, gain, shift):
    centred = values - jnp.mean(values, axis=-1, keepdims=True)
    inverse = lax.rsqrt(jnp.mean(centred * centred, axis=-1, keepdims=True) + norm_eps)
    normed = centred * inverse
    return (normed, inverse, normed * gain + shift)


def norm_back(grad_out, normed, inverse, gain):
    scaled = grad_out * gain
    grad_in = inverse * (
        scaled
        - jnp.mean(scaled, axis=-1, keepdims=True)
        - normed * jnp.mean(scaled * normed, axis=-1, keepdims=True)
    )
    return (grad_in, jnp.sum(grad_out * normed, axis=0), jnp.sum(grad_out, axis=0))


def gelu_parts(preact):
    inner = tanh_coeff * (preact + cubic_coeff * preact * preact * preact)
    tangent = jnp.tanh(inner)
    gelu_value = 0.5 * preact * (1.0 + tangent)
    gelu_slope = 0.5 * (1.0 + tangent) + 0.5 * preact * (1.0 - tangent * tangent) * tanh_coeff * (
        1.0 + 3.0 * cubic_coeff * preact * preact
    )
    return (gelu_value, gelu_slope)


def block_rows():
    return 512


def gather_owned(matrix_qkv, matrix_attn, matrix_fc, matrix_proj, vector_part, bias_part):
    return (
        lax.all_gather(matrix_qkv, "fsdp", axis=0, tiled=True),
        lax.all_gather(matrix_attn, "fsdp", axis=0, tiled=True),
        lax.all_gather(matrix_fc, "fsdp", axis=1, tiled=True),
        lax.all_gather(matrix_proj, "fsdp", axis=0, tiled=True),
        lax.all_gather(vector_part, "fsdp", axis=0, tiled=True),
        lax.all_gather(bias_part, "fsdp", axis=0, tiled=True),
    )


def gather_attention(matrix_qkv, matrix_attn, vector_part, id_part):
    return (
        lax.all_gather(matrix_qkv, "seq", axis=1, tiled=True),
        lax.all_gather(matrix_attn, "seq", axis=1, tiled=True),
        lax.all_gather(vector_part, "seq", axis=1, tiled=True),
        lax.all_gather(id_part, "seq", axis=0, tiled=True),
    )


def gathered_weights(
    tokens,
    segment_ids,
    cotangent,
    qkv_weight,
    attn_out_weight,
    fc_weight,
    proj_weight,
    vectors,
    fc_bias,
):
    width = tokens.shape[2]
    local_rows = tokens.shape[1]
    heads = HEADS
    head_width = HEAD_DIM
    score_scale = head_width ** (-0.5)
    own_index = lax.axis_index("seq")
    inputs_bf = tokens[0]
    inputs = inputs_bf.astype(jnp.float32)
    doc_ids = segment_ids[0].astype(jnp.bfloat16)
    grad_out_bf = cotangent[0]
    owned = gather_owned(qkv_weight, attn_out_weight, fc_weight, proj_weight, vectors, fc_bias)
    w_qkv, w_attn, vector_bf, ids_all = gather_attention(owned[0], owned[1], owned[4], doc_ids)

    def gather_feedforward(matrix_fc, matrix_proj, bias_part):
        return (
            lax.all_gather(matrix_fc, "seq", axis=1, tiled=True),
            lax.all_gather(matrix_proj, "seq", axis=0, tiled=True),
            lax.all_gather(bias_part, "seq", axis=0, tiled=True),
        )

    w_fc, w_proj, bias_units = gather_feedforward(owned[2], owned[3], owned[5])
    vector_rows = vector_bf.astype(jnp.float32)
    fc_shift = bias_units.astype(jnp.float32)
    normed1, inverse1, shifted1 = layer_norm(inputs, vector_rows[0], vector_rows[1])
    hidden1 = shifted1.astype(jnp.bfloat16)
    projected = jnp.dot(hidden1, w_qkv, preferred_element_type=jnp.float32)
    queries = (projected[:, :width] + vector_rows[2]).astype(jnp.bfloat16)
    keys_own = projected[:, width : 2 * width].astype(jnp.bfloat16)
    values_own = (projected[:, 2 * width :] + vector_rows[3]).astype(jnp.bfloat16)
    query_heads = queries.reshape(local_rows, heads, head_width)
    positions = own_index * local_rows + lax.iota(jnp.int32, local_rows)

    def scores_for(key_block, ids_block, pos_block):
        scores = (
            jnp.einsum("qhd,khd->hqk", query_heads, key_block, preferred_element_type=jnp.float32)
            * score_scale
        )
        allowed = (
            (pos_block[None, :] <= positions[:, None])
            & (pos_block[None, :] >= 0)
            & (ids_block[None, :] == doc_ids[:, None])
        )
        return (scores, allowed)

    def stat_step(running, block_items):
        running_max, running_sum = running
        key_block, value_block, ids_block, pos_block = block_items
        scores, allowed = scores_for(key_block, ids_block, pos_block)
        masked = jnp.where(allowed[None], scores, masked_score)
        new_max = jnp.maximum(running_max, jnp.max(masked, axis=2))
        fading = jnp.exp(running_max - new_max)
        weights = jnp.where(allowed[None], jnp.exp(masked - new_max[:, :, None]), 0.0)
        running_sum = running_sum * fading + jnp.sum(weights, axis=2)
        return ((new_max, running_sum), None)

    initial = (
        jnp.full((heads, local_rows), masked_score, jnp.float32),
        jnp.zeros((heads, local_rows), jnp.float32),
    )
    keys_all, values_all = (
        lax.all_gather(keys_own, "seq", axis=0, tiled=True),
        lax.all_gather(values_own, "seq", axis=0, tiled=True),
    )
    key_count = keys_all.shape[0]
    step_rows = block_rows()
    blocks = key_count // step_rows
    key_items = (
        keys_all.reshape(blocks, step_rows, heads, head_width),
        values_all.reshape(blocks, step_rows, heads, head_width),
        ids_all.reshape(blocks, step_rows),
        lax.iota(jnp.int32, key_count).reshape(blocks, step_rows),
    )
    running, _ = lax.scan(stat_step, initial, key_items)
    final_max, final_sum = running
    log_total = final_max + jnp.log(final_sum)

    def weigh_step(total, block_items):
        key_block, value_block, ids_block, pos_block = block_items
        scores, allowed = scores_for(key_block, ids_block, pos_block)
        probs_bf = jnp.where(allowed[None], jnp.exp(scores - log_total[:, :, None]), 0.0).astype(
            jnp.bfloat16
        )
        return (
            total
            + jnp.einsum("hqk,khd->hqd", probs_bf, value_block, preferred_element_type=jnp.float32),
            None,
        )

    final_acc, _ = lax.scan(
        weigh_step, jnp.zeros((heads, local_rows, head_width), jnp.float32), key_items
    )
    attn_bf = final_acc.astype(jnp.bfloat16).transpose(1, 0, 2).reshape(local_rows, width)
    resid = inputs + jnp.dot(attn_bf, w_attn, preferred_element_type=jnp.float32) + vector_rows[4]
    normed2, inverse2, shifted2 = layer_norm(resid, vector_rows[5], vector_rows[6])
    hidden2 = shifted2.astype(jnp.bfloat16)
    preact = jnp.dot(hidden2, w_fc, preferred_element_type=jnp.float32) + fc_shift
    gelu_value, gelu_slope = gelu_parts(preact)
    act_bf = gelu_value.astype(jnp.bfloat16)
    mlp_out = jnp.dot(act_bf, w_proj, preferred_element_type=jnp.float32)
    result = resid + mlp_out + vector_rows[7]
    fenced = lax.optimization_barrier(
        (qkv_weight, attn_out_weight, fc_weight, proj_weight, vectors, fc_bias, doc_ids, result)
    )
    owned_again = gather_owned(fenced[0], fenced[1], fenced[2], fenced[3], fenced[4], fenced[5])
    back_qkv, back_attn, back_vec_bf, ids_again = gather_attention(
        owned_again[0], owned_again[1], owned_again[4], fenced[6]
    )
    back_fc, back_proj, bias_again = gather_feedforward(
        owned_again[2], owned_again[3], owned_again[5]
    )
    back_vec = back_vec_bf.astype(jnp.float32)
    grad_out = grad_out_bf.astype(jnp.float32)
    grad_proj_full = jnp.einsum(
        "tf,td->fd", act_bf, grad_out_bf, preferred_element_type=jnp.float32
    )
    grad_act = jnp.einsum("td,fd->tf", grad_out_bf, back_proj, preferred_element_type=jnp.float32)
    grad_pre = grad_act * gelu_slope
    grad_pre_bf = grad_pre.astype(jnp.bfloat16)
    grad_fc_full = jnp.einsum("td,tf->df", hidden2, grad_pre_bf, preferred_element_type=jnp.float32)
    grad_hidden2 = jnp.einsum("tf,df->td", grad_pre_bf, back_fc, preferred_element_type=jnp.float32)
    bias_full = jnp.sum(grad_pre, axis=0)
    part_fc, part_proj, part_bias = (
        lax.psum_scatter(
            grad_fc_full.astype(jnp.bfloat16), "seq", scatter_dimension=1, tiled=True
        ).astype(jnp.float32),
        lax.psum_scatter(
            grad_proj_full.astype(jnp.bfloat16), "seq", scatter_dimension=0, tiled=True
        ).astype(jnp.float32),
        lax.psum_scatter(
            bias_full.astype(jnp.bfloat16), "seq", scatter_dimension=0, tiled=True
        ).astype(jnp.float32),
    )
    grad_resid_norm, gain2_grad, shift2_grad = norm_back(
        grad_hidden2, normed2, inverse2, back_vec[5]
    )
    grad_resid = grad_out + grad_resid_norm
    grad_resid_bf = grad_resid.astype(jnp.bfloat16)
    grad_attn_out_full = jnp.einsum(
        "tc,td->cd", attn_bf, grad_resid_bf, preferred_element_type=jnp.float32
    )
    grad_attn_bf = jnp.einsum(
        "td,cd->tc", grad_resid_bf, back_attn, preferred_element_type=jnp.float32
    ).astype(jnp.bfloat16)
    grad_heads = grad_attn_bf.reshape(local_rows, heads, head_width)
    attn_heads = attn_bf.reshape(local_rows, heads, head_width)
    delta = jnp.sum(grad_heads.astype(jnp.float32) * attn_heads.astype(jnp.float32), axis=2).T

    def back_step(grad_query, block_items):
        key_block, value_block, ids_block, pos_block = block_items
        scores, allowed = scores_for(key_block, ids_block, pos_block)
        probs = jnp.where(allowed[None], jnp.exp(scores - log_total[:, :, None]), 0.0)
        probs_bf = probs.astype(jnp.bfloat16)
        value_grad = jnp.einsum(
            "hqk,qhd->khd", probs_bf, grad_heads, preferred_element_type=jnp.float32
        )
        prob_grad = jnp.einsum(
            "qhd,khd->hqk", grad_heads, value_block, preferred_element_type=jnp.float32
        )
        score_grad = (probs * (prob_grad - delta[:, :, None])).astype(jnp.bfloat16)
        grad_query = grad_query + score_scale * jnp.einsum(
            "hqk,khd->qhd", score_grad, key_block, preferred_element_type=jnp.float32
        )
        key_grad = score_scale * jnp.einsum(
            "hqk,qhd->khd", score_grad, query_heads, preferred_element_type=jnp.float32
        )
        return (grad_query, (key_grad, value_grad))

    query_zero = jnp.zeros((local_rows, heads, head_width), jnp.float32)
    grad_query, stacked_grads = lax.scan(back_step, query_zero, key_items)
    key_terms = stacked_grads[0].reshape(key_count, width)
    value_terms = stacked_grads[1].reshape(key_count, width)
    key_own_grad, value_own_grad = (
        lax.psum_scatter(
            key_terms.astype(jnp.bfloat16), "seq", scatter_dimension=0, tiled=True
        ).astype(jnp.float32),
        lax.psum_scatter(
            value_terms.astype(jnp.bfloat16), "seq", scatter_dimension=0, tiled=True
        ).astype(jnp.float32),
    )
    query_grad = grad_query.reshape(local_rows, width)
    grad_qkv_bf = jnp.concatenate([query_grad, key_own_grad, value_own_grad], axis=1).astype(
        jnp.bfloat16
    )
    grad_qkv_full = jnp.einsum(
        "td,te->de", hidden1, grad_qkv_bf, preferred_element_type=jnp.float32
    )
    grad_hidden1 = jnp.einsum(
        "te,de->td", grad_qkv_bf, back_qkv, preferred_element_type=jnp.float32
    )
    grad_input_norm, gain1_grad, shift1_grad = norm_back(
        grad_hidden1, normed1, inverse1, back_vec[0]
    )
    input_grad = grad_resid + grad_input_norm
    vector_grad = jnp.stack(
        [
            gain1_grad,
            shift1_grad,
            jnp.sum(query_grad, axis=0),
            jnp.sum(value_own_grad, axis=0),
            jnp.sum(grad_resid, axis=0),
            gain2_grad,
            shift2_grad,
            jnp.sum(grad_out, axis=0),
        ]
    )
    part_qkv, part_attn, part_vec = (
        lax.psum_scatter(
            grad_qkv_full.astype(jnp.bfloat16), "seq", scatter_dimension=1, tiled=True
        ).astype(jnp.float32),
        lax.psum_scatter(
            grad_attn_out_full.astype(jnp.bfloat16), "seq", scatter_dimension=1, tiled=True
        ).astype(jnp.float32),
        lax.psum_scatter(
            vector_grad.astype(jnp.bfloat16), "seq", scatter_dimension=1, tiled=True
        ).astype(jnp.float32),
    )
    own_qkv, own_attn, own_fc, own_proj, own_vec, own_bias = (
        lax.psum_scatter(
            part_qkv.astype(jnp.bfloat16), "fsdp", scatter_dimension=0, tiled=True
        ).astype(jnp.float32),
        lax.psum_scatter(
            part_attn.astype(jnp.bfloat16), "fsdp", scatter_dimension=0, tiled=True
        ).astype(jnp.float32),
        lax.psum_scatter(
            part_fc.astype(jnp.bfloat16), "fsdp", scatter_dimension=1, tiled=True
        ).astype(jnp.float32),
        lax.psum_scatter(
            part_proj.astype(jnp.bfloat16), "fsdp", scatter_dimension=0, tiled=True
        ).astype(jnp.float32),
        lax.psum_scatter(
            part_vec.astype(jnp.bfloat16), "fsdp", scatter_dimension=0, tiled=True
        ).astype(jnp.float32),
        lax.psum_scatter(
            part_bias.astype(jnp.bfloat16), "fsdp", scatter_dimension=0, tiled=True
        ).astype(jnp.float32),
    )
    return (result[None], input_grad[None], own_qkv, own_attn, own_fc, own_proj, own_vec, own_bias)


resident_most = 2 * 1024 * 1024


def contract_last(left, right):
    return lax.dot_general(left, right, (((1,), (1,)), ((), ())), preferred_element_type=jnp.float32)


def contract_first(left, right):
    return lax.dot_general(left, right, (((0,), (0,)), ((), ())), preferred_element_type=jnp.float32)


def head_lanes(head, shape):
    lane = lax.broadcasted_iota(jnp.int32, shape, 1)
    return (lane >= head * HEAD_DIM) & (lane < (head + 1) * HEAD_DIM)


def only_head(values, head):
    return jnp.where(head_lanes(head, values.shape), values, jnp.zeros_like(values))


def tile_pairs(length, tile, reach):
    for start in range(0, length, tile):
        first = max(0, (start - reach) // tile * tile)
        yield start, first, start + tile - first


def allowed_pairs(ids_col, ids_row, start, first, tile, count):
    q_pos = start + lax.broadcasted_iota(jnp.int32, (tile, count), 0)
    k_pos = first + lax.broadcasted_iota(jnp.int32, (tile, count), 1)
    return (k_pos <= q_pos) & (ids_col[start : start + tile, :1] == ids_row[:1, first : first + count])


def attention_backward_kernel(
    tile, reach, qkv_ref, attn_ref, grad_ref, lse_ref, ids_col, ids_row, out_ref
):
    head = pl.program_id(0)
    length, span = attn_ref.shape
    scale = HEAD_DIM**-0.5

    @pl.when(head == 0)
    def _():
        out_ref[...] = jnp.zeros_like(out_ref)

    for start, first, count in tile_pairs(length, tile, reach):
        rows, keys = pl.ds(start, tile), pl.ds(first, count)
        query = only_head(qkv_ref[rows, :span], head)
        key = qkv_ref[keys, span : 2 * span]
        grad = only_head(grad_ref[rows, :], head)
        delta = jnp.sum(
            grad.astype(jnp.float32) * attn_ref[rows, :].astype(jnp.float32), axis=1, keepdims=True
        )
        scores = contract_last(query, key) * scale
        allowed = allowed_pairs(ids_col, ids_row, start, first, tile, count)
        probs = jnp.where(allowed, jnp.exp(scores - lse_ref[0, rows, :]), 0.0)
        prob_grad = contract_last(grad, qkv_ref[keys, 2 * span :])
        score_grad = (probs * (prob_grad - delta)).astype(jnp.bfloat16)
        out_ref[rows, :span] += scale * jnp.dot(
            score_grad, only_head(key, head), preferred_element_type=jnp.float32
        )
        out_ref[keys, span : 2 * span] += scale * contract_first(score_grad, query)
        out_ref[keys, 2 * span :] += contract_first(probs.astype(jnp.bfloat16), grad)


def whole(shape):
    return pl.BlockSpec(shape, lambda head: (0,) * len(shape))


def per_head(shape):
    return pl.BlockSpec((1,) + shape, lambda head: (head,) + (0,) * len(shape))


def attention_backward(qkv, attn, grad, lse, ids_col, ids_row, reach):
    length, span = attn.shape
    tile = min(256, length)
    return pl.pallas_call(
        lambda *refs: attention_backward_kernel(tile, reach, *refs),
        grid=(lse.shape[0],),
        in_specs=[
            whole(qkv.shape),
            whole(attn.shape),
            whole(grad.shape),
            per_head((length, 1)),
            whole(ids_col.shape),
            whole(ids_row.shape),
        ],
        out_specs=whole(qkv.shape),
        out_shape=jax.ShapeDtypeStruct(qkv.shape, jnp.float32),
        compiler_params=pltpu.CompilerParams(vmem_limit_bytes=48 * 1024 * 1024),
    )(qkv, attn, grad, lse, ids_col, ids_row)


def join_seq(block, axis=0):
    return lax.all_gather(block, "seq", axis=axis, tiled=True)


def join_fsdp(block, axis=0):
    return lax.all_gather(block, "fsdp", axis=axis, tiled=True)


def sum_seq(terms, axis=0):
    return lax.psum_scatter(
        terms.astype(jnp.bfloat16), "seq", scatter_dimension=axis, tiled=True
    ).astype(jnp.float32)


def sum_fsdp(terms, axis=0):
    return lax.psum_scatter(
        terms.astype(jnp.bfloat16), "fsdp", scatter_dimension=axis, tiled=True
    ).astype(jnp.float32)


MESH = pl.DeviceIdType.MESH


def remote(source, target, sent, landed, axis, index):
    return pltpu.make_async_remote_copy(
        src_ref=source,
        dst_ref=target,
        send_sem=sent,
        recv_sem=landed,
        device_id={axis: index},
        device_id_type=MESH,
    )


def greet(row, plane):
    barrier = pltpu.get_barrier_semaphore()
    for axis, size in (("seq", row), ("fsdp", plane)):
        own = lax.axis_index(axis)
        for ahead in range(1, size):
            pl.semaphore_signal(
                barrier,
                inc=1,
                device_id={axis: lax.rem(own + ahead, size)},
                device_id_type=MESH,
            )
    pl.semaphore_wait(barrier, row + plane - 2)


class RowGather:
    def __init__(self, own, view, sent, landed, row, chunks=1, has=None):
        self.own, self.view, self.sent, self.landed = own, view, sent, landed
        self.row, self.chips, self.chunks = row, row // 2, chunks
        self.has = has or (lambda i, c: None)
        self.me = lax.axis_index("seq")
        self.chip, self.core = self.me // 2, self.me % 2
        self.other = self.me + 1 - 2 * self.core

    def hop(self, i, c, way, source=None):
        place = self.view(i, c)
        target = (self.me + 2, self.me - 2, self.other)[way]
        return remote(
            place if source is None else source,
            place,
            self.sent.at[i, c, way],
            self.landed.at[i, c],
            "seq",
            target,
        )

    def when(self, i, c, condition, action):
        has = self.has(i, c)
        if has is not None:
            condition = has if condition is None else has & condition
        if condition is None:
            action()
        else:
            pl.when(condition)(action)

    def spread(self, i, c, forward, backward, source=None):
        self.when(i, c, forward, lambda: self.hop(i, c, 0, source).start())
        self.when(i, c, backward, lambda: self.hop(i, c, 1, source).start())
        self.when(i, c, None, lambda: self.hop(i, c, 2, source).start())

    def start(self):
        for c in range(self.chunks):
            self.spread(
                self.me, c, self.chip < self.chips - 1, self.chip > 0, self.own(c) if self.own else None
            )

    def pass_on(self, distance):
        def from_before():
            i = self.me - 2 * distance
            for c in range(self.chunks):
                self.when(i, c, None, lambda: self.hop(i, c, 2).wait_recv())
                self.when(i, c, self.chip < self.chips - 1, lambda: self.hop(i, c, 0).start())
                self.when(i, c, None, lambda: self.hop(i, c, 2).start())

        def from_after():
            i = self.me + 2 * distance
            for c in range(self.chunks):
                self.when(i, c, None, lambda: self.hop(i, c, 2).wait_recv())
                self.when(i, c, self.chip > 0, lambda: self.hop(i, c, 1).start())
                self.when(i, c, None, lambda: self.hop(i, c, 2).start())

        pl.when(self.chip >= distance)(from_before)
        pl.when(self.chip + distance < self.chips)(from_after)

    def from_other_core(self):
        for k in range(self.chips):
            i = 2 * k + 1 - self.core
            for c in range(self.chunks):
                self.when(i, c, None, lambda: self.hop(i, c, 2).wait_recv())

    def drain(self):
        for k in range(self.chips):
            i = 2 * k + self.core
            for c in range(self.chunks):
                forward = (self.chip >= k) & (self.chip < self.chips - 1)
                backward = (self.chip <= k) & (self.chip > 0)
                self.when(i, c, forward, lambda: self.hop(i, c, 0).wait_send())
                self.when(i, c, backward, lambda: self.hop(i, c, 1).wait_send())
                self.when(i, c, None, lambda: self.hop(i, c, 2).wait_send())


class PlaneGather:
    def __init__(self, own, view, parts, sent, landed):
        self.own, self.view, self.parts, self.sent, self.landed = own, view, parts, sent, landed
        me = lax.axis_index("fsdp")
        self.me = me
        self.beside = me + 1 - 2 * (me % 2)
        self.above = lax.rem(me + 2, 4)
        self.corner = lax.rem(self.beside + 2, 4)

    def whole(self, i, slot, target, source=None):
        place = self.view(i, None)
        return remote(
            place if source is None else source,
            place,
            self.sent.at[slot],
            self.landed.at[slot],
            "fsdp",
            target,
        )

    def part(self, i, slot, target):
        place = self.view(i, self.parts[slot - 2])
        return remote(place, place, self.sent.at[slot], self.landed.at[slot], "fsdp", target)

    def start(self):
        self.whole(self.me, 0, self.beside, self.own).start()
        self.whole(self.me, 1, self.above, self.own).start()

    def pass_on(self):
        self.whole(self.beside, 0, self.beside).wait_recv()
        self.part(self.beside, 2, self.above).start()
        self.whole(self.above, 1, self.above).wait_recv()
        self.part(self.above, 3, self.beside).start()

    def finish(self):
        self.part(self.corner, 2, self.above).wait_recv()
        self.part(self.corner, 3, self.beside).wait_recv()

    def drain(self):
        self.whole(self.me, 0, self.beside).wait_send()
        self.whole(self.me, 1, self.above).wait_send()
        self.part(self.beside, 2, self.above).wait_send()
        self.part(self.above, 3, self.beside).wait_send()


def group_of(device):
    third = (device + 5) // 8 - (device + 4) // 8
    fifth = (device + 3) // 8 - (device + 2) // 8
    return device - (device + 4) // 8 - (device + 2) // 8 + 3 * third + 3 * fifth


def device_of(group):
    return group + (group + 5) // 8 + (group + 4) // 8 - 5 * ((group + 2) // 8)


def own_blocks(device, columns, width, span):
    groups = -(-width // span)

    def block_at(column):
        return groups * (column // width) + (column % width) // span

    return block_at(device * columns), block_at(device * columns + columns - 1)


def norm_rows(values, gain, shift):
    centred = values - jnp.mean(values, axis=-1, keepdims=True)
    inverse = lax.rsqrt(jnp.mean(centred * centred, axis=-1, keepdims=True) + norm_eps)
    return (centred * inverse) * gain + shift


def attend(head, start, first, count, tile, qkv_ref, ids_col, ids_row, out_ref, lse_ref):
    span = out_ref.shape[1]
    rows, keys = pl.ds(start, tile), pl.ds(first, count)
    query = only_head(qkv_ref[rows, :span], head)
    scores = contract_last(query, qkv_ref[keys, span : 2 * span]) * (HEAD_DIM**-0.5)
    q_pos = start + lax.broadcasted_iota(jnp.int32, (tile, count), 0)
    k_pos = first + lax.broadcasted_iota(jnp.int32, (tile, count), 1)
    allowed = (k_pos <= q_pos) & (ids_col[rows, :1] == ids_row[:1, keys])
    masked = jnp.where(allowed, scores, masked_score)
    top = jnp.max(masked, axis=1, keepdims=True)
    weights = jnp.exp(masked - top)
    total = jnp.sum(weights, axis=1, keepdims=True)
    probs = (weights * (1.0 / total)).astype(jnp.bfloat16)
    value = only_head(qkv_ref[keys, 2 * span :], head)
    mixed = jnp.dot(probs, value, preferred_element_type=jnp.float32)
    out_ref[rows, :] += mixed.astype(jnp.bfloat16)
    lse_ref[head, rows, :] = top + jnp.log(total)


def attention_kernel(
    reach,
    x_ref,
    cot_ref,
    small_ref,
    blocks_ref,
    fc_ref,
    proj_ref,
    x_all,
    cot_all,
    small_all,
    h1_all,
    qkv_all,
    w_all,
    lse_all,
    attn_own_out,
    attn_all,
    fc_all,
    proj_all,
    x_v,
    small_v,
    vec,
    ids_col,
    ids_row,
    pieces,
    w_v,
    h1_v,
    qkv_v,
    attn_v,
    small_sent,
    small_landed,
    plane_sent,
    plane_landed,
    piece_sent,
    piece_landed,
    w_sent,
    w_landed,
    x_sent,
    x_landed,
    cot_sent,
    cot_landed,
    attn_sent,
    attn_landed,
    fc_sent,
    fc_landed,
    proj_sent,
    proj_landed,
    local_sem,
):
    row, plane = 8, 4
    seq, fsdp = lax.axis_index("seq"), lax.axis_index("fsdp")
    own_rows, width = x_ref.shape
    span = attn_v.shape[1]
    length = own_rows * row
    depth = blocks_ref.shape[1]
    groups = -(-width // span)
    group = group_of(seq)
    used = []

    def keep(source, target):
        copy = pltpu.make_async_copy(source, target, local_sem.at[len(used)])
        copy.start()
        used.append(copy)

    vec[...] = jnp.zeros_like(vec)
    w_v[...] = jnp.zeros_like(w_v)
    greet(row, plane)
    own_small = pltpu.make_async_copy(small_ref, small_v.at[fsdp, seq], small_landed.at[seq])
    own_small.start()

    def small_to(target, slot):
        return remote(
            small_ref, small_v.at[fsdp, seq], small_sent.at[slot], small_landed.at[seq], "seq", target
        )

    for ahead in range(1, row):
        small_to(lax.rem(seq + ahead, row), ahead - 1).start()

    first_block, last_block = own_blocks(seq, qkv_columns(width, row), width, span)

    def piece(k):
        block = first_block + k
        kind, at = block // groups, block % groups
        begins = kind * width + at * span
        later = (seq * qkv_columns(width, row) + width * 3 - begins - 1) // (width * 3)
        target = device_of(at)
        place = pieces.at[kind, later]
        return block <= last_block, target, place, piece_landed.at[kind, later]

    for k in range(4):
        there, target, place, landed = piece(k)

        @pl.when(there & (target == seq))
        def _():
            pltpu.make_async_copy(blocks_ref.at[k], place, landed).start()

        @pl.when(there & (target != seq))
        def _():
            remote(blocks_ref.at[k], place, piece_sent.at[k], landed, "seq", target).start()

    x_line = RowGather(lambda c: x_ref, lambda i, c: x_v.at[i], x_sent, x_landed, row)
    own_x = pltpu.make_async_copy(x_ref, x_v.at[seq], local_sem.at[0])
    own_x.start()
    used.append(None)
    x_line.start()

    for other in range(row):
        pltpu.make_async_copy(small_ref, small_v.at[fsdp, other], small_landed.at[other]).wait()

    def small_plane(ahead):
        return remote(
            small_v.at[fsdp],
            small_v.at[fsdp],
            plane_sent.at[ahead - 1],
            plane_landed.at[ahead - 1],
            "fsdp",
            lax.rem(fsdp + ahead, plane),
        )

    for ahead in range(1, plane):
        small_plane(ahead).start()
    for other in range(row):
        lanes = pl.ds(other * own_rows, own_rows)
        ids = jnp.broadcast_to(small_v[fsdp, other, 3:4, :own_rows], (own_rows, own_rows))
        ids_row[:, lanes] = ids[:8]
        ids_col[lanes, :] = ids.T
    for ahead in range(1, plane):
        remote(
            small_v.at[fsdp],
            small_v.at[lax.rem(fsdp + plane - ahead, plane)],
            plane_sent.at[ahead - 1],
            plane_landed.at[ahead - 1],
            "fsdp",
            lax.rem(fsdp + ahead, plane),
        ).wait_recv()
    share = width // row
    for i in range(plane):
        for other in range(row):
            vec[2 * i : 2 * i + 2, share * other : share * (other + 1)] = small_v[i, other, 0:2, :share]

    own_w = pl.ds(pl.multiple_of(fsdp * depth, 16), depth)

    @pl.when(group < groups)
    def _():
        for kind in range(3):
            begins = kind * width + group * span
            ends = begins + jnp.minimum(span, width - group * span) - 1
            cols = qkv_columns(width, row)
            straddles = ends // cols != begins // cols
            pltpu.make_async_copy(
                blocks_ref.at[0], pieces.at[kind, 0], piece_landed.at[kind, 0]
            ).wait()
            w_v[own_w, kind * span : (kind + 1) * span] = pieces[kind, 0]

            @pl.when(straddles)
            def _():
                pltpu.make_async_copy(
                    blocks_ref.at[0], pieces.at[kind, 1], piece_landed.at[kind, 1]
                ).wait()
                w_v[own_w, kind * span : (kind + 1) * span] = pieces[kind, 0] + pieces[kind, 1]

    def w_view(i, part):
        start, count = (0, depth) if part is None else part
        return w_v.at[pl.ds(pl.multiple_of(i * depth + start, 16), count)]

    half = depth // 32 * 16
    w_plane = PlaneGather(None, w_view, ((0, half), (half, depth - half)), w_sent, w_landed)
    w_plane.start()
    x_line.pass_on(1)
    w_plane.pass_on()

    def slab(target):
        def view(i, part):
            start, count = (0, target.shape[1]) if part is None else part
            return target.at[i, pl.ds(start, count)]

        return view

    units = fc_ref.shape[0]
    cut = units // 32 * 16
    parts = ((0, cut), (cut, units - cut))
    fc_plane = PlaneGather(fc_ref, slab(fc_all), parts, fc_sent, fc_landed)
    proj_plane = PlaneGather(proj_ref, slab(proj_all), parts, proj_sent, proj_landed)
    fc_plane.start()
    proj_plane.start()
    x_line.pass_on(2)
    x_line.pass_on(3)
    cot_line = RowGather(lambda c: cot_ref, lambda i, c: cot_all.at[i], cot_sent, cot_landed, row)
    cot_line.start()
    keep(cot_ref, cot_all.at[seq])
    keep(fc_ref, fc_all.at[fsdp])
    keep(proj_ref, proj_all.at[fsdp])
    x_line.from_other_core()
    own_x.wait()
    w_plane.finish()
    lanes = pl.ds(pl.multiple_of(group * span, span), span)
    query_shift, value_shift = vec[2:3, lanes], vec[3:4, lanes]

    def project(i, carry):
        hidden = norm_rows(x_v[i].astype(jnp.float32), vec[0:1, :width], vec[1:2, :width])
        hidden = hidden.astype(jnp.bfloat16)
        h1_v[i] = hidden
        rows = pl.ds(pl.multiple_of(i * own_rows, own_rows), own_rows)
        mixed = jnp.dot(hidden, w_v[...], preferred_element_type=jnp.float32)
        qkv_v[rows, :span] = (mixed[:, :span] + query_shift).astype(jnp.bfloat16)
        qkv_v[rows, span : 2 * span] = mixed[:, span : 2 * span].astype(jnp.bfloat16)
        qkv_v[rows, 2 * span :] = (mixed[:, 2 * span :] + value_shift).astype(jnp.bfloat16)
        return carry

    lax.fori_loop(0, row, project, 0)
    cot_line.pass_on(1)
    keep(x_v, x_all)
    keep(small_v, small_all)
    keep(h1_v, h1_all)
    keep(qkv_v, qkv_all)
    keep(w_v, w_all)

    attn_v[...] = jnp.zeros_like(attn_v)
    tile = 256

    def heads(h, carry):
        for start, first, count in tile_pairs(length, tile, reach):
            attend(h, start, first, count, tile, qkv_v, ids_col, ids_row, attn_v, lse_all)
        return carry

    lax.fori_loop(0, 2, heads, 0)
    cot_line.pass_on(2)
    lax.fori_loop(2, 4, heads, 0)

    def chunk(i, c):
        return attn_all.at[:, pl.ds(pl.multiple_of(group_of(i) * span + c * 128, 128), 128)]

    attn_line = RowGather(
        lambda c: attn_v.at[:, pl.ds(c * 128, 128)],
        chunk,
        attn_sent,
        attn_landed,
        row,
        chunks=2,
        has=lambda i, c: group_of(i) < groups - c,
    )
    attn_line.start()
    for c in range(2):
        lanes = pl.ds(pl.multiple_of(group * span + c * 128, 128), 128)

        @pl.when(group < groups - c)
        def _():
            pltpu.make_async_copy(
                attn_v.at[:, pl.ds(c * 128, 128)], attn_all.at[:, lanes], piece_landed.at[c, 0]
            ).start()

    keep(attn_v, attn_own_out)
    fc_plane.pass_on()
    proj_plane.pass_on()
    cot_line.pass_on(3)
    for distance in range(1, row // 2):
        attn_line.pass_on(distance)
    attn_line.from_other_core()
    cot_line.from_other_core()
    fc_plane.finish()
    proj_plane.finish()

    for c in range(2):
        lanes = pl.ds(pl.multiple_of(group * span + c * 128, 128), 128)

        @pl.when(group < groups - c)
        def _():
            pltpu.make_async_copy(
                attn_v.at[:, pl.ds(c * 128, 128)], attn_all.at[:, lanes], piece_landed.at[c, 0]
            ).wait()

    for ahead in range(1, row):
        small_to(lax.rem(seq + ahead, row), ahead - 1).wait_send()
    for ahead in range(1, plane):
        small_plane(ahead).wait_send()
    for k in range(4):
        there, target, place, landed = piece(k)

        @pl.when(there & (target != seq))
        def _():
            remote(blocks_ref.at[k], place, piece_sent.at[k], landed, "seq", target).wait_send()

    for line in (x_line, cot_line, attn_line, w_plane, fc_plane, proj_plane):
        line.drain()
    for copy in used:
        if copy is not None:
            copy.wait()


def qkv_columns(width, row):
    return 3 * width // row


def attention_phase(x_own, cot_own, small, blocks, fc_own, proj_own, reach):
    own_rows, width = x_own.shape
    row, plane, span = 8, 4, 256
    length = own_rows * row
    units = fc_own.shape[0]
    bf, f32 = jnp.bfloat16, jnp.float32
    anywhere = pl.BlockSpec(memory_space=pl.ANY)
    in_vmem = pl.BlockSpec(memory_space=pltpu.VMEM)
    dma = pltpu.SemaphoreType.DMA

    def shaped(*shape, dtype=bf):
        return jax.ShapeDtypeStruct(shape, dtype)

    return pl.pallas_call(
        lambda *refs: attention_kernel(reach, *refs),
        out_shape=[
            shaped(row, own_rows, width),
            shaped(row, own_rows, width),
            shaped(plane, row, 8, span, dtype=f32),
            shaped(row, own_rows, width),
            shaped(length, 3 * span),
            shaped(width, 3 * span),
            shaped(4, length, 1, dtype=f32),
            shaped(length, span),
            shaped(length, 7 * span),
            shaped(plane, units, width),
            shaped(plane, units, width),
        ],
        in_specs=[anywhere] * 6,
        out_specs=[anywhere] * 6 + [in_vmem] + [anywhere] * 4,
        scratch_shapes=[
            pltpu.VMEM((row, own_rows, width), bf),
            pltpu.VMEM((plane, row, 8, span), f32),
            pltpu.VMEM((8, 8 * span), f32),
            pltpu.VMEM((length, own_rows), f32),
            pltpu.VMEM((8, length), f32),
            pltpu.VMEM((3, 2, width // plane, span), bf),
            pltpu.VMEM((width, 3 * span), bf),
            pltpu.VMEM((row, own_rows, width), bf),
            pltpu.VMEM((length, 3 * span), bf),
            pltpu.VMEM((length, span), bf),
            dma((row - 1,)),
            dma((row,)),
            dma((plane - 1,)),
            dma((plane - 1,)),
            dma((4,)),
            dma((3, 2)),
            dma((4,)),
            dma((4,)),
            dma((row, 1, 3)),
            dma((row, 1)),
            dma((row, 1, 3)),
            dma((row, 1)),
            dma((row, 2, 3)),
            dma((row, 2)),
            dma((4,)),
            dma((4,)),
            dma((4,)),
            dma((4,)),
            dma((12,)),
        ],
        compiler_params=pltpu.CompilerParams(
            collective_id=0, has_side_effects=True, vmem_limit_bytes=50 * 1024 * 1024
        ),
    )(x_own, cot_own, small, blocks, fc_own, proj_own)


def column_blocks(shard, own, width, span):
    columns = shard.shape[1]
    groups = -(-width // span)
    first, last = own_blocks(own, columns, width, span)
    place = lax.iota(jnp.int32, 4 * span)
    block, lane = first + place // span, place % span
    at = (block % groups) * span + lane
    there = (block <= last) & (at < width)
    source = jnp.where(there, (block // groups) * width + at - own * columns, -1)
    chosen = lax.broadcasted_iota(jnp.int32, (columns, 4 * span), 0) == source[None, :]
    cut = jnp.dot(shard, chosen.astype(jnp.bfloat16), preferred_element_type=jnp.float32)
    return cut.astype(jnp.bfloat16).reshape(-1, 4, span).transpose(1, 0, 2)


def token_plan(
    tokens,
    segment_ids,
    cotangent,
    qkv_weight,
    attn_out_weight,
    fc_weight,
    proj_weight,
    vectors,
    fc_bias,
):
    own_rows, width = tokens.shape[1], tokens.shape[2]
    parts = lax.axis_size("seq")
    own = lax.axis_index("seq")
    length = own_rows * parts
    reach = length // 2
    span = 4 * HEAD_DIM
    share = vectors.shape[1]
    units = proj_weight.shape[0]
    extra = -units % 16
    group = group_of(own)

    lines = [vectors.astype(jnp.float32), fc_bias.astype(jnp.float32)[None]]
    lines = [jnp.pad(line, ((0, 0), (0, span - share))) for line in lines]
    lines.append(jnp.pad(segment_ids.astype(jnp.float32), ((0, 4), (0, span - own_rows))))
    small = jnp.concatenate(lines)
    blocks = column_blocks(qkv_weight, own, width, span)
    fc_own = jnp.pad(fc_weight.T, ((0, extra), (0, 0)))
    proj_own = jnp.pad(proj_weight, ((0, extra), (0, 0)))
    w_attn = join_fsdp(join_seq(attn_out_weight, 1))

    inputs_all, grad_out_all, small_all, hidden1, qkv, w_qkv, lse, attn_own, attn_all, w_fc, w_proj = (
        attention_phase(tokens[0], cotangent[0], small, blocks, fc_own, proj_own, reach)
    )
    inputs_all = inputs_all.reshape(length, width)
    grad_out_all = grad_out_all.reshape(length, width)
    hidden1 = hidden1.reshape(length, width)
    w_fc, w_proj = w_fc.reshape(-1, width), w_proj.reshape(-1, width)
    vector_rows = small_all[:, :, :2, :share].transpose(0, 2, 1, 3).reshape(-1, width)
    own_small = lax.dynamic_index_in_dim(small_all, own, 1, keepdims=False)
    fc_shift = jnp.pad(own_small[:, 2, :units], ((0, 0), (0, extra))).reshape(-1)
    ids_all = lax.dynamic_index_in_dim(small_all, lax.axis_index("fsdp"), 0, keepdims=False)
    ids_all = ids_all[:, 3, :own_rows].reshape(length)
    ids_col, ids_row = ids_all[:, None], ids_all[None, :]
    attn_bf = attn_all[:, :width]

    def own_tokens(values):
        return lax.dynamic_slice_in_dim(values, own * own_rows, own_rows)

    resid = (
        inputs_all.astype(jnp.float32)
        + jnp.dot(attn_bf, w_attn, preferred_element_type=jnp.float32)
        + vector_rows[4]
    )

    normed2, inverse2, shifted2 = layer_norm(resid, vector_rows[5], vector_rows[6])
    hidden2 = shifted2.astype(jnp.bfloat16)
    preact = contract_last(hidden2, w_fc) + fc_shift
    gelu_value, gelu_slope = gelu_parts(preact)
    act_bf = gelu_value.astype(jnp.bfloat16)
    grad_act = contract_last(grad_out_all, w_proj)
    grad_pre = grad_act * gelu_slope
    grad_pre_bf = grad_pre.astype(jnp.bfloat16)
    grad_hidden2 = sum_seq(jnp.dot(grad_pre_bf, w_fc, preferred_element_type=jnp.float32))
    result = (
        own_tokens(resid)
        + sum_seq(jnp.dot(act_bf, w_proj, preferred_element_type=jnp.float32))
        + vector_rows[7]
    )
    own_proj = sum_fsdp(contract_first(act_bf, grad_out_all))[:units]
    own_fc = sum_fsdp(contract_first(grad_pre_bf, hidden2))[:units].T
    own_bias = sum_fsdp(jnp.sum(grad_pre, axis=0))[:units]

    grad_out = cotangent[0].astype(jnp.float32)
    grad_resid_norm, gain2_grad, shift2_grad = norm_back(
        grad_hidden2, own_tokens(normed2), own_tokens(inverse2), vector_rows[5]
    )
    grad_resid = grad_out + grad_resid_norm
    grad_resid_all = join_seq(grad_resid.astype(jnp.bfloat16))
    padded_rows = jnp.pad(w_attn, ((0, 8 * span - width), (0, 0)))
    attn_rows = lax.dynamic_slice_in_dim(padded_rows, group * span, span)
    grad_attn = contract_last(grad_resid_all, attn_rows).astype(jnp.bfloat16)
    grad_qkv = attention_backward(qkv, attn_own, grad_attn, lse, ids_col, ids_row, reach)
    grad_qkv_bf = grad_qkv.astype(jnp.bfloat16)
    grad_hidden1 = sum_seq(contract_last(grad_qkv_bf, w_qkv))
    normed1, inverse1, _ = layer_norm(tokens[0].astype(jnp.float32), vector_rows[0], vector_rows[1])
    grad_input_norm, gain1_grad, shift1_grad = norm_back(
        grad_hidden1, normed1, inverse1, vector_rows[0]
    )
    input_grad = grad_resid + grad_input_norm

    out_columns = attn_out_weight.shape[1]
    own_columns = lax.dynamic_slice_in_dim(grad_resid_all, own * out_columns, out_columns, axis=1)
    own_attn = sum_fsdp(contract_first(attn_bf, own_columns))
    qkv_terms = sum_fsdp(contract_first(hidden1, grad_qkv_bf)).astype(jnp.bfloat16)
    spread = lax.all_gather(qkv_terms, "seq", axis=0).reshape(parts, -1, 3, span)
    natural = jnp.concatenate(
        [spread[i] for i in (0, 1, 2, 4, 6, 7)] + [spread[3, :, :, : width % span]], axis=2
    ).reshape(-1, 3 * width)
    columns = qkv_weight.shape[1]
    own_qkv = lax.dynamic_slice_in_dim(natural, own * columns, columns, axis=1).astype(jnp.float32)

    def at_own_lanes(sums):
        padded = jnp.zeros((8 * span,), jnp.float32)
        return lax.dynamic_update_slice_in_dim(padded, sums, group * span, 0)[:width]

    column_sums = jnp.sum(grad_qkv, axis=0)
    vector_grad = jnp.stack(
        [
            gain1_grad,
            shift1_grad,
            at_own_lanes(column_sums[:span]),
            at_own_lanes(column_sums[2 * span :]),
            jnp.sum(grad_resid, axis=0),
            gain2_grad,
            shift2_grad,
            jnp.sum(grad_out, axis=0),
        ]
    )
    own_vec = sum_fsdp(sum_seq(vector_grad, 1))
    return (result[None], input_grad[None], own_qkv, own_attn, own_fc, own_proj, own_vec, own_bias)


def solution(mesh):
    in_specs = (
        P("fsdp", "seq", None),
        P("fsdp", "seq"),
        P("fsdp", "seq", None),
        P("fsdp", "seq"),
        P("fsdp", "seq"),
        P(None, ("fsdp", "seq")),
        P(("fsdp", "seq"), None),
        P("fsdp", "seq"),
        P(("fsdp", "seq")),
    )
    out_specs = (
        P("fsdp", "seq", None),
        P("fsdp", "seq", None),
        P("fsdp", "seq"),
        P("fsdp", "seq"),
        P(None, ("fsdp", "seq")),
        P(("fsdp", "seq"), None),
        P("fsdp", "seq"),
        P(("fsdp", "seq")),
    )

    def per_device(tokens, *rest):
        length = tokens.shape[1] * mesh.shape["seq"]
        fits = length * tokens.shape[2] <= resident_most
        square = mesh.shape["fsdp"] == 4 and mesh.shape["seq"] == 8
        plan = token_plan if fits and square else gathered_weights
        return plan(tokens, *rest)

    return jax.shard_map(
        per_device, mesh=mesh, in_specs=in_specs, out_specs=out_specs, check_vma=False
    )
```

```python
import math

import jax
import jax.numpy as jnp
from jax import lax
from jax.experimental import pallas as pl
from jax.experimental.pallas import tpu as pltpu
from jax.sharding import PartitionSpec as P

HEADS = 25
HEAD_DIM = 64


norm_eps = 1e-05
tanh_coeff = math.sqrt(2.0 / math.pi)
cubic_coeff = 0.044715
masked_score = -1e30


def layer_norm(values, gain, shift):
    centred = values - jnp.mean(values, axis=-1, keepdims=True)
    inverse = lax.rsqrt(jnp.mean(centred * centred, axis=-1, keepdims=True) + norm_eps)
    normed = centred * inverse
    return (normed, inverse, normed * gain + shift)


def norm_back(grad_out, normed, inverse, gain):
    scaled = grad_out * gain
    grad_in = inverse * (
        scaled
        - jnp.mean(scaled, axis=-1, keepdims=True)
        - normed * jnp.mean(scaled * normed, axis=-1, keepdims=True)
    )
    return (grad_in, jnp.sum(grad_out * normed, axis=0), jnp.sum(grad_out, axis=0))


def gelu_parts(preact):
    inner = tanh_coeff * (preact + cubic_coeff * preact * preact * preact)
    tangent = jnp.tanh(inner)
    gelu_value = 0.5 * preact * (1.0 + tangent)
    gelu_slope = 0.5 * (1.0 + tangent) + 0.5 * preact * (1.0 - tangent * tangent) * tanh_coeff * (
        1.0 + 3.0 * cubic_coeff * preact * preact
    )
    return (gelu_value, gelu_slope)


def block_rows():
    return 512


def gather_owned(matrix_qkv, matrix_attn, matrix_fc, matrix_proj, vector_part, bias_part):
    return (
        lax.all_gather(matrix_qkv, "fsdp", axis=0, tiled=True),
        lax.all_gather(matrix_attn, "fsdp", axis=0, tiled=True),
        lax.all_gather(matrix_fc, "fsdp", axis=1, tiled=True),
        lax.all_gather(matrix_proj, "fsdp", axis=0, tiled=True),
        lax.all_gather(vector_part, "fsdp", axis=0, tiled=True),
        lax.all_gather(bias_part, "fsdp", axis=0, tiled=True),
    )


def gather_attention(matrix_qkv, matrix_attn, vector_part, id_part):
    return (
        lax.all_gather(matrix_qkv, "seq", axis=1, tiled=True),
        lax.all_gather(matrix_attn, "seq", axis=1, tiled=True),
        lax.all_gather(vector_part, "seq", axis=1, tiled=True),
        lax.all_gather(id_part, "seq", axis=0, tiled=True),
    )


def gathered_weights(
    tokens,
    segment_ids,
    cotangent,
    qkv_weight,
    attn_out_weight,
    fc_weight,
    proj_weight,
    vectors,
    fc_bias,
):
    width = tokens.shape[2]
    local_rows = tokens.shape[1]
    heads = HEADS
    head_width = HEAD_DIM
    score_scale = head_width ** (-0.5)
    own_index = lax.axis_index("seq")
    inputs_bf = tokens[0]
    inputs = inputs_bf.astype(jnp.float32)
    doc_ids = segment_ids[0].astype(jnp.bfloat16)
    grad_out_bf = cotangent[0]
    owned = gather_owned(qkv_weight, attn_out_weight, fc_weight, proj_weight, vectors, fc_bias)
    w_qkv, w_attn, vector_bf, ids_all = gather_attention(owned[0], owned[1], owned[4], doc_ids)

    def gather_feedforward(matrix_fc, matrix_proj, bias_part):
        return (
            lax.all_gather(matrix_fc, "seq", axis=1, tiled=True),
            lax.all_gather(matrix_proj, "seq", axis=0, tiled=True),
            lax.all_gather(bias_part, "seq", axis=0, tiled=True),
        )

    w_fc, w_proj, bias_units = gather_feedforward(owned[2], owned[3], owned[5])
    vector_rows = vector_bf.astype(jnp.float32)
    fc_shift = bias_units.astype(jnp.float32)
    normed1, inverse1, shifted1 = layer_norm(inputs, vector_rows[0], vector_rows[1])
    hidden1 = shifted1.astype(jnp.bfloat16)
    projected = jnp.dot(hidden1, w_qkv, preferred_element_type=jnp.float32)
    queries = (projected[:, :width] + vector_rows[2]).astype(jnp.bfloat16)
    keys_own = projected[:, width : 2 * width].astype(jnp.bfloat16)
    values_own = (projected[:, 2 * width :] + vector_rows[3]).astype(jnp.bfloat16)
    query_heads = queries.reshape(local_rows, heads, head_width)
    positions = own_index * local_rows + lax.iota(jnp.int32, local_rows)

    def scores_for(key_block, ids_block, pos_block):
        scores = (
            jnp.einsum("qhd,khd->hqk", query_heads, key_block, preferred_element_type=jnp.float32)
            * score_scale
        )
        allowed = (
            (pos_block[None, :] <= positions[:, None])
            & (pos_block[None, :] >= 0)
            & (ids_block[None, :] == doc_ids[:, None])
        )
        return (scores, allowed)

    def stat_step(running, block_items):
        running_max, running_sum = running
        key_block, value_block, ids_block, pos_block = block_items
        scores, allowed = scores_for(key_block, ids_block, pos_block)
        masked = jnp.where(allowed[None], scores, masked_score)
        new_max = jnp.maximum(running_max, jnp.max(masked, axis=2))
        fading = jnp.exp(running_max - new_max)
        weights = jnp.where(allowed[None], jnp.exp(masked - new_max[:, :, None]), 0.0)
        running_sum = running_sum * fading + jnp.sum(weights, axis=2)
        return ((new_max, running_sum), None)

    initial = (
        jnp.full((heads, local_rows), masked_score, jnp.float32),
        jnp.zeros((heads, local_rows), jnp.float32),
    )
    keys_all, values_all = (
        lax.all_gather(keys_own, "seq", axis=0, tiled=True),
        lax.all_gather(values_own, "seq", axis=0, tiled=True),
    )
    key_count = keys_all.shape[0]
    step_rows = block_rows()
    blocks = key_count // step_rows
    key_items = (
        keys_all.reshape(blocks, step_rows, heads, head_width),
        values_all.reshape(blocks, step_rows, heads, head_width),
        ids_all.reshape(blocks, step_rows),
        lax.iota(jnp.int32, key_count).reshape(blocks, step_rows),
    )
    running, _ = lax.scan(stat_step, initial, key_items)
    final_max, final_sum = running
    log_total = final_max + jnp.log(final_sum)

    def weigh_step(total, block_items):
        key_block, value_block, ids_block, pos_block = block_items
        scores, allowed = scores_for(key_block, ids_block, pos_block)
        probs_bf = jnp.where(allowed[None], jnp.exp(scores - log_total[:, :, None]), 0.0).astype(
            jnp.bfloat16
        )
        return (
            total
            + jnp.einsum("hqk,khd->hqd", probs_bf, value_block, preferred_element_type=jnp.float32),
            None,
        )

    final_acc, _ = lax.scan(
        weigh_step, jnp.zeros((heads, local_rows, head_width), jnp.float32), key_items
    )
    attn_bf = final_acc.astype(jnp.bfloat16).transpose(1, 0, 2).reshape(local_rows, width)
    resid = inputs + jnp.dot(attn_bf, w_attn, preferred_element_type=jnp.float32) + vector_rows[4]
    normed2, inverse2, shifted2 = layer_norm(resid, vector_rows[5], vector_rows[6])
    hidden2 = shifted2.astype(jnp.bfloat16)
    preact = jnp.dot(hidden2, w_fc, preferred_element_type=jnp.float32) + fc_shift
    gelu_value, gelu_slope = gelu_parts(preact)
    act_bf = gelu_value.astype(jnp.bfloat16)
    mlp_out = jnp.dot(act_bf, w_proj, preferred_element_type=jnp.float32)
    result = resid + mlp_out + vector_rows[7]
    fenced = lax.optimization_barrier(
        (qkv_weight, attn_out_weight, fc_weight, proj_weight, vectors, fc_bias, doc_ids, result)
    )
    owned_again = gather_owned(fenced[0], fenced[1], fenced[2], fenced[3], fenced[4], fenced[5])
    back_qkv, back_attn, back_vec_bf, ids_again = gather_attention(
        owned_again[0], owned_again[1], owned_again[4], fenced[6]
    )
    back_fc, back_proj, bias_again = gather_feedforward(
        owned_again[2], owned_again[3], owned_again[5]
    )
    back_vec = back_vec_bf.astype(jnp.float32)
    grad_out = grad_out_bf.astype(jnp.float32)
    grad_proj_full = jnp.einsum(
        "tf,td->fd", act_bf, grad_out_bf, preferred_element_type=jnp.float32
    )
    grad_act = jnp.einsum("td,fd->tf", grad_out_bf, back_proj, preferred_element_type=jnp.float32)
    grad_pre = grad_act * gelu_slope
    grad_pre_bf = grad_pre.astype(jnp.bfloat16)
    grad_fc_full = jnp.einsum("td,tf->df", hidden2, grad_pre_bf, preferred_element_type=jnp.float32)
    grad_hidden2 = jnp.einsum("tf,df->td", grad_pre_bf, back_fc, preferred_element_type=jnp.float32)
    bias_full = jnp.sum(grad_pre, axis=0)
    part_fc, part_proj, part_bias = (
        lax.psum_scatter(
            grad_fc_full.astype(jnp.bfloat16), "seq", scatter_dimension=1, tiled=True
        ).astype(jnp.float32),
        lax.psum_scatter(
            grad_proj_full.astype(jnp.bfloat16), "seq", scatter_dimension=0, tiled=True
        ).astype(jnp.float32),
        lax.psum_scatter(
            bias_full.astype(jnp.bfloat16), "seq", scatter_dimension=0, tiled=True
        ).astype(jnp.float32),
    )
    grad_resid_norm, gain2_grad, shift2_grad = norm_back(
        grad_hidden2, normed2, inverse2, back_vec[5]
    )
    grad_resid = grad_out + grad_resid_norm
    grad_resid_bf = grad_resid.astype(jnp.bfloat16)
    grad_attn_out_full = jnp.einsum(
        "tc,td->cd", attn_bf, grad_resid_bf, preferred_element_type=jnp.float32
    )
    grad_attn_bf = jnp.einsum(
        "td,cd->tc", grad_resid_bf, back_attn, preferred_element_type=jnp.float32
    ).astype(jnp.bfloat16)
    grad_heads = grad_attn_bf.reshape(local_rows, heads, head_width)
    attn_heads = attn_bf.reshape(local_rows, heads, head_width)
    delta = jnp.sum(grad_heads.astype(jnp.float32) * attn_heads.astype(jnp.float32), axis=2).T

    def back_step(grad_query, block_items):
        key_block, value_block, ids_block, pos_block = block_items
        scores, allowed = scores_for(key_block, ids_block, pos_block)
        probs = jnp.where(allowed[None], jnp.exp(scores - log_total[:, :, None]), 0.0)
        probs_bf = probs.astype(jnp.bfloat16)
        value_grad = jnp.einsum(
            "hqk,qhd->khd", probs_bf, grad_heads, preferred_element_type=jnp.float32
        )
        prob_grad = jnp.einsum(
            "qhd,khd->hqk", grad_heads, value_block, preferred_element_type=jnp.float32
        )
        score_grad = (probs * (prob_grad - delta[:, :, None])).astype(jnp.bfloat16)
        grad_query = grad_query + score_scale * jnp.einsum(
            "hqk,khd->qhd", score_grad, key_block, preferred_element_type=jnp.float32
        )
        key_grad = score_scale * jnp.einsum(
            "hqk,qhd->khd", score_grad, query_heads, preferred_element_type=jnp.float32
        )
        return (grad_query, (key_grad, value_grad))

    query_zero = jnp.zeros((local_rows, heads, head_width), jnp.float32)
    grad_query, stacked_grads = lax.scan(back_step, query_zero, key_items)
    key_terms = stacked_grads[0].reshape(key_count, width)
    value_terms = stacked_grads[1].reshape(key_count, width)
    key_own_grad, value_own_grad = (
        lax.psum_scatter(
            key_terms.astype(jnp.bfloat16), "seq", scatter_dimension=0, tiled=True
        ).astype(jnp.float32),
        lax.psum_scatter(
            value_terms.astype(jnp.bfloat16), "seq", scatter_dimension=0, tiled=True
        ).astype(jnp.float32),
    )
    query_grad = grad_query.reshape(local_rows, width)
    grad_qkv_bf = jnp.concatenate([query_grad, key_own_grad, value_own_grad], axis=1).astype(
        jnp.bfloat16
    )
    grad_qkv_full = jnp.einsum(
        "td,te->de", hidden1, grad_qkv_bf, preferred_element_type=jnp.float32
    )
    grad_hidden1 = jnp.einsum(
        "te,de->td", grad_qkv_bf, back_qkv, preferred_element_type=jnp.float32
    )
    grad_input_norm, gain1_grad, shift1_grad = norm_back(
        grad_hidden1, normed1, inverse1, back_vec[0]
    )
    input_grad = grad_resid + grad_input_norm
    vector_grad = jnp.stack(
        [
            gain1_grad,
            shift1_grad,
            jnp.sum(query_grad, axis=0),
            jnp.sum(value_own_grad, axis=0),
            jnp.sum(grad_resid, axis=0),
            gain2_grad,
            shift2_grad,
            jnp.sum(grad_out, axis=0),
        ]
    )
    part_qkv, part_attn, part_vec = (
        lax.psum_scatter(
            grad_qkv_full.astype(jnp.bfloat16), "seq", scatter_dimension=1, tiled=True
        ).astype(jnp.float32),
        lax.psum_scatter(
            grad_attn_out_full.astype(jnp.bfloat16), "seq", scatter_dimension=1, tiled=True
        ).astype(jnp.float32),
        lax.psum_scatter(
            vector_grad.astype(jnp.bfloat16), "seq", scatter_dimension=1, tiled=True
        ).astype(jnp.float32),
    )
    own_qkv, own_attn, own_fc, own_proj, own_vec, own_bias = (
        lax.psum_scatter(
            part_qkv.astype(jnp.bfloat16), "fsdp", scatter_dimension=0, tiled=True
        ).astype(jnp.float32),
        lax.psum_scatter(
            part_attn.astype(jnp.bfloat16), "fsdp", scatter_dimension=0, tiled=True
        ).astype(jnp.float32),
        lax.psum_scatter(
            part_fc.astype(jnp.bfloat16), "fsdp", scatter_dimension=1, tiled=True
        ).astype(jnp.float32),
        lax.psum_scatter(
            part_proj.astype(jnp.bfloat16), "fsdp", scatter_dimension=0, tiled=True
        ).astype(jnp.float32),
        lax.psum_scatter(
            part_vec.astype(jnp.bfloat16), "fsdp", scatter_dimension=0, tiled=True
        ).astype(jnp.float32),
        lax.psum_scatter(
            part_bias.astype(jnp.bfloat16), "fsdp", scatter_dimension=0, tiled=True
        ).astype(jnp.float32),
    )
    return (result[None], input_grad[None], own_qkv, own_attn, own_fc, own_proj, own_vec, own_bias)


resident_most = 2 * 1024 * 1024


def contract_last(left, right):
    return lax.dot_general(left, right, (((1,), (1,)), ((), ())), preferred_element_type=jnp.float32)


def contract_first(left, right):
    return lax.dot_general(left, right, (((0,), (0,)), ((), ())), preferred_element_type=jnp.float32)


def head_lanes(head, shape):
    lane = lax.broadcasted_iota(jnp.int32, shape, 1)
    return (lane >= head * HEAD_DIM) & (lane < (head + 1) * HEAD_DIM)


def only_head(values, head):
    return jnp.where(head_lanes(head, values.shape), values, jnp.zeros_like(values))


def tile_pairs(length, tile, reach):
    for start in range(0, length, tile):
        first = max(0, (start - reach) // tile * tile)
        yield start, first, start + tile - first


def join_seq(block, axis=0):
    return lax.all_gather(block, "seq", axis=axis, tiled=True)


def join_fsdp(block, axis=0):
    return lax.all_gather(block, "fsdp", axis=axis, tiled=True)


MESH = pl.DeviceIdType.MESH


def remote(source, target, sent, landed, axis, index):
    return pltpu.make_async_remote_copy(
        src_ref=source,
        dst_ref=target,
        send_sem=sent,
        recv_sem=landed,
        device_id={axis: index},
        device_id_type=MESH,
    )


def greet(row, plane):
    barrier = pltpu.get_barrier_semaphore()
    for axis, size in (("seq", row), ("fsdp", plane)):
        own = lax.axis_index(axis)
        for ahead in range(1, size):
            pl.semaphore_signal(
                barrier,
                inc=1,
                device_id={axis: lax.rem(own + ahead, size)},
                device_id_type=MESH,
            )
    pl.semaphore_wait(barrier, row + plane - 2)


class RowGather:
    def __init__(self, own, view, sent, landed, row, chunks=1, has=None):
        self.own, self.view, self.sent, self.landed = own, view, sent, landed
        self.row, self.chips, self.chunks = row, row // 2, chunks
        self.has = has or (lambda i, c: None)
        self.me = lax.axis_index("seq")
        self.chip, self.core = self.me // 2, self.me % 2
        self.other = self.me + 1 - 2 * self.core

    def hop(self, i, c, way, source=None):
        place = self.view(i, c)
        target = (self.me + 2, self.me - 2, self.other)[way]
        return remote(
            place if source is None else source,
            place,
            self.sent.at[i, c, way],
            self.landed.at[i, c],
            "seq",
            target,
        )

    def when(self, i, c, condition, action):
        has = self.has(i, c)
        if has is not None:
            condition = has if condition is None else has & condition
        if condition is None:
            action()
        else:
            pl.when(condition)(action)

    def spread(self, i, c, forward, backward, source=None):
        self.when(i, c, forward, lambda: self.hop(i, c, 0, source).start())
        self.when(i, c, backward, lambda: self.hop(i, c, 1, source).start())
        self.when(i, c, None, lambda: self.hop(i, c, 2, source).start())

    def start(self):
        for c in range(self.chunks):
            self.spread(
                self.me, c, self.chip < self.chips - 1, self.chip > 0, self.own(c) if self.own else None
            )

    def pass_on(self, distance):
        def from_before():
            i = self.me - 2 * distance
            for c in range(self.chunks):
                self.when(i, c, None, lambda: self.hop(i, c, 2).wait_recv())
                self.when(i, c, self.chip < self.chips - 1, lambda: self.hop(i, c, 0).start())
                self.when(i, c, None, lambda: self.hop(i, c, 2).start())

        def from_after():
            i = self.me + 2 * distance
            for c in range(self.chunks):
                self.when(i, c, None, lambda: self.hop(i, c, 2).wait_recv())
                self.when(i, c, self.chip > 0, lambda: self.hop(i, c, 1).start())
                self.when(i, c, None, lambda: self.hop(i, c, 2).start())

        pl.when(self.chip >= distance)(from_before)
        pl.when(self.chip + distance < self.chips)(from_after)

    def from_other_core(self):
        for k in range(self.chips):
            i = 2 * k + 1 - self.core
            for c in range(self.chunks):
                self.when(i, c, None, lambda: self.hop(i, c, 2).wait_recv())

    def drain(self):
        for k in range(self.chips):
            i = 2 * k + self.core
            for c in range(self.chunks):
                forward = (self.chip >= k) & (self.chip < self.chips - 1)
                backward = (self.chip <= k) & (self.chip > 0)
                self.when(i, c, forward, lambda: self.hop(i, c, 0).wait_send())
                self.when(i, c, backward, lambda: self.hop(i, c, 1).wait_send())
                self.when(i, c, None, lambda: self.hop(i, c, 2).wait_send())


class PlaneGather:
    def __init__(self, own, view, parts, sent, landed):
        self.own, self.view, self.parts, self.sent, self.landed = own, view, parts, sent, landed
        me = lax.axis_index("fsdp")
        self.me = me
        self.beside = me + 1 - 2 * (me % 2)
        self.above = lax.rem(me + 2, 4)
        self.corner = lax.rem(self.beside + 2, 4)

    def whole(self, i, slot, target, source=None):
        place = self.view(i, None)
        return remote(
            place if source is None else source,
            place,
            self.sent.at[slot],
            self.landed.at[slot],
            "fsdp",
            target,
        )

    def part(self, i, slot, target):
        place = self.view(i, self.parts[slot - 2])
        return remote(place, place, self.sent.at[slot], self.landed.at[slot], "fsdp", target)

    def start(self):
        self.whole(self.me, 0, self.beside, self.own).start()
        self.whole(self.me, 1, self.above, self.own).start()

    def pass_on(self):
        self.whole(self.beside, 0, self.beside).wait_recv()
        self.part(self.beside, 2, self.above).start()
        self.whole(self.above, 1, self.above).wait_recv()
        self.part(self.above, 3, self.beside).start()

    def finish(self):
        self.part(self.corner, 2, self.above).wait_recv()
        self.part(self.corner, 3, self.beside).wait_recv()

    def drain(self):
        self.whole(self.me, 0, self.beside).wait_send()
        self.whole(self.me, 1, self.above).wait_send()
        self.part(self.beside, 2, self.above).wait_send()
        self.part(self.above, 3, self.beside).wait_send()


def group_of(device):
    third = (device + 5) // 8 - (device + 4) // 8
    fifth = (device + 3) // 8 - (device + 2) // 8
    return device - (device + 4) // 8 - (device + 2) // 8 + 3 * third + 3 * fifth


def device_of(group):
    return group + (group + 5) // 8 + (group + 4) // 8 - 5 * ((group + 2) // 8)


def own_blocks(device, columns, width, span):
    groups = -(-width // span)

    def block_at(column):
        return groups * (column // width) + (column % width) // span

    return block_at(device * columns), block_at(device * columns + columns - 1)


def norm_rows(values, gain, shift):
    centred = values - jnp.mean(values, axis=-1, keepdims=True)
    inverse = lax.rsqrt(jnp.mean(centred * centred, axis=-1, keepdims=True) + norm_eps)
    return (centred * inverse) * gain + shift


def attend(head, start, first, count, tile, qkv_ref, ids_col, ids_row, out_ref, lse_ref):
    span = out_ref.shape[1]
    rows, keys = pl.ds(start, tile), pl.ds(first, count)
    query = only_head(qkv_ref[rows, :span], head)
    scores = contract_last(query, qkv_ref[keys, span : 2 * span]) * (HEAD_DIM**-0.5)
    q_pos = start + lax.broadcasted_iota(jnp.int32, (tile, count), 0)
    k_pos = first + lax.broadcasted_iota(jnp.int32, (tile, count), 1)
    allowed = (k_pos <= q_pos) & (ids_col[rows, :1] == ids_row[:1, keys])
    masked = jnp.where(allowed, scores, masked_score)
    top = jnp.max(masked, axis=1, keepdims=True)
    weights = jnp.exp(masked - top)
    total = jnp.sum(weights, axis=1, keepdims=True)
    probs = (weights * (1.0 / total)).astype(jnp.bfloat16)
    value = only_head(qkv_ref[keys, 2 * span :], head)
    mixed = jnp.dot(probs, value, preferred_element_type=jnp.float32)
    out_ref[rows, :] += mixed.astype(jnp.bfloat16)
    lane = lax.broadcasted_iota(jnp.int32, (tile, lse_ref.shape[1]), 1)
    lse_ref[rows, :] = jnp.where(lane == head, top + jnp.log(total), lse_ref[rows, :])


def attention_kernel(
    reach,
    x_ref,
    cot_ref,
    small_ref,
    blocks_ref,
    fc_ref,
    proj_ref,
    x_all,
    cot_all,
    small_all,
    vec_all,
    col_all,
    row_all,
    h1_all,
    qkv_all,
    w_all,
    lse_all,
    attn_own_out,
    attn_all,
    fc_all,
    proj_all,
    x_v,
    small_v,
    vec,
    ids_col,
    ids_row,
    pieces,
    w_v,
    h1_v,
    qkv_v,
    attn_v,
    small_sent,
    small_landed,
    plane_sent,
    plane_landed,
    piece_sent,
    piece_landed,
    w_sent,
    w_landed,
    x_sent,
    x_landed,
    cot_sent,
    cot_landed,
    attn_sent,
    attn_landed,
    fc_sent,
    fc_landed,
    proj_sent,
    proj_landed,
    local_sem,
):
    row, plane = 8, 4
    seq, fsdp = lax.axis_index("seq"), lax.axis_index("fsdp")
    own_rows, width = x_ref.shape
    span = attn_v.shape[1]
    length = own_rows * row
    depth = blocks_ref.shape[1]
    groups = -(-width // span)
    group = group_of(seq)
    used = []

    def keep(source, target):
        copy = pltpu.make_async_copy(source, target, local_sem.at[len(used)])
        copy.start()
        used.append(copy)

    vec[...] = jnp.zeros_like(vec)
    w_v[...] = jnp.zeros_like(w_v)
    greet(row, plane)
    own_small = pltpu.make_async_copy(small_ref, small_v.at[fsdp, seq], small_landed.at[seq])
    own_small.start()

    def small_to(target, slot):
        return remote(
            small_ref, small_v.at[fsdp, seq], small_sent.at[slot], small_landed.at[seq], "seq", target
        )

    for ahead in range(1, row):
        small_to(lax.rem(seq + ahead, row), ahead - 1).start()

    first_block, last_block = own_blocks(seq, qkv_columns(width, row), width, span)

    def piece(k):
        block = first_block + k
        kind, at = block // groups, block % groups
        begins = kind * width + at * span
        later = (seq * qkv_columns(width, row) + width * 3 - begins - 1) // (width * 3)
        target = device_of(at)
        place = pieces.at[kind, later]
        return block <= last_block, target, place, piece_landed.at[kind, later]

    for k in range(4):
        there, target, place, landed = piece(k)

        @pl.when(there & (target == seq))
        def _():
            pltpu.make_async_copy(blocks_ref.at[k], place, landed).start()

        @pl.when(there & (target != seq))
        def _():
            remote(blocks_ref.at[k], place, piece_sent.at[k], landed, "seq", target).start()

    def block_of(target):
        return lambda i, c: target.at[pl.ds(pl.multiple_of(i * own_rows, own_rows), own_rows)]

    x_line = RowGather(lambda c: x_ref, block_of(x_v), x_sent, x_landed, row)
    own_x = pltpu.make_async_copy(x_ref, block_of(x_v)(seq, 0), local_sem.at[0])
    own_x.start()
    used.append(None)
    x_line.start()

    for other in range(row):
        pltpu.make_async_copy(small_ref, small_v.at[fsdp, other], small_landed.at[other]).wait()

    def small_plane(ahead):
        return remote(
            small_v.at[fsdp],
            small_v.at[fsdp],
            plane_sent.at[ahead - 1],
            plane_landed.at[ahead - 1],
            "fsdp",
            lax.rem(fsdp + ahead, plane),
        )

    for ahead in range(1, plane):
        small_plane(ahead).start()
    for other in range(row):
        lanes = pl.ds(other * own_rows, own_rows)
        ids = jnp.broadcast_to(small_v[fsdp, other, 3:4, :own_rows], (own_rows, own_rows))
        ids_row[:, lanes] = ids[:8]
        ids_col[lanes, :] = ids.T
    for ahead in range(1, plane):
        remote(
            small_v.at[fsdp],
            small_v.at[lax.rem(fsdp + plane - ahead, plane)],
            plane_sent.at[ahead - 1],
            plane_landed.at[ahead - 1],
            "fsdp",
            lax.rem(fsdp + ahead, plane),
        ).wait_recv()
    share = width // row
    for i in range(plane):
        for other in range(row):
            vec[2 * i : 2 * i + 2, share * other : share * (other + 1)] = small_v[i, other, 0:2, :share]

    own_w = pl.ds(pl.multiple_of(fsdp * depth, 16), depth)

    @pl.when(group < groups)
    def _():
        for kind in range(3):
            begins = kind * width + group * span
            ends = begins + jnp.minimum(span, width - group * span) - 1
            cols = qkv_columns(width, row)
            straddles = ends // cols != begins // cols
            pltpu.make_async_copy(
                blocks_ref.at[0], pieces.at[kind, 0], piece_landed.at[kind, 0]
            ).wait()
            w_v[own_w, kind * span : (kind + 1) * span] = pieces[kind, 0]

            @pl.when(straddles)
            def _():
                pltpu.make_async_copy(
                    blocks_ref.at[0], pieces.at[kind, 1], piece_landed.at[kind, 1]
                ).wait()
                w_v[own_w, kind * span : (kind + 1) * span] = pieces[kind, 0] + pieces[kind, 1]

    def w_view(i, part):
        start, count = (0, depth) if part is None else part
        return w_v.at[pl.ds(pl.multiple_of(i * depth + start, 16), count)]

    half = depth // 32 * 16
    w_plane = PlaneGather(None, w_view, ((0, half), (half, depth - half)), w_sent, w_landed)
    w_plane.start()
    x_line.pass_on(1)
    w_plane.pass_on()

    def slab(target):
        def view(i, part):
            start, count = (0, target.shape[1]) if part is None else part
            return target.at[i, pl.ds(start, count)]

        return view

    units = fc_ref.shape[0]
    cut = units // 32 * 16
    parts = ((0, cut), (cut, units - cut))
    fc_plane = PlaneGather(fc_ref, slab(fc_all), parts, fc_sent, fc_landed)
    proj_plane = PlaneGather(proj_ref, slab(proj_all), parts, proj_sent, proj_landed)
    fc_plane.start()
    proj_plane.start()
    x_line.pass_on(2)
    x_line.pass_on(3)
    cot_line = RowGather(lambda c: cot_ref, block_of(cot_all), cot_sent, cot_landed, row)
    cot_line.start()
    keep(cot_ref, block_of(cot_all)(seq, 0))
    keep(fc_ref, fc_all.at[fsdp])
    keep(proj_ref, proj_all.at[fsdp])
    x_line.from_other_core()
    own_x.wait()
    w_plane.finish()
    lanes = pl.ds(pl.multiple_of(group * span, span), span)
    query_shift, value_shift = vec[2:3, lanes], vec[3:4, lanes]

    def project(i, carry):
        rows = pl.ds(pl.multiple_of(i * own_rows, own_rows), own_rows)
        hidden = norm_rows(x_v[rows, :].astype(jnp.float32), vec[0:1, :width], vec[1:2, :width])
        hidden = hidden.astype(jnp.bfloat16)
        h1_v[rows, :] = hidden
        mixed = jnp.dot(hidden, w_v[...], preferred_element_type=jnp.float32)
        qkv_v[rows, :span] = (mixed[:, :span] + query_shift).astype(jnp.bfloat16)
        qkv_v[rows, span : 2 * span] = mixed[:, span : 2 * span].astype(jnp.bfloat16)
        qkv_v[rows, 2 * span :] = (mixed[:, 2 * span :] + value_shift).astype(jnp.bfloat16)
        return carry

    lax.fori_loop(0, row, project, 0)
    cot_line.pass_on(1)
    keep(x_v, x_all)
    keep(small_v, small_all)
    keep(vec, vec_all)
    keep(ids_col, col_all)
    keep(ids_row, row_all)
    keep(h1_v, h1_all)
    keep(qkv_v, qkv_all)
    keep(w_v, w_all)

    attn_v[...] = jnp.zeros_like(attn_v)
    lse_all[...] = jnp.zeros_like(lse_all)
    tile = 256

    def heads(h, carry):
        for start, first, count in tile_pairs(length, tile, reach):
            attend(h, start, first, count, tile, qkv_v, ids_col, ids_row, attn_v, lse_all)
        return carry

    lax.fori_loop(0, 2, heads, 0)
    cot_line.pass_on(2)
    lax.fori_loop(2, 4, heads, 0)

    def chunk(i, c):
        return attn_all.at[:, pl.ds(pl.multiple_of(group_of(i) * span + c * 128, 128), 128)]

    attn_line = RowGather(
        lambda c: attn_v.at[:, pl.ds(c * 128, 128)],
        chunk,
        attn_sent,
        attn_landed,
        row,
        chunks=2,
        has=lambda i, c: group_of(i) < groups - c,
    )
    attn_line.start()
    for c in range(2):
        lanes = pl.ds(pl.multiple_of(group * span + c * 128, 128), 128)

        @pl.when(group < groups - c)
        def _():
            pltpu.make_async_copy(
                attn_v.at[:, pl.ds(c * 128, 128)], attn_all.at[:, lanes], piece_landed.at[c, 0]
            ).start()

    keep(attn_v, attn_own_out)
    fc_plane.pass_on()
    proj_plane.pass_on()
    cot_line.pass_on(3)
    for distance in range(1, row // 2):
        attn_line.pass_on(distance)
    attn_line.from_other_core()
    cot_line.from_other_core()
    fc_plane.finish()
    proj_plane.finish()

    for c in range(2):
        lanes = pl.ds(pl.multiple_of(group * span + c * 128, 128), 128)

        @pl.when(group < groups - c)
        def _():
            pltpu.make_async_copy(
                attn_v.at[:, pl.ds(c * 128, 128)], attn_all.at[:, lanes], piece_landed.at[c, 0]
            ).wait()

    for ahead in range(1, row):
        small_to(lax.rem(seq + ahead, row), ahead - 1).wait_send()
    for ahead in range(1, plane):
        small_plane(ahead).wait_send()
    for k in range(4):
        there, target, place, landed = piece(k)

        @pl.when(there & (target != seq))
        def _():
            remote(blocks_ref.at[k], place, piece_sent.at[k], landed, "seq", target).wait_send()

    for line in (x_line, cot_line, attn_line, w_plane, fc_plane, proj_plane):
        line.drain()
    for copy in used:
        if copy is not None:
            copy.wait()


def qkv_columns(width, row):
    return 3 * width // row


def attention_phase(x_own, cot_own, small, blocks, fc_own, proj_own, reach):
    own_rows, width = x_own.shape
    row, plane, span = 8, 4, 256
    length = own_rows * row
    units = fc_own.shape[0]
    bf, f32 = jnp.bfloat16, jnp.float32
    anywhere = pl.BlockSpec(memory_space=pl.ANY)
    in_vmem = pl.BlockSpec(memory_space=pltpu.VMEM)
    dma = pltpu.SemaphoreType.DMA

    def shaped(*shape, dtype=bf):
        return jax.ShapeDtypeStruct(shape, dtype)

    return pl.pallas_call(
        lambda *refs: attention_kernel(reach, *refs),
        out_shape=[
            shaped(length, width),
            shaped(length, width),
            shaped(plane, row, 8, span, dtype=f32),
            shaped(8, 8 * span, dtype=f32),
            shaped(length, own_rows, dtype=f32),
            shaped(8, length, dtype=f32),
            shaped(length, width),
            shaped(length, 3 * span),
            shaped(width, 3 * span),
            shaped(length, 128, dtype=f32),
            shaped(length, span),
            shaped(length, 7 * span),
            shaped(plane, units, width),
            shaped(plane, units, width),
        ],
        in_specs=[anywhere] * 6,
        out_specs=[anywhere] * 9 + [in_vmem] + [anywhere] * 4,
        scratch_shapes=[
            pltpu.VMEM((length, width), bf),
            pltpu.VMEM((plane, row, 8, span), f32),
            pltpu.VMEM((8, 8 * span), f32),
            pltpu.VMEM((length, own_rows), f32),
            pltpu.VMEM((8, length), f32),
            pltpu.VMEM((3, 2, width // plane, span), bf),
            pltpu.VMEM((width, 3 * span), bf),
            pltpu.VMEM((length, width), bf),
            pltpu.VMEM((length, 3 * span), bf),
            pltpu.VMEM((length, span), bf),
            dma((row - 1,)),
            dma((row,)),
            dma((plane - 1,)),
            dma((plane - 1,)),
            dma((4,)),
            dma((3, 2)),
            dma((4,)),
            dma((4,)),
            dma((row, 1, 3)),
            dma((row, 1)),
            dma((row, 1, 3)),
            dma((row, 1)),
            dma((row, 2, 3)),
            dma((row, 2)),
            dma((4,)),
            dma((4,)),
            dma((4,)),
            dma((4,)),
            dma((16,)),
        ],
        compiler_params=pltpu.CompilerParams(
            collective_id=0, has_side_effects=True, vmem_limit_bytes=50 * 1024 * 1024
        ),
    )(x_own, cot_own, small, blocks, fc_own, proj_own)


def pick(index, values):
    chosen = values[-1]
    for k in range(len(values) - 1):
        chosen = jnp.where(index == k, values[k], chosen)
    return chosen


def chip_order(chip, step):
    rows = ((3, 3, 0, 0), (2, 0, 3, 1), (1, 2, 1, 2), (0, 1, 2, 3))
    return pick(step, [pick(chip, row) for row in rows])


class RowSum:
    def __init__(self, own, away, pair, chain, pair_sent, pair_landed, chain_sent, chain_landed):
        self.own, self.away, self.pair, self.chain = own, away, pair, chain
        self.pair_sent, self.pair_landed = pair_sent, pair_landed
        self.chain_sent, self.chain_landed = chain_sent, chain_landed
        self.me = lax.axis_index("seq")
        self.chips = 4
        self.chip, self.core = self.me // 2, self.me % 2
        self.other = self.me + 1 - 2 * self.core

    def exchange(self, t):
        return remote(
            self.away.at[t],
            self.pair.at[t],
            self.pair_sent.at[t],
            self.pair_landed.at[t],
            "seq",
            self.other,
        )

    def onward(self, t, slot, target):
        return remote(
            self.own.at[t],
            self.chain.at[slot],
            self.chain_sent.at[t],
            self.chain_landed.at[slot],
            "seq",
            target,
        )

    def put(self, t, terms):
        rows = self.own.shape[1]
        self.away[t] = terms[pl.ds(pl.multiple_of((1 - self.core) * rows, rows), rows), :].astype(
            jnp.bfloat16
        )
        self.exchange(t).start()
        self.own[t] = terms[pl.ds(pl.multiple_of(self.core * rows, rows), rows), :].astype(jnp.bfloat16)

    def add(self, t, arrived, slot):
        total = self.own[t].astype(jnp.float32) + arrived[slot].astype(jnp.float32)
        self.own[t] = total.astype(jnp.bfloat16)

    def step(self, t):
        self.exchange(t).wait_recv()
        self.add(t, self.pair, t)

        def forward():
            @pl.when(self.chip > 0)
            def _():
                self.onward(t, t, self.me + 2).wait_recv()
                self.add(t, self.chain, t)

            self.onward(t, t, self.me + 2).start()

        def backward():
            @pl.when(self.chip < self.chips - 1)
            def _():
                self.onward(t, t, self.me - 2).wait_recv()
                self.add(t, self.chain, t)

            slot = jnp.where(t == self.chip - 1, self.chips, t)
            self.onward(t, slot, self.me - 2).start()

        pl.when(t > self.chip)(forward)
        pl.when(t < self.chip)(backward)

    def final(self, total):
        t = self.chip
        self.exchange(t).wait_recv()
        total[...] = self.own[t].astype(jnp.float32) + self.pair[t].astype(jnp.float32)

        @pl.when(self.chip > 0)
        def _():
            self.onward(t, t, self.other).wait_recv()
            total[...] += self.chain[t].astype(jnp.float32)

        @pl.when(self.chip < self.chips - 1)
        def _():
            self.onward(t, self.chips, self.other).wait_recv()
            total[...] += self.chain[self.chips].astype(jnp.float32)

    def drain(self):
        for t in range(self.chips):
            self.exchange(t).wait_send()

            @pl.when(self.chip != t)
            def _():
                self.onward(t, t, self.other).wait_send()


class PlaneTerms:
    def __init__(self, view, terms, sent, landed):
        self.view, self.terms, self.sent, self.landed = view, terms, sent, landed
        self.me = lax.axis_index("fsdp")

    def to(self, ahead):
        i = lax.rem(self.me + ahead, 4)
        return remote(
            self.view(i), self.terms.at[self.me], self.sent.at[ahead], self.landed.at[self.me], "fsdp", i
        )

    def keep(self):
        return pltpu.make_async_copy(
            self.view(self.me), self.terms.at[self.me], self.landed.at[self.me]
        )

    def start(self):
        self.keep().start()
        for ahead in (3, 1, 2):
            self.to(ahead).start()

    def arrive(self):
        self.keep().wait()
        for ahead in range(1, 4):
            i = lax.rem(self.me + ahead, 4)
            remote(
                self.view(i), self.terms.at[i], self.sent.at[ahead], self.landed.at[i], "fsdp", i
            ).wait_recv()

    def drain(self):
        for ahead in range(1, 4):
            self.to(ahead).wait_send()


def backward_attend(
    head, start, first, count, tile, qkv_ref, attn_ref, grad_ref, lse_ref, ids_col, ids_row, out_ref
):
    span = attn_ref.shape[1]
    scale = HEAD_DIM**-0.5
    rows, keys = pl.ds(start, tile), pl.ds(first, count)
    query = only_head(qkv_ref[rows, :span], head)
    key = qkv_ref[keys, span : 2 * span]
    grad = only_head(grad_ref[rows, :], head)
    delta = jnp.sum(
        grad.astype(jnp.float32) * attn_ref[rows, :].astype(jnp.float32), axis=1, keepdims=True
    )
    scores = contract_last(query, key) * scale
    q_pos = start + lax.broadcasted_iota(jnp.int32, (tile, count), 0)
    k_pos = first + lax.broadcasted_iota(jnp.int32, (tile, count), 1)
    allowed = (k_pos <= q_pos) & (ids_col[rows, :1] == ids_row[:1, keys])
    lane = lax.broadcasted_iota(jnp.int32, (tile, lse_ref.shape[1]), 1)
    lse = jnp.sum(jnp.where(lane == head, lse_ref[rows, :], 0.0), axis=1, keepdims=True)
    probs = jnp.where(allowed, jnp.exp(scores - lse), 0.0)
    prob_grad = contract_last(grad, qkv_ref[keys, 2 * span :])
    score_grad = (probs * (prob_grad - delta)).astype(jnp.bfloat16)
    out_ref[rows, :span] += scale * jnp.dot(
        score_grad, only_head(key, head), preferred_element_type=jnp.float32
    )
    out_ref[keys, span : 2 * span] += scale * contract_first(score_grad, query)
    out_ref[keys, 2 * span :] += contract_first(probs.astype(jnp.bfloat16), grad)


def row_tiles(count, size, body):
    def step(i, carry):
        body(pl.multiple_of(i * size, size))
        return carry

    lax.fori_loop(0, count // size, step, 0)


def backward_kernel(
    reach,
    x_ref,
    cot_ref,
    vec_ref,
    bias_ref,
    w_attn_ref,
    attn_ref,
    fc_ref,
    proj_ref,
    h1_ref,
    qkv_ref,
    w_qkv_ref,
    lse_ref,
    attn_own_ref,
    ids_col_ref,
    ids_row_ref,
    result_ref,
    input_grad_ref,
    fc_terms,
    proj_terms,
    attn_terms,
    nat_blocks,
    vec_out,
    qkv_terms,
    attn_v,
    own1,
    away1,
    pair1,
    chain1,
    own2,
    away2,
    pair2,
    chain2,
    dr_all,
    resid_own,
    dresid_own,
    total,
    wide,
    fc_stage,
    proj_stage,
    vec_v,
    bias_v,
    bias_sum,
    gv,
    vec_send,
    vec_land,
    plane_send,
    plane_land,
    pair_sent,
    pair_landed,
    chain_sent,
    chain_landed,
    dr_sent,
    dr_landed,
    terms_sent,
    terms_landed,
    nat_sent,
    nat_landed,
    vec_sent,
    vec_landed,
    plane_sent,
    plane_landed,
    load_sem,
):
    row, plane, chips = 8, 4, 4
    seq, fsdp = lax.axis_index("seq"), lax.axis_index("fsdp")
    chip, core = seq // 2, seq % 2
    ends = (chip == 0) | (chip == chips - 1)
    length, width = x_ref.shape
    own_rows = length // row
    pair_rows = 2 * own_rows
    units = fc_ref.shape[1]
    span = attn_own_ref.shape[1]
    depth = width // plane
    groups = -(-width // span)
    group = group_of(seq)
    columns = qkv_columns(width, row)
    bf, f32 = jnp.bfloat16, jnp.float32
    tiles = [(0, 512), (512, 1024), (1024, width)]

    def load(source, target, slot):
        copy = pltpu.make_async_copy(source, target, load_sem.at[slot])
        copy.start()
        return copy

    def pair_at(t):
        return pl.ds(pl.multiple_of(t * pair_rows, pair_rows), pair_rows)

    own_at = pl.ds(pl.multiple_of(seq * own_rows, own_rows), own_rows)
    half_at = pl.ds(pl.multiple_of(core * own_rows, own_rows), own_rows)
    hidden_sum = RowSum(
        own1, away1, pair1, chain1, pair_sent.at[0], pair_landed.at[0], chain_sent.at[0], chain_landed.at[0]
    )
    out_sum = RowSum(
        own2, away2, pair2, chain2, pair_sent.at[1], pair_landed.at[1], chain_sent.at[1], chain_landed.at[1]
    )
    dr_line = RowGather(
        None,
        lambda i, c: dr_all.at[pl.ds(pl.multiple_of(i * own_rows, own_rows), own_rows)],
        dr_sent,
        dr_landed,
        row,
    )
    fc_plane = PlaneTerms(lambda i: fc_stage.at[i], fc_terms, terms_sent.at[0], terms_landed.at[0])
    proj_plane = PlaneTerms(lambda i: proj_stage.at[i], proj_terms, terms_sent.at[1], terms_landed.at[1])

    def feed_forward(w_attn, x_v, cot_v, fc_v, proj_v, h2_v, act_v, dpre_v, pre_v, dact_v):
        first = chip_order(chip, 0)
        loads = [
            load(attn_ref, attn_v, 0),
            load(w_attn_ref.at[pl.ds(0, width)], w_attn, 1),
            load(x_ref.at[pair_at(first)], x_v, 2),
            load(vec_ref, vec_v, 3),
            load(fc_ref, fc_v, 4),
            load(cot_ref, cot_v, 5),
            load(proj_ref, proj_v, 6),
            load(bias_ref, bias_v, 7),
        ]
        bias_sum[...] = jnp.zeros_like(bias_sum)
        gv[...] = jnp.zeros_like(gv)
        greet(row, plane)
        for copy in loads:
            copy.wait()

        def chunk(p, carry):
            t = chip_order(chip, p)
            rows = pair_at(t)
            for low, high in tiles:
                wide[:, low:high] = jnp.dot(
                    attn_v[rows, :width], w_attn[:, low:high], preferred_element_type=f32
                )

            @pl.when(p > 0)
            def _():
                pltpu.make_async_copy(x_ref.at[rows], x_v, load_sem.at[2]).wait()

            def second_norm(i):
                part = pl.ds(i, 16)
                resid = wide[part, :] + x_v[part, :].astype(f32) + vec_v[4:5, :width]
                wide[part, :] = resid
                hidden = norm_rows(resid, vec_v[5:6, :width], vec_v[6:7, :width])
                h2_v[pl.ds(pl.multiple_of(t * pair_rows + i, 16), 16), :] = hidden.astype(bf)

            row_tiles(pair_rows, 16, second_norm)

            @pl.when(p < chips - 1)
            def _():
                load(x_ref.at[pair_at(chip_order(chip, p + 1))], x_v, 2)

            @pl.when(t == chip)
            def _():
                resid_own[...] = wide[half_at, :]

            def unit_block(f, carry):
                pre_v[...] = contract_last(h2_v[rows, :], fc_v[f])
                dact_v[...] = contract_last(cot_v[rows, :], proj_v[f])
                shift = bias_v[pl.ds(f, 1), :units]

                def gelu(i):
                    part = pl.ds(i, 32)
                    gelu_value, gelu_slope = gelu_parts(pre_v[part, :] + shift)
                    dpre = dact_v[part, :] * gelu_slope
                    place = pl.ds(pl.multiple_of(t * pair_rows + i, 32), 32)
                    act_v[f, place, :] = gelu_value.astype(bf)
                    dpre_v[f, place, :] = dpre.astype(bf)
                    bias_sum[pl.ds(f, 1), :units] += jnp.sum(dpre, axis=0, keepdims=True)

                row_tiles(pair_rows, 32, gelu)
                return carry

            lax.fori_loop(0, plane, unit_block, 0)

            def back_through(values, weights):
                for low, high in tiles:
                    terms = jnp.dot(
                        values[0, rows, :], weights[0, :, low:high], preferred_element_type=f32
                    )
                    for f in range(1, plane):
                        terms += jnp.dot(
                            values[f, rows, :], weights[f, :, low:high], preferred_element_type=f32
                        )
                    wide[:, low:high] = terms

            back_through(dpre_v, fc_v)
            hidden_sum.put(t, wide)
            back_through(act_v, proj_v)
            out_sum.put(t, wide)

            @pl.when(ends & (p < chips - 1))
            def _():
                hidden_sum.step(t)

            @pl.when(jnp.logical_not(ends) & (p == 2))
            def _():
                hidden_sum.step(chip_order(chip, 0))

            return carry

        lax.fori_loop(0, chips, chunk, 0)

        @pl.when(jnp.logical_not(ends))
        def _():
            hidden_sum.step(chip_order(chip, 1))
            hidden_sum.step(chip_order(chip, 2))

        hidden_sum.final(total)

        def second_norm_back(i):
            part = pl.ds(i, 16)
            resid = resid_own[part, :]
            centred = resid - jnp.mean(resid, axis=-1, keepdims=True)
            inverse = lax.rsqrt(jnp.mean(centred * centred, axis=-1, keepdims=True) + norm_eps)
            normed = centred * inverse
            grad_hidden = total[part, :]
            scaled = grad_hidden * vec_v[5:6, :width]
            back = inverse * (
                scaled
                - jnp.mean(scaled, axis=-1, keepdims=True)
                - normed * jnp.mean(scaled * normed, axis=-1, keepdims=True)
            )
            place = pl.ds(pl.multiple_of(seq * own_rows + i, 16), 16)
            cot = cot_v[place, :].astype(f32)
            grad_resid = cot + back
            dresid_own[part, :] = grad_resid
            dr_all[place, :] = grad_resid.astype(bf)
            for at, values in ((4, grad_resid), (5, grad_hidden * normed), (6, grad_hidden), (7, cot)):
                gv[at : at + 1, :width] += jnp.sum(values, axis=0, keepdims=True)

        row_tiles(own_rows, 16, second_norm_back)
        dr_line.start()

        @pl.when(ends)
        def _():
            for p in range(chips - 1):
                out_sum.step(chip_order(chip, p))

        def weight_terms(values, others, stage):
            def unit_block(f, carry):
                for low, high in tiles:
                    stage[f, :, low:high] = contract_first(values[f], others[:, low:high]).astype(bf)
                return carry

            lax.fori_loop(0, plane, unit_block, 0)

        weight_terms(act_v, cot_v, proj_stage)
        proj_plane.start()
        dr_line.pass_on(1)
        weight_terms(dpre_v, h2_v, fc_stage)
        fc_plane.start()
        dr_line.pass_on(2)

    pl.run_scoped(
        feed_forward,
        pltpu.VMEM((width, width), bf),
        pltpu.VMEM((pair_rows, width), bf),
        pltpu.VMEM((length, width), bf),
        pltpu.VMEM((plane, units, width), bf),
        pltpu.VMEM((plane, units, width), bf),
        pltpu.VMEM((length, width), bf),
        pltpu.VMEM((plane, length, units), bf),
        pltpu.VMEM((plane, length, units), bf),
        pltpu.VMEM((pair_rows, units), f32),
        pltpu.VMEM((pair_rows, units), f32),
    )

    def attention_back(w_rows, h1_v, qkv_v, w_qkv, lse_v, attn_own, col_v, row_v, da_v, dqkv, dqkv16, ga, gq, gqt, own_x):
        loads = [
            load(w_attn_ref.at[pl.ds(pl.multiple_of(group * span, span), span)], w_rows, 0),
            load(qkv_ref, qkv_v, 1),
            load(lse_ref, lse_v, 2),
            load(attn_own_ref, attn_own, 3),
            load(ids_col_ref, col_v, 4),
            load(ids_row_ref, row_v, 5),
            load(h1_ref, h1_v, 6),
            load(w_qkv_ref, w_qkv, 7),
            load(x_ref.at[own_at], own_x, 8),
        ]
        dqkv[...] = jnp.zeros_like(dqkv)
        dr_line.pass_on(3)
        dr_line.from_other_core()
        for copy in loads:
            copy.wait()

        def into_heads(i):
            rows = pl.ds(i, pair_rows)
            da_v[rows, :] = contract_last(dr_all[rows, :], w_rows[...]).astype(bf)

        row_tiles(length, pair_rows, into_heads)

        @pl.when(jnp.logical_not(ends))
        def _():
            out_sum.step(chip_order(chip, 0))

        def heads(h, carry):
            for start, first, count in tile_pairs(length, 256, reach):
                backward_attend(
                    h, start, first, count, 256, qkv_v, attn_own, da_v, lse_v, col_v, row_v, dqkv
                )
            return carry

        lax.fori_loop(0, 2, heads, 0)

        @pl.when(jnp.logical_not(ends))
        def _():
            out_sum.step(chip_order(chip, 1))

        lax.fori_loop(2, 4, heads, 0)

        @pl.when(jnp.logical_not(ends))
        def _():
            out_sum.step(chip_order(chip, 2))

        lanes = pl.ds(pl.multiple_of(group * span, span), span)
        gv[2:3, lanes] = jnp.sum(dqkv[:, :span], axis=0, keepdims=True)
        gv[3:4, lanes] = jnp.sum(dqkv[:, 2 * span :], axis=0, keepdims=True)
        dqkv16[...] = dqkv[...].astype(bf)

        for low in range(0, width, span):
            high = min(low + span, width)
            gq[low:high, :] = contract_first(h1_v[:, low:high], dqkv16[...]).astype(bf)
        qkv_plane = PlaneTerms(
            lambda i: gq.at[pl.ds(pl.multiple_of(i * depth, 16), depth)],
            qkv_terms,
            terms_sent.at[2],
            terms_landed.at[2],
        )
        qkv_plane.start()

        hidden_sum.drain()

        def chunk(p, carry):
            t = chip_order(chip, p)
            for low, high in tiles:
                wide[:, low:high] = contract_last(dqkv16[pair_at(t), :], w_qkv[low:high, :])
            hidden_sum.put(t, wide)

            @pl.when(ends & (p < chips - 1))
            def _():
                hidden_sum.step(t)

            return carry

        lax.fori_loop(0, chips, chunk, 0)

        share = width // row
        place = lax.broadcasted_iota(jnp.int32, (width, span), 0)
        lane = lax.broadcasted_iota(jnp.int32, (width, span), 1)
        chosen = ((place == seq * share + lane) & (lane < share)).astype(f32).astype(bf)

        def own_columns(i):
            rows = pl.ds(i, pair_rows)
            da_v[rows, :] = jnp.dot(dr_all[rows, :], chosen, preferred_element_type=f32).astype(bf)

        row_tiles(length, pair_rows, own_columns)
        for low in range(0, width, span):
            high = min(low + span, width)
            ga[low:high, :] = contract_first(attn_v[:, low:high], da_v[...]).astype(bf)
        attn_plane = PlaneTerms(
            lambda i: ga.at[pl.ds(pl.multiple_of(i * depth, 16), depth)],
            attn_terms,
            terms_sent.at[3],
            terms_landed.at[3],
        )
        attn_plane.start()

        @pl.when(jnp.logical_not(ends))
        def _():
            for p in range(chips - 1):
                hidden_sum.step(chip_order(chip, p))

        qkv_plane.arrive()
        load(qkv_terms, gqt, 0).wait()
        qkv_plane.drain()
        for kind in range(3):
            part = gqt[0, :, kind * span : (kind + 1) * span].astype(f32)
            for f in range(1, plane):
                part += gqt[f, :, kind * span : (kind + 1) * span].astype(f32)
            gq[kind * depth : (kind + 1) * depth, :span] = part.astype(bf)

        def nat(kind, late):
            begins = kind * width + group * span
            last = begins + jnp.minimum(span, width - group * span) - 1
            before, after = begins // columns, last // columns
            target = after if late else before
            slot = kind * groups + group - own_blocks(target, columns, width, span)[0]
            there = (group < groups) & (before != after) if late else group < groups
            return there, target, slot

        def nat_copy(kind, late, target, slot):
            return remote(
                gq.at[pl.ds(kind * depth, depth), pl.ds(0, span)],
                nat_blocks.at[slot],
                nat_sent.at[kind, late],
                nat_landed.at[slot],
                "seq",
                target,
            )

        for kind in range(3):
            for late in range(2):
                there, target, slot = nat(kind, late)

                @pl.when(there & (target != seq))
                def _():
                    nat_copy(kind, late, target, slot).start()

                @pl.when(there & (target == seq))
                def _():
                    pltpu.make_async_copy(
                        gq.at[pl.ds(kind * depth, depth), pl.ds(0, span)],
                        nat_blocks.at[slot],
                        nat_landed.at[slot],
                    ).start()

        hidden_sum.final(total)

        def first_norm_back(i):
            part = pl.ds(i, 16)
            values = own_x[part, :].astype(f32)
            centred = values - jnp.mean(values, axis=-1, keepdims=True)
            inverse = lax.rsqrt(jnp.mean(centred * centred, axis=-1, keepdims=True) + norm_eps)
            normed = centred * inverse
            grad_hidden = total[part, :]
            scaled = grad_hidden * vec_v[0:1, :width]
            back = inverse * (
                scaled
                - jnp.mean(scaled, axis=-1, keepdims=True)
                - normed * jnp.mean(scaled * normed, axis=-1, keepdims=True)
            )
            input_grad_ref[part, :] = dresid_own[part, :] + back
            for at, summed in ((0, grad_hidden * normed), (1, grad_hidden)):
                gv[at : at + 1, :width] += jnp.sum(summed, axis=0, keepdims=True)

        row_tiles(own_rows, 16, first_norm_back)

        vec_send[...] = jnp.zeros_like(vec_send)
        plane_send[...] = jnp.zeros_like(plane_send)
        for i in range(row):
            vec_send[i, :, :share] = gv[:, share * i : share * (i + 1)]

        def vec_to(ahead):
            i = lax.rem(seq + ahead, row)
            return remote(
                vec_send.at[i], vec_land.at[seq], vec_sent.at[ahead], vec_landed.at[seq], "seq", i
            )

        keep = pltpu.make_async_copy(vec_send.at[seq], vec_land.at[seq], vec_landed.at[seq])
        keep.start()
        for ahead in range(1, row):
            vec_to(ahead).start()
        out_sum.final(total)
        for low, high in tiles:
            result_ref[:, low:high] = (
                resid_own[:, low:high] + total[:, low:high] + vec_v[7:8, low:high]
            )
        for i in range(row):
            pltpu.make_async_copy(vec_send.at[i], vec_land.at[i], vec_landed.at[i]).wait()
        summed = vec_land[0]
        for i in range(1, row):
            summed += vec_land[i]
        for i in range(plane):
            plane_send[i, 0:2, :] = summed[2 * i : 2 * i + 2, :]
            plane_send[i, 2:3, :] = bias_sum[i : i + 1, :]
        vec_plane = PlaneTerms(lambda i: plane_send.at[i], plane_land, plane_sent, plane_landed)
        vec_plane.start()
        first_block, last_block = own_blocks(seq, columns, width, span)
        for k in range(4):

            @pl.when(first_block + k <= last_block)
            def _():
                pltpu.make_async_copy(
                    gq.at[pl.ds(0, depth), pl.ds(0, span)], nat_blocks.at[k], nat_landed.at[k]
                ).wait()

        vec_plane.arrive()
        vec_out[...] = plane_land[0] + plane_land[1] + plane_land[2] + plane_land[3]
        vec_plane.drain()
        for ahead in range(1, row):
            vec_to(ahead).wait_send()
        for kind in range(3):
            for late in range(2):
                there, target, slot = nat(kind, late)

                @pl.when(there & (target != seq))
                def _():
                    nat_copy(kind, late, target, slot).wait_send()

        attn_plane.drain()
        attn_plane.arrive()

    pl.run_scoped(
        attention_back,
        pltpu.VMEM((span, width), bf),
        pltpu.VMEM((length, width), bf),
        pltpu.VMEM((length, 3 * span), bf),
        pltpu.VMEM((width, 3 * span), bf),
        pltpu.VMEM((length, 128), f32),
        pltpu.VMEM((length, span), bf),
        pltpu.VMEM((length, 128), f32),
        pltpu.VMEM((8, length), f32),
        pltpu.VMEM((length, span), bf),
        pltpu.VMEM((length, 3 * span), f32),
        pltpu.VMEM((length, 3 * span), bf),
        pltpu.VMEM((width, span), bf),
        pltpu.VMEM((width, 3 * span), bf),
        pltpu.VMEM((plane, depth, 3 * span), bf),
        pltpu.VMEM((own_rows, width), bf),
    )
    for summing in (hidden_sum, out_sum):
        summing.drain()
    dr_line.drain()
    for terms in (fc_plane, proj_plane):
        terms.drain()
        terms.arrive()


def backward_phase(
    x_all, cot_all, vec, bias, w_attn, attn_all, w_fc, w_proj, h1_all, qkv, w_qkv, lse, attn_own, ids_col, ids_row, reach
):
    length, width = x_all.shape
    row, plane, chips, span = 8, 4, 4, attn_own.shape[1]
    own_rows, units, depth = length // row, w_fc.shape[1], width // plane
    bf, f32 = jnp.bfloat16, jnp.float32
    anywhere = pl.BlockSpec(memory_space=pl.ANY)
    in_vmem = pl.BlockSpec(memory_space=pltpu.VMEM)
    dma = pltpu.SemaphoreType.DMA

    def shaped(*shape, dtype=bf):
        return jax.ShapeDtypeStruct(shape, dtype)

    block = (own_rows, width)
    return pl.pallas_call(
        lambda *refs: backward_kernel(reach, *refs),
        out_shape=[
            shaped(*block, dtype=f32),
            shaped(*block, dtype=f32),
            shaped(plane, units, width),
            shaped(plane, units, width),
            shaped(plane, depth, span),
            shaped(4, depth, span),
            shaped(8, span, dtype=f32),
            shaped(plane, depth, 3 * span),
        ],
        in_specs=[anywhere] * 15,
        out_specs=[in_vmem] * 2 + [anywhere] * 4 + [in_vmem] + [anywhere],
        scratch_shapes=[
            pltpu.VMEM(attn_all.shape, bf),
            pltpu.VMEM((chips,) + block, bf),
            pltpu.VMEM((chips,) + block, bf),
            pltpu.VMEM((chips,) + block, bf),
            pltpu.VMEM((chips + 1,) + block, bf),
            pltpu.VMEM((chips,) + block, bf),
            pltpu.VMEM((chips,) + block, bf),
            pltpu.VMEM((chips,) + block, bf),
            pltpu.VMEM((chips + 1,) + block, bf),
            pltpu.VMEM((length, width), bf),
            pltpu.VMEM(block, f32),
            pltpu.VMEM(block, f32),
            pltpu.VMEM(block, f32),
            pltpu.VMEM((2 * own_rows, width), f32),
            pltpu.VMEM((plane, units, width), bf),
            pltpu.VMEM((plane, units, width), bf),
            pltpu.VMEM((8, 8 * span), f32),
            pltpu.VMEM((8, span), f32),
            pltpu.VMEM((8, span), f32),
            pltpu.VMEM((8, 8 * span), f32),
            pltpu.VMEM((row, 8, span), f32),
            pltpu.VMEM((row, 8, span), f32),
            pltpu.VMEM((plane, 8, span), f32),
            pltpu.VMEM((plane, 8, span), f32),
            dma((2, chips)),
            dma((2, chips)),
            dma((2, chips)),
            dma((2, chips + 1)),
            dma((row, 1, 3)),
            dma((row, 1)),
            dma((4, 4)),
            dma((4, 4)),
            dma((3, 2)),
            dma((4,)),
            dma((row,)),
            dma((row,)),
            dma((4,)),
            dma((4,)),
            dma((9,)),
        ],
        compiler_params=pltpu.CompilerParams(
            collective_id=1, has_side_effects=True, vmem_limit_bytes=62 * 1024 * 1024
        ),
    )(x_all, cot_all, vec, bias, w_attn, attn_all, w_fc, w_proj, h1_all, qkv, w_qkv, lse, attn_own, ids_col, ids_row)


def block_places(own, columns, width, span):
    groups = -(-width // span)
    first, last = own_blocks(own, columns, width, span)
    place = lax.iota(jnp.int32, 4 * span)
    block, lane = first + place // span, place % span
    at = (block % groups) * span + lane
    source = (block // groups) * width + at - own * columns
    there = (block <= last) & (at < width) & (source >= 0) & (source < columns)
    return jnp.where(there, source, -1)


def joined_blocks(blocks, own, columns, width):
    span = blocks.shape[2]
    source = block_places(own, columns, width, span)
    chosen = lax.broadcasted_iota(jnp.int32, (4 * span, columns), 1) == source[:, None]
    lanes = blocks.transpose(1, 0, 2).reshape(-1, 4 * span)
    lanes = jnp.where(source[None, :] >= 0, lanes, jnp.zeros_like(lanes))
    return jnp.dot(lanes, chosen.astype(jnp.bfloat16), preferred_element_type=jnp.float32)


def column_blocks(shard, own, width, span):
    columns = shard.shape[1]
    source = block_places(own, columns, width, span)
    chosen = lax.broadcasted_iota(jnp.int32, (columns, 4 * span), 0) == source[None, :]
    cut = jnp.dot(shard, chosen.astype(jnp.bfloat16), preferred_element_type=jnp.float32)
    return cut.astype(jnp.bfloat16).reshape(-1, 4, span).transpose(1, 0, 2)


def token_plan(
    tokens,
    segment_ids,
    cotangent,
    qkv_weight,
    attn_out_weight,
    fc_weight,
    proj_weight,
    vectors,
    fc_bias,
):
    own_rows, width = tokens.shape[1], tokens.shape[2]
    parts = lax.axis_size("seq")
    own = lax.axis_index("seq")
    length = own_rows * parts
    reach = length // 2
    span = 4 * HEAD_DIM
    share = vectors.shape[1]
    units = proj_weight.shape[0]
    extra = -units % 16
    group = group_of(own)

    lines = [vectors.astype(jnp.float32), fc_bias.astype(jnp.float32)[None]]
    lines = [jnp.pad(line, ((0, 0), (0, span - share))) for line in lines]
    lines.append(jnp.pad(segment_ids.astype(jnp.float32), ((0, 4), (0, span - own_rows))))
    small = jnp.concatenate(lines)
    blocks = column_blocks(qkv_weight, own, width, span)
    fc_own = jnp.pad(fc_weight.T, ((0, extra), (0, 0)))
    proj_own = jnp.pad(proj_weight, ((0, extra), (0, 0)))
    w_attn = join_fsdp(join_seq(attn_out_weight, 1))

    x_all, cot_all, small_all, vec, ids_col, ids_row, h1, qkv, w_qkv, lse, attn_own, attn_all, w_fc, w_proj = (
        attention_phase(tokens[0], cotangent[0], small, blocks, fc_own, proj_own, reach)
    )
    own_small = lax.dynamic_index_in_dim(small_all, own, 1, keepdims=False)
    bias = jnp.pad(own_small[:, 2], ((0, 4), (0, 0)))
    w_attn = jnp.pad(w_attn, ((0, 8 * span - width), (0, 0)))
    result, input_grad, fc_terms, proj_terms, attn_terms, nat_blocks, vec_sums, _ = backward_phase(
        x_all, cot_all, vec, bias, w_attn, attn_all, w_fc, w_proj, h1, qkv, w_qkv, lse, attn_own, ids_col, ids_row, reach
    )

    def added(terms):
        return jnp.sum(terms.astype(jnp.float32), axis=0)

    own_qkv = joined_blocks(nat_blocks, own, qkv_weight.shape[1], width)
    own_attn = added(attn_terms)[:, : attn_out_weight.shape[1]]
    own_fc = added(fc_terms)[:units].T
    own_proj = added(proj_terms)[:units]
    own_vec = vec_sums[:2, :share]
    own_bias = vec_sums[2, :units]
    return (result[None], input_grad[None], own_qkv, own_attn, own_fc, own_proj, own_vec, own_bias)


def solution(mesh):
    in_specs = (
        P("fsdp", "seq", None),
        P("fsdp", "seq"),
        P("fsdp", "seq", None),
        P("fsdp", "seq"),
        P("fsdp", "seq"),
        P(None, ("fsdp", "seq")),
        P(("fsdp", "seq"), None),
        P("fsdp", "seq"),
        P(("fsdp", "seq")),
    )
    out_specs = (
        P("fsdp", "seq", None),
        P("fsdp", "seq", None),
        P("fsdp", "seq"),
        P("fsdp", "seq"),
        P(None, ("fsdp", "seq")),
        P(("fsdp", "seq"), None),
        P("fsdp", "seq"),
        P(("fsdp", "seq")),
    )

    def per_device(tokens, *rest):
        length = tokens.shape[1] * mesh.shape["seq"]
        fits = length * tokens.shape[2] <= resident_most
        square = mesh.shape["fsdp"] == 4 and mesh.shape["seq"] == 8
        plan = token_plan if fits and square else gathered_weights
        return plan(tokens, *rest)

    return jax.shard_map(
        per_device, mesh=mesh, in_specs=in_specs, out_specs=out_specs, check_vma=False
    )
```

```python
import functools
import math

import jax
import jax.numpy as jnp
from jax import lax
from jax.experimental import pallas as pl
from jax.experimental.pallas import tpu as pltpu
from jax.sharding import PartitionSpec as P

HEADS = 25
HEAD_DIM = 64


norm_eps = 1e-05
tanh_coeff = math.sqrt(2.0 / math.pi)
cubic_coeff = 0.044715
masked_score = -1e30


def layer_norm(values, gain, shift):
    centred = values - jnp.mean(values, axis=-1, keepdims=True)
    inverse = lax.rsqrt(jnp.mean(centred * centred, axis=-1, keepdims=True) + norm_eps)
    normed = centred * inverse
    return (normed, inverse, normed * gain + shift)


def norm_back(grad_out, normed, inverse, gain):
    scaled = grad_out * gain
    grad_in = inverse * (
        scaled
        - jnp.mean(scaled, axis=-1, keepdims=True)
        - normed * jnp.mean(scaled * normed, axis=-1, keepdims=True)
    )
    return (grad_in, jnp.sum(grad_out * normed, axis=0), jnp.sum(grad_out, axis=0))


def gelu_parts(preact):
    inner = tanh_coeff * (preact + cubic_coeff * preact * preact * preact)
    tangent = jnp.tanh(inner)
    gelu_value = 0.5 * preact * (1.0 + tangent)
    gelu_slope = 0.5 * (1.0 + tangent) + 0.5 * preact * (1.0 - tangent * tangent) * tanh_coeff * (
        1.0 + 3.0 * cubic_coeff * preact * preact
    )
    return (gelu_value, gelu_slope)


def block_rows():
    return 512


def gather_owned(matrix_qkv, matrix_attn, matrix_fc, matrix_proj, vector_part, bias_part):
    return (
        lax.all_gather(matrix_qkv, "fsdp", axis=0, tiled=True),
        lax.all_gather(matrix_attn, "fsdp", axis=0, tiled=True),
        lax.all_gather(matrix_fc, "fsdp", axis=1, tiled=True),
        lax.all_gather(matrix_proj, "fsdp", axis=0, tiled=True),
        lax.all_gather(vector_part, "fsdp", axis=0, tiled=True),
        lax.all_gather(bias_part, "fsdp", axis=0, tiled=True),
    )


def gather_attention(matrix_qkv, matrix_attn, vector_part, id_part):
    return (
        lax.all_gather(matrix_qkv, "seq", axis=1, tiled=True),
        lax.all_gather(matrix_attn, "seq", axis=1, tiled=True),
        lax.all_gather(vector_part, "seq", axis=1, tiled=True),
        lax.all_gather(id_part, "seq", axis=0, tiled=True),
    )


def gathered_weights(
    tokens,
    segment_ids,
    cotangent,
    qkv_weight,
    attn_out_weight,
    fc_weight,
    proj_weight,
    vectors,
    fc_bias,
):
    width = tokens.shape[2]
    local_rows = tokens.shape[1]
    heads = HEADS
    head_width = HEAD_DIM
    score_scale = head_width ** (-0.5)
    own_index = lax.axis_index("seq")
    inputs_bf = tokens[0]
    inputs = inputs_bf.astype(jnp.float32)
    doc_ids = segment_ids[0].astype(jnp.bfloat16)
    grad_out_bf = cotangent[0]
    owned = gather_owned(qkv_weight, attn_out_weight, fc_weight, proj_weight, vectors, fc_bias)
    w_qkv, w_attn, vector_bf, ids_all = gather_attention(owned[0], owned[1], owned[4], doc_ids)

    def gather_feedforward(matrix_fc, matrix_proj, bias_part):
        return (
            lax.all_gather(matrix_fc, "seq", axis=1, tiled=True),
            lax.all_gather(matrix_proj, "seq", axis=0, tiled=True),
            lax.all_gather(bias_part, "seq", axis=0, tiled=True),
        )

    w_fc, w_proj, bias_units = gather_feedforward(owned[2], owned[3], owned[5])
    vector_rows = vector_bf.astype(jnp.float32)
    fc_shift = bias_units.astype(jnp.float32)
    normed1, inverse1, shifted1 = layer_norm(inputs, vector_rows[0], vector_rows[1])
    hidden1 = shifted1.astype(jnp.bfloat16)
    projected = jnp.dot(hidden1, w_qkv, preferred_element_type=jnp.float32)
    queries = (projected[:, :width] + vector_rows[2]).astype(jnp.bfloat16)
    keys_own = projected[:, width : 2 * width].astype(jnp.bfloat16)
    values_own = (projected[:, 2 * width :] + vector_rows[3]).astype(jnp.bfloat16)
    query_heads = queries.reshape(local_rows, heads, head_width)
    positions = own_index * local_rows + lax.iota(jnp.int32, local_rows)

    def scores_for(key_block, ids_block, pos_block):
        scores = (
            jnp.einsum("qhd,khd->hqk", query_heads, key_block, preferred_element_type=jnp.float32)
            * score_scale
        )
        allowed = (
            (pos_block[None, :] <= positions[:, None])
            & (pos_block[None, :] >= 0)
            & (ids_block[None, :] == doc_ids[:, None])
        )
        return (scores, allowed)

    def stat_step(running, block_items):
        running_max, running_sum = running
        key_block, value_block, ids_block, pos_block = block_items
        scores, allowed = scores_for(key_block, ids_block, pos_block)
        masked = jnp.where(allowed[None], scores, masked_score)
        new_max = jnp.maximum(running_max, jnp.max(masked, axis=2))
        fading = jnp.exp(running_max - new_max)
        weights = jnp.where(allowed[None], jnp.exp(masked - new_max[:, :, None]), 0.0)
        running_sum = running_sum * fading + jnp.sum(weights, axis=2)
        return ((new_max, running_sum), None)

    initial = (
        jnp.full((heads, local_rows), masked_score, jnp.float32),
        jnp.zeros((heads, local_rows), jnp.float32),
    )
    keys_all, values_all = (
        lax.all_gather(keys_own, "seq", axis=0, tiled=True),
        lax.all_gather(values_own, "seq", axis=0, tiled=True),
    )
    key_count = keys_all.shape[0]
    step_rows = block_rows()
    blocks = key_count // step_rows
    key_items = (
        keys_all.reshape(blocks, step_rows, heads, head_width),
        values_all.reshape(blocks, step_rows, heads, head_width),
        ids_all.reshape(blocks, step_rows),
        lax.iota(jnp.int32, key_count).reshape(blocks, step_rows),
    )
    running, _ = lax.scan(stat_step, initial, key_items)
    final_max, final_sum = running
    log_total = final_max + jnp.log(final_sum)

    def weigh_step(total, block_items):
        key_block, value_block, ids_block, pos_block = block_items
        scores, allowed = scores_for(key_block, ids_block, pos_block)
        probs_bf = jnp.where(allowed[None], jnp.exp(scores - log_total[:, :, None]), 0.0).astype(
            jnp.bfloat16
        )
        return (
            total
            + jnp.einsum("hqk,khd->hqd", probs_bf, value_block, preferred_element_type=jnp.float32),
            None,
        )

    final_acc, _ = lax.scan(
        weigh_step, jnp.zeros((heads, local_rows, head_width), jnp.float32), key_items
    )
    attn_bf = final_acc.astype(jnp.bfloat16).transpose(1, 0, 2).reshape(local_rows, width)
    resid = inputs + jnp.dot(attn_bf, w_attn, preferred_element_type=jnp.float32) + vector_rows[4]
    normed2, inverse2, shifted2 = layer_norm(resid, vector_rows[5], vector_rows[6])
    hidden2 = shifted2.astype(jnp.bfloat16)
    preact = jnp.dot(hidden2, w_fc, preferred_element_type=jnp.float32) + fc_shift
    gelu_value, gelu_slope = gelu_parts(preact)
    act_bf = gelu_value.astype(jnp.bfloat16)
    mlp_out = jnp.dot(act_bf, w_proj, preferred_element_type=jnp.float32)
    result = resid + mlp_out + vector_rows[7]
    fenced = lax.optimization_barrier(
        (qkv_weight, attn_out_weight, fc_weight, proj_weight, vectors, fc_bias, doc_ids, result)
    )
    owned_again = gather_owned(fenced[0], fenced[1], fenced[2], fenced[3], fenced[4], fenced[5])
    back_qkv, back_attn, back_vec_bf, ids_again = gather_attention(
        owned_again[0], owned_again[1], owned_again[4], fenced[6]
    )
    back_fc, back_proj, bias_again = gather_feedforward(
        owned_again[2], owned_again[3], owned_again[5]
    )
    back_vec = back_vec_bf.astype(jnp.float32)
    grad_out = grad_out_bf.astype(jnp.float32)
    grad_proj_full = jnp.einsum(
        "tf,td->fd", act_bf, grad_out_bf, preferred_element_type=jnp.float32
    )
    grad_act = jnp.einsum("td,fd->tf", grad_out_bf, back_proj, preferred_element_type=jnp.float32)
    grad_pre = grad_act * gelu_slope
    grad_pre_bf = grad_pre.astype(jnp.bfloat16)
    grad_fc_full = jnp.einsum("td,tf->df", hidden2, grad_pre_bf, preferred_element_type=jnp.float32)
    grad_hidden2 = jnp.einsum("tf,df->td", grad_pre_bf, back_fc, preferred_element_type=jnp.float32)
    bias_full = jnp.sum(grad_pre, axis=0)
    part_fc, part_proj, part_bias = (
        lax.psum_scatter(
            grad_fc_full.astype(jnp.bfloat16), "seq", scatter_dimension=1, tiled=True
        ).astype(jnp.float32),
        lax.psum_scatter(
            grad_proj_full.astype(jnp.bfloat16), "seq", scatter_dimension=0, tiled=True
        ).astype(jnp.float32),
        lax.psum_scatter(
            bias_full.astype(jnp.bfloat16), "seq", scatter_dimension=0, tiled=True
        ).astype(jnp.float32),
    )
    grad_resid_norm, gain2_grad, shift2_grad = norm_back(
        grad_hidden2, normed2, inverse2, back_vec[5]
    )
    grad_resid = grad_out + grad_resid_norm
    grad_resid_bf = grad_resid.astype(jnp.bfloat16)
    grad_attn_out_full = jnp.einsum(
        "tc,td->cd", attn_bf, grad_resid_bf, preferred_element_type=jnp.float32
    )
    grad_attn_bf = jnp.einsum(
        "td,cd->tc", grad_resid_bf, back_attn, preferred_element_type=jnp.float32
    ).astype(jnp.bfloat16)
    grad_heads = grad_attn_bf.reshape(local_rows, heads, head_width)
    attn_heads = attn_bf.reshape(local_rows, heads, head_width)
    delta = jnp.sum(grad_heads.astype(jnp.float32) * attn_heads.astype(jnp.float32), axis=2).T

    def back_step(grad_query, block_items):
        key_block, value_block, ids_block, pos_block = block_items
        scores, allowed = scores_for(key_block, ids_block, pos_block)
        probs = jnp.where(allowed[None], jnp.exp(scores - log_total[:, :, None]), 0.0)
        probs_bf = probs.astype(jnp.bfloat16)
        value_grad = jnp.einsum(
            "hqk,qhd->khd", probs_bf, grad_heads, preferred_element_type=jnp.float32
        )
        prob_grad = jnp.einsum(
            "qhd,khd->hqk", grad_heads, value_block, preferred_element_type=jnp.float32
        )
        score_grad = (probs * (prob_grad - delta[:, :, None])).astype(jnp.bfloat16)
        grad_query = grad_query + score_scale * jnp.einsum(
            "hqk,khd->qhd", score_grad, key_block, preferred_element_type=jnp.float32
        )
        key_grad = score_scale * jnp.einsum(
            "hqk,qhd->khd", score_grad, query_heads, preferred_element_type=jnp.float32
        )
        return (grad_query, (key_grad, value_grad))

    query_zero = jnp.zeros((local_rows, heads, head_width), jnp.float32)
    grad_query, stacked_grads = lax.scan(back_step, query_zero, key_items)
    key_terms = stacked_grads[0].reshape(key_count, width)
    value_terms = stacked_grads[1].reshape(key_count, width)
    key_own_grad, value_own_grad = (
        lax.psum_scatter(
            key_terms.astype(jnp.bfloat16), "seq", scatter_dimension=0, tiled=True
        ).astype(jnp.float32),
        lax.psum_scatter(
            value_terms.astype(jnp.bfloat16), "seq", scatter_dimension=0, tiled=True
        ).astype(jnp.float32),
    )
    query_grad = grad_query.reshape(local_rows, width)
    grad_qkv_bf = jnp.concatenate([query_grad, key_own_grad, value_own_grad], axis=1).astype(
        jnp.bfloat16
    )
    grad_qkv_full = jnp.einsum(
        "td,te->de", hidden1, grad_qkv_bf, preferred_element_type=jnp.float32
    )
    grad_hidden1 = jnp.einsum(
        "te,de->td", grad_qkv_bf, back_qkv, preferred_element_type=jnp.float32
    )
    grad_input_norm, gain1_grad, shift1_grad = norm_back(
        grad_hidden1, normed1, inverse1, back_vec[0]
    )
    input_grad = grad_resid + grad_input_norm
    vector_grad = jnp.stack(
        [
            gain1_grad,
            shift1_grad,
            jnp.sum(query_grad, axis=0),
            jnp.sum(value_own_grad, axis=0),
            jnp.sum(grad_resid, axis=0),
            gain2_grad,
            shift2_grad,
            jnp.sum(grad_out, axis=0),
        ]
    )
    part_qkv, part_attn, part_vec = (
        lax.psum_scatter(
            grad_qkv_full.astype(jnp.bfloat16), "seq", scatter_dimension=1, tiled=True
        ).astype(jnp.float32),
        lax.psum_scatter(
            grad_attn_out_full.astype(jnp.bfloat16), "seq", scatter_dimension=1, tiled=True
        ).astype(jnp.float32),
        lax.psum_scatter(
            vector_grad.astype(jnp.bfloat16), "seq", scatter_dimension=1, tiled=True
        ).astype(jnp.float32),
    )
    own_qkv, own_attn, own_fc, own_proj, own_vec, own_bias = (
        lax.psum_scatter(
            part_qkv.astype(jnp.bfloat16), "fsdp", scatter_dimension=0, tiled=True
        ).astype(jnp.float32),
        lax.psum_scatter(
            part_attn.astype(jnp.bfloat16), "fsdp", scatter_dimension=0, tiled=True
        ).astype(jnp.float32),
        lax.psum_scatter(
            part_fc.astype(jnp.bfloat16), "fsdp", scatter_dimension=1, tiled=True
        ).astype(jnp.float32),
        lax.psum_scatter(
            part_proj.astype(jnp.bfloat16), "fsdp", scatter_dimension=0, tiled=True
        ).astype(jnp.float32),
        lax.psum_scatter(
            part_vec.astype(jnp.bfloat16), "fsdp", scatter_dimension=0, tiled=True
        ).astype(jnp.float32),
        lax.psum_scatter(
            part_bias.astype(jnp.bfloat16), "fsdp", scatter_dimension=0, tiled=True
        ).astype(jnp.float32),
    )
    return (result[None], input_grad[None], own_qkv, own_attn, own_fc, own_proj, own_vec, own_bias)


resident_most = 2 * 1024 * 1024


def contract_last(left, right):
    return lax.dot_general(left, right, (((1,), (1,)), ((), ())), preferred_element_type=jnp.float32)


def contract_first(left, right):
    return lax.dot_general(left, right, (((0,), (0,)), ((), ())), preferred_element_type=jnp.float32)


def head_lanes(head, shape):
    lane = lax.broadcasted_iota(jnp.int32, shape, 1)
    return (lane >= head * HEAD_DIM) & (lane < (head + 1) * HEAD_DIM)


def only_head(values, head):
    return jnp.where(head_lanes(head, values.shape), values, jnp.zeros_like(values))


def tile_pairs(length, tile, reach):
    for start in range(0, length, tile):
        first = max(0, (start - reach) // tile * tile)
        yield start, first, start + tile - first


norm_part = 32


def row_tiles(count, size, body):
    def step(i, carry):
        body(pl.multiple_of(i * size, size))
        return carry

    lax.fori_loop(0, count // size, step, 0)


MESH = pl.DeviceIdType.MESH


def remote(source, target, sent, landed, axis, index):
    return pltpu.make_async_remote_copy(
        src_ref=source,
        dst_ref=target,
        send_sem=sent,
        recv_sem=landed,
        device_id={axis: index},
        device_id_type=MESH,
    )


def greet(row, plane):
    barrier = pltpu.get_barrier_semaphore()
    for axis, size in (("seq", row), ("fsdp", plane)):
        own = lax.axis_index(axis)
        for ahead in range(1, size):
            pl.semaphore_signal(
                barrier,
                inc=1,
                device_id={axis: lax.rem(own + ahead, size)},
                device_id_type=MESH,
            )
    pl.semaphore_wait(barrier, row + plane - 2)


class RowGather:
    def __init__(self, own, view, sent, landed, row, chunks=1, has=None):
        self.own, self.view, self.sent, self.landed = own, view, sent, landed
        self.row, self.chips, self.chunks = row, row // 2, chunks
        self.has = has or (lambda i, c: None)
        self.me = lax.axis_index("seq")
        self.chip, self.core = self.me // 2, self.me % 2
        self.other = self.me + 1 - 2 * self.core

    def hop(self, i, c, way, source=None):
        place = self.view(i, c)
        target = (self.me + 2, self.me - 2, self.other)[way]
        return remote(
            place if source is None else source,
            place,
            self.sent.at[i, c, way],
            self.landed.at[i, c],
            "seq",
            target,
        )

    def when(self, i, c, condition, action):
        has = self.has(i, c)
        if has is not None:
            condition = has if condition is None else has & condition
        if condition is None:
            action()
        else:
            pl.when(condition)(action)

    def spread(self, i, c, forward, backward, source=None):
        self.when(i, c, forward, lambda: self.hop(i, c, 0, source).start())
        self.when(i, c, backward, lambda: self.hop(i, c, 1, source).start())
        self.when(i, c, None, lambda: self.hop(i, c, 2, source).start())

    def start(self, chunks=None):
        for c in chunks or range(self.chunks):
            self.spread(
                self.me, c, self.chip < self.chips - 1, self.chip > 0, self.own(c) if self.own else None
            )

    def pass_on(self, distance, chunks=None):
        chunks = chunks or range(self.chunks)

        def from_before():
            i = self.me - 2 * distance
            for c in chunks:
                self.when(i, c, None, lambda: self.hop(i, c, 2).wait_recv())
                self.when(i, c, self.chip < self.chips - 1, lambda: self.hop(i, c, 0).start())
                self.when(i, c, None, lambda: self.hop(i, c, 2).start())

        def from_after():
            i = self.me + 2 * distance
            for c in chunks:
                self.when(i, c, None, lambda: self.hop(i, c, 2).wait_recv())
                self.when(i, c, self.chip > 0, lambda: self.hop(i, c, 1).start())
                self.when(i, c, None, lambda: self.hop(i, c, 2).start())

        pl.when(self.chip >= distance)(from_before)
        pl.when(self.chip + distance < self.chips)(from_after)

    def wait_other(self, i):
        for c in range(self.chunks):
            self.when(i, c, None, lambda: self.hop(i, c, 2).wait_recv())

    def from_other_core(self):
        for k in range(self.chips):
            self.wait_other(2 * k + 1 - self.core)

    def drain(self):
        for k in range(self.chips):
            i = 2 * k + self.core
            for c in range(self.chunks):
                forward = (self.chip >= k) & (self.chip < self.chips - 1)
                backward = (self.chip <= k) & (self.chip > 0)
                self.when(i, c, forward, lambda: self.hop(i, c, 0).wait_send())
                self.when(i, c, backward, lambda: self.hop(i, c, 1).wait_send())
                self.when(i, c, None, lambda: self.hop(i, c, 2).wait_send())


class PlaneGather:
    def __init__(self, own, view, parts, sent, landed):
        self.own, self.view, self.parts, self.sent, self.landed = own, view, parts, sent, landed
        me = lax.axis_index("fsdp")
        self.me = me
        self.beside = me + 1 - 2 * (me % 2)
        self.above = lax.rem(me + 2, 4)
        self.corner = lax.rem(self.beside + 2, 4)

    def whole(self, i, slot, target, source=None):
        place = self.view(i, None)
        return remote(
            place if source is None else source,
            place,
            self.sent.at[slot],
            self.landed.at[slot],
            "fsdp",
            target,
        )

    def part(self, i, slot, target):
        place = self.view(i, self.parts[slot - 2])
        return remote(place, place, self.sent.at[slot], self.landed.at[slot], "fsdp", target)

    def start(self):
        self.whole(self.me, 0, self.beside, self.own).start()
        self.whole(self.me, 1, self.above, self.own).start()

    def pass_on(self):
        self.whole(self.beside, 0, self.beside).wait_recv()
        self.part(self.beside, 2, self.above).start()
        self.whole(self.above, 1, self.above).wait_recv()
        self.part(self.above, 3, self.beside).start()

    def finish(self):
        self.part(self.corner, 2, self.above).wait_recv()
        self.part(self.corner, 3, self.beside).wait_recv()

    def drain(self):
        self.whole(self.me, 0, self.beside).wait_send()
        self.whole(self.me, 1, self.above).wait_send()
        self.part(self.beside, 2, self.above).wait_send()
        self.part(self.above, 3, self.beside).wait_send()


def group_of(device):
    third = (device + 5) // 8 - (device + 4) // 8
    fifth = (device + 3) // 8 - (device + 2) // 8
    return device - (device + 4) // 8 - (device + 2) // 8 + 3 * third + 3 * fifth


def device_of(group):
    return group + (group + 5) // 8 + (group + 4) // 8 - 5 * ((group + 2) // 8)


def own_blocks(device, columns, width, span):
    groups = -(-width // span)

    def block_at(column):
        return groups * (column // width) + (column % width) // span

    return block_at(device * columns), block_at(device * columns + columns - 1)


def norm_rows(values, gain, shift):
    centred = values - jnp.mean(values, axis=-1, keepdims=True)
    inverse = lax.rsqrt(jnp.mean(centred * centred, axis=-1, keepdims=True) + norm_eps)
    return (centred * inverse) * gain + shift


def attend(head, pair, start, first, count, tile, qkv_ref, ids_col, ids_row, out_ref, lse_ref):
    span = out_ref.shape[1]
    rows, keys = pl.ds(start, tile), pl.ds(first, count)

    def lanes(kind):
        return pl.ds(kind * span + pair * 128, 128)

    query = only_head(qkv_ref[rows, lanes(0)], head)
    scores = contract_last(query, qkv_ref[keys, lanes(1)]) * (HEAD_DIM**-0.5)
    q_pos = start + lax.broadcasted_iota(jnp.int32, (tile, count), 0)
    k_pos = first + lax.broadcasted_iota(jnp.int32, (tile, count), 1)
    allowed = (k_pos <= q_pos) & (ids_col[rows, :1] == ids_row[:1, keys])
    masked = jnp.where(allowed, scores, masked_score)
    top = jnp.max(masked, axis=1, keepdims=True)
    weights = jnp.exp(masked - top)
    total = jnp.sum(weights, axis=1, keepdims=True)
    probs = (weights * (1.0 / total)).astype(jnp.bfloat16)
    value = only_head(qkv_ref[keys, lanes(2)], head)
    mixed = jnp.dot(probs, value, preferred_element_type=jnp.float32)
    out_ref[rows, lanes(0)] += mixed.astype(jnp.bfloat16)
    lane = lax.broadcasted_iota(jnp.int32, (tile, lse_ref.shape[1]), 1)
    lse_ref[rows, :] = jnp.where(lane == 2 * pair + head, top + jnp.log(total), lse_ref[rows, :])


def attention_kernel(
    reach,
    x_ref,
    cot_ref,
    small_ref,
    blocks_ref,
    wo_ref,
    fc_ref,
    proj_ref,
    x_all,
    cot_all,
    small_all,
    vec_all,
    col_all,
    row_all,
    h1_all,
    qkv_all,
    w_all,
    lse_all,
    attn_own_out,
    attn_all,
    fc_all,
    proj_all,
    wo_all,
    x_v,
    small_v,
    vec,
    ids_col,
    ids_row,
    pieces,
    w_v,
    h1_v,
    qkv_v,
    attn_v,
    wo_z,
    wo_own,
    small_sent,
    small_landed,
    plane_sent,
    plane_landed,
    piece_sent,
    piece_landed,
    w_sent,
    w_landed,
    x_sent,
    x_landed,
    cot_sent,
    cot_landed,
    attn_sent,
    attn_landed,
    fc_sent,
    fc_landed,
    proj_sent,
    proj_landed,
    wo_sent,
    wo_landed,
    wo_plane_sent,
    wo_plane_landed,
    wo_pair_sent,
    wo_pair_landed,
    local_sem,
):
    row, plane = 8, 4
    seq, fsdp = lax.axis_index("seq"), lax.axis_index("fsdp")
    own_rows, width = x_ref.shape
    span = attn_v.shape[1]
    length = own_rows * row
    depth = blocks_ref.shape[1]
    groups = -(-width // span)
    group = group_of(seq)
    used = []

    def keep(source, target):
        copy = pltpu.make_async_copy(source, target, local_sem.at[len(used)])
        copy.start()
        used.append(copy)

    share = width // row

    vec[...] = jnp.zeros_like(vec)
    w_v[...] = jnp.zeros_like(w_v)
    greet(row, plane)
    own_small = pltpu.make_async_copy(small_ref, small_v.at[fsdp, seq], small_landed.at[seq])
    own_small.start()

    def small_to(target, slot):
        return remote(
            small_ref, small_v.at[fsdp, seq], small_sent.at[slot], small_landed.at[seq], "seq", target
        )

    for ahead in range(1, row):
        small_to(lax.rem(seq + ahead, row), ahead - 1).start()

    first_block, last_block = own_blocks(seq, qkv_columns(width, row), width, span)

    def piece(k):
        block = first_block + k
        kind, at = block // groups, block % groups
        begins = kind * width + at * span
        later = (seq * qkv_columns(width, row) + width * 3 - begins - 1) // (width * 3)
        target = device_of(at)
        place = pieces.at[kind, later]
        return block <= last_block, target, place, piece_landed.at[kind, later]

    for k in range(4):
        there, target, place, landed = piece(k)

        @pl.when(there & (target == seq))
        def _():
            pltpu.make_async_copy(blocks_ref.at[k], place, landed).start()

        @pl.when(there & (target != seq))
        def _():
            remote(blocks_ref.at[k], place, piece_sent.at[k], landed, "seq", target).start()

    def block_of(target):
        return lambda i, c: target.at[pl.ds(pl.multiple_of(i * own_rows, own_rows), own_rows)]

    x_line = RowGather(lambda c: x_ref, block_of(x_v), x_sent, x_landed, row)
    own_x = pltpu.make_async_copy(x_ref, block_of(x_v)(seq, 0), local_sem.at[0])
    own_x.start()
    used.append(None)
    x_line.start()

    wo_line = RowGather(lambda c: wo_ref, lambda i, c: wo_z.at[i], wo_sent, wo_landed, row)
    wo_line.start()
    keep(wo_ref, wo_z.at[seq])
    def slab(target):
        def view(i, part):
            start, count = (0, target.shape[1]) if part is None else part
            return target.at[i, pl.ds(start, count)]

        return view

    units = fc_ref.shape[0]
    cut = units // 32 * 16
    parts = ((0, cut), (cut, units - cut))
    fc_plane = PlaneGather(fc_ref, slab(fc_all), parts, fc_sent, fc_landed)
    proj_plane = PlaneGather(proj_ref, slab(proj_all), parts, proj_sent, proj_landed)
    fc_plane.start()

    for other in range(row):
        pltpu.make_async_copy(small_ref, small_v.at[fsdp, other], small_landed.at[other]).wait()

    def small_plane(ahead):
        return remote(
            small_v.at[fsdp],
            small_v.at[fsdp],
            plane_sent.at[ahead - 1],
            plane_landed.at[ahead - 1],
            "fsdp",
            lax.rem(fsdp + ahead, plane),
        )

    for ahead in range(1, plane):
        small_plane(ahead).start()
    for other in range(row):
        lanes = pl.ds(other * own_rows, own_rows)
        ids = jnp.broadcast_to(small_v[fsdp, other, 3:4, :own_rows], (own_rows, own_rows))
        ids_row[:, lanes] = ids[:8]
        ids_col[lanes, :] = ids.T
    for ahead in range(1, plane):
        remote(
            small_v.at[fsdp],
            small_v.at[lax.rem(fsdp + plane - ahead, plane)],
            plane_sent.at[ahead - 1],
            plane_landed.at[ahead - 1],
            "fsdp",
            lax.rem(fsdp + ahead, plane),
        ).wait_recv()
    for i in range(plane):
        for other in range(row):
            vec[2 * i : 2 * i + 2, share * other : share * (other + 1)] = small_v[i, other, 0:2, :share]

    own_w = pl.ds(pl.multiple_of(fsdp * depth, 16), depth)

    @pl.when(group < groups)
    def _():
        for kind in range(3):
            begins = kind * width + group * span
            ends = begins + jnp.minimum(span, width - group * span) - 1
            cols = qkv_columns(width, row)
            straddles = ends // cols != begins // cols
            pltpu.make_async_copy(
                blocks_ref.at[0], pieces.at[kind, 0], piece_landed.at[kind, 0]
            ).wait()
            w_v[own_w, kind * span : (kind + 1) * span] = pieces[kind, 0]

            @pl.when(straddles)
            def _():
                pltpu.make_async_copy(
                    blocks_ref.at[0], pieces.at[kind, 1], piece_landed.at[kind, 1]
                ).wait()
                w_v[own_w, kind * span : (kind + 1) * span] = pieces[kind, 0] + pieces[kind, 1]

    def w_view(i, part):
        start, count = (0, depth) if part is None else part
        return w_v.at[pl.ds(pl.multiple_of(i * depth + start, 16), count)]

    half = depth // 32 * 16
    w_plane = PlaneGather(None, w_view, ((0, half), (half, depth - half)), w_sent, w_landed)
    w_plane.start()

    def norm_block(i):
        def part(j):
            rows = pl.ds(pl.multiple_of(i * own_rows + j, norm_part), norm_part)
            hidden = norm_rows(x_v[rows, :].astype(jnp.float32), vec[0:1, :width], vec[1:2, :width])
            h1_v[rows, :] = hidden.astype(jnp.bfloat16)

        row_tiles(own_rows, norm_part, part)

    def norm_arrived(distance):
        if 0 < distance < row // 2:
            pl.when(x_line.chip >= distance)(lambda: norm_block(seq - 2 * distance))
            pl.when(x_line.chip + distance < row // 2)(lambda: norm_block(seq + 2 * distance))

        def other(i):
            x_line.wait_other(i)
            norm_block(i)

        if distance == 1:
            other(x_line.other)
        elif distance > 1:
            nearer = distance - 1
            pl.when(x_line.chip >= nearer)(lambda: other(x_line.other - 2 * nearer))
            pl.when(x_line.chip + nearer < row // 2)(lambda: other(x_line.other + 2 * nearer))

    own_x.wait()
    norm_block(seq)
    x_line.pass_on(1)
    wo_line.pass_on(1)
    norm_arrived(1)
    w_plane.pass_on()
    x_line.pass_on(2)
    wo_line.pass_on(2)
    norm_arrived(2)
    x_line.pass_on(3)
    wo_line.pass_on(3)
    cot_line = RowGather(lambda c: cot_ref, block_of(cot_all), cot_sent, cot_landed, row)
    cot_line.start()
    norm_arrived(3)
    keep(cot_ref, block_of(cot_all)(seq, 0))
    keep(fc_ref, fc_all.at[fsdp])
    keep(proj_ref, proj_all.at[fsdp])
    norm_arrived(4)
    w_plane.finish()
    fc_plane.pass_on()

    wo_line.from_other_core()
    used[1].wait()
    used[1] = None
    for i in range(row):
        wo_own[:, share * i : share * (i + 1)] = wo_z[i]
    wo_cut = 6 * 128
    wo_lanes = ((0, wo_cut), (wo_cut, width - wo_cut))

    def wo_view(lanes):
        def view(i, part):
            start, count = (0, depth) if part is None else part
            rows = pl.ds(pl.multiple_of(i * depth + start, 16), count)
            return wo_all.at[rows, pl.ds(*lanes)]

        return view

    wo_planes = [
        PlaneGather(
            wo_own.at[:, pl.ds(*lanes)],
            wo_view(lanes),
            ((0, half), (half, depth - half)),
            wo_plane_sent,
            wo_plane_landed,
        )
        for lanes in wo_lanes
    ]

    def wo_pair(core, ahead):
        i = lax.rem(fsdp + ahead, plane)
        place = wo_view(wo_lanes[core])(i, None)
        return remote(place, place, wo_pair_sent.at[i], wo_pair_landed.at[i], "seq", x_line.other)

    def wo_pairs(action, core):
        for ahead in range(1, plane):
            action(wo_pair(core, ahead))

    def on_own_core(action):
        for core in range(2):
            pl.when(x_line.core == core)(functools.partial(action, core))

    on_own_core(lambda core: wo_planes[core].start())
    proj_plane.start()
    keep(wo_own, wo_view((0, width))(fsdp, None))
    lanes = pl.ds(pl.multiple_of(group * span, span), span)
    query_shift, value_shift = vec[2:3, lanes], vec[3:4, lanes]

    def project(i):
        rows = pl.ds(i, 2 * own_rows)
        mixed = jnp.dot(h1_v[rows, :], w_v[...], preferred_element_type=jnp.float32)
        qkv_v[rows, :span] = (mixed[:, :span] + query_shift).astype(jnp.bfloat16)
        qkv_v[rows, span : 2 * span] = mixed[:, span : 2 * span].astype(jnp.bfloat16)
        qkv_v[rows, 2 * span :] = (mixed[:, 2 * span :] + value_shift).astype(jnp.bfloat16)

    row_tiles(length, 2 * own_rows, project)
    cot_line.pass_on(1)
    keep(x_v, x_all)
    keep(small_v, small_all)
    keep(vec, vec_all)
    keep(ids_col, col_all)
    keep(ids_row, row_all)
    keep(h1_v, h1_all)
    keep(qkv_v, qkv_all)
    keep(w_v, w_all)

    attn_v[...] = jnp.zeros_like(attn_v)
    lse_all[...] = jnp.zeros_like(lse_all)
    tile = 256

    def heads(pair):
        def head(h, carry):
            for start, first, count in tile_pairs(length, tile, reach):
                attend(h, pair, start, first, count, tile, qkv_v, ids_col, ids_row, attn_v, lse_all)
            return carry

        lax.fori_loop(0, 2, head, 0)

    heads(0)

    def chunk(i, c):
        return attn_all.at[:, pl.ds(pl.multiple_of(group_of(i) * span + c * 128, 128), 128)]

    attn_line = RowGather(
        lambda c: attn_v.at[:, pl.ds(c * 128, 128)],
        chunk,
        attn_sent,
        attn_landed,
        row,
        chunks=2,
        has=lambda i, c: group_of(i) < groups - c,
    )
    def own_chunk(c):
        lanes = pl.ds(pl.multiple_of(group * span + c * 128, 128), 128)
        return pltpu.make_async_copy(
            attn_v.at[:, pl.ds(c * 128, 128)], attn_all.at[:, lanes], piece_landed.at[c, 0]
        )

    def send_chunk(c):
        attn_line.start([c])
        pl.when(group < groups - c)(lambda: own_chunk(c).start())

    send_chunk(0)
    fc_plane.finish()
    on_own_core(lambda core: wo_planes[core].pass_on())
    heads(1)
    send_chunk(1)
    keep(attn_v, attn_own_out)
    for distance in range(1, row // 2):
        attn_line.pass_on(distance, [0])
        attn_line.pass_on(distance, [1])
        if distance == 2:
            proj_plane.pass_on()
            on_own_core(lambda core: wo_planes[core].finish())
            on_own_core(lambda core: wo_pairs(lambda copy: copy.start(), core))
    cot_line.pass_on(2)
    cot_line.pass_on(3)
    attn_line.from_other_core()
    cot_line.from_other_core()
    on_own_core(lambda core: wo_pairs(lambda copy: copy.wait_recv(), 1 - core))
    proj_plane.finish()

    for c in range(2):
        pl.when(group < groups - c)(lambda: own_chunk(c).wait())
    for ahead in range(1, row):
        small_to(lax.rem(seq + ahead, row), ahead - 1).wait_send()
    for ahead in range(1, plane):
        small_plane(ahead).wait_send()
    for k in range(4):
        there, target, place, landed = piece(k)

        @pl.when(there & (target != seq))
        def _():
            remote(blocks_ref.at[k], place, piece_sent.at[k], landed, "seq", target).wait_send()

    for line in (x_line, wo_line, cot_line, attn_line, w_plane, fc_plane, proj_plane):
        line.drain()
    on_own_core(lambda core: wo_planes[core].drain())
    on_own_core(lambda core: wo_pairs(lambda copy: copy.wait_send(), core))
    for copy in used:
        if copy is not None:
            copy.wait()


def qkv_columns(width, row):
    return 3 * width // row


def attention_phase(x_own, cot_own, small, blocks, wo_own, fc_own, proj_own, reach):
    own_rows, width = x_own.shape
    row, plane, span = 8, 4, 256
    length = own_rows * row
    units = fc_own.shape[0]
    bf, f32 = jnp.bfloat16, jnp.float32
    anywhere = pl.BlockSpec(memory_space=pl.ANY)
    in_vmem = pl.BlockSpec(memory_space=pltpu.VMEM)
    dma = pltpu.SemaphoreType.DMA

    def shaped(*shape, dtype=bf):
        return jax.ShapeDtypeStruct(shape, dtype)

    return pl.pallas_call(
        lambda *refs: attention_kernel(reach, *refs),
        out_shape=[
            shaped(length, width),
            shaped(length, width),
            shaped(plane, row, 8, span, dtype=f32),
            shaped(8, 8 * span, dtype=f32),
            shaped(length, own_rows, dtype=f32),
            shaped(8, length, dtype=f32),
            shaped(length, width),
            shaped(length, 3 * span),
            shaped(width, 3 * span),
            shaped(length, 128, dtype=f32),
            shaped(length, span),
            shaped(length, 7 * span),
            shaped(plane, units, width),
            shaped(plane, units, width),
            shaped(8 * span, width),
        ],
        in_specs=[anywhere] * 7,
        out_specs=[anywhere] * 9 + [in_vmem] + [anywhere] * 5,
        scratch_shapes=[
            pltpu.VMEM((length, width), bf),
            pltpu.VMEM((plane, row, 8, span), f32),
            pltpu.VMEM((8, 8 * span), f32),
            pltpu.VMEM((length, own_rows), f32),
            pltpu.VMEM((8, length), f32),
            pltpu.VMEM((3, 2, width // plane, span), bf),
            pltpu.VMEM((width, 3 * span), bf),
            pltpu.VMEM((length, width), bf),
            pltpu.VMEM((length, 3 * span), bf),
            pltpu.VMEM((length, span), bf),
            pltpu.VMEM((row,) + wo_own.shape, bf),
            pltpu.VMEM((width // plane, width), bf),
            dma((row - 1,)),
            dma((row,)),
            dma((plane - 1,)),
            dma((plane - 1,)),
            dma((4,)),
            dma((3, 2)),
            dma((4,)),
            dma((4,)),
            dma((row, 1, 3)),
            dma((row, 1)),
            dma((row, 1, 3)),
            dma((row, 1)),
            dma((row, 2, 3)),
            dma((row, 2)),
            dma((4,)),
            dma((4,)),
            dma((4,)),
            dma((4,)),
            dma((row, 1, 3)),
            dma((row, 1)),
            dma((4,)),
            dma((4,)),
            dma((4,)),
            dma((4,)),
            dma((20,)),
        ],
        compiler_params=pltpu.CompilerParams(
            collective_id=0, has_side_effects=True, vmem_limit_bytes=50 * 1024 * 1024
        ),
    )(x_own, cot_own, small, blocks, wo_own, fc_own, proj_own)


def pick(index, values):
    chosen = values[-1]
    for k in range(len(values) - 1):
        chosen = jnp.where(index == k, values[k], chosen)
    return chosen


def chip_order(chip, step):
    rows = ((3, 3, 0, 0), (2, 0, 3, 1), (1, 2, 1, 2), (0, 1, 2, 3))
    return pick(step, [pick(chip, row) for row in rows])


class RowSum:
    def __init__(self, own, away, pair, chain, pair_sent, pair_landed, chain_sent, chain_landed):
        self.own, self.away, self.pair, self.chain = own, away, pair, chain
        self.pair_sent, self.pair_landed = pair_sent, pair_landed
        self.chain_sent, self.chain_landed = chain_sent, chain_landed
        self.me = lax.axis_index("seq")
        self.chips = 4
        self.chip, self.core = self.me // 2, self.me % 2
        self.other = self.me + 1 - 2 * self.core

    def exchange(self, t):
        return remote(
            self.away.at[t],
            self.pair.at[t],
            self.pair_sent.at[t],
            self.pair_landed.at[t],
            "seq",
            self.other,
        )

    def onward(self, t, slot, target):
        return remote(
            self.own.at[t],
            self.chain.at[slot],
            self.chain_sent.at[t],
            self.chain_landed.at[slot],
            "seq",
            target,
        )

    def put(self, t, terms):
        rows = self.own.shape[1]
        self.away[t] = terms[pl.ds(pl.multiple_of((1 - self.core) * rows, rows), rows), :].astype(
            jnp.bfloat16
        )
        self.exchange(t).start()
        self.own[t] = terms[pl.ds(pl.multiple_of(self.core * rows, rows), rows), :].astype(jnp.bfloat16)

    def add(self, t, arrived, slot):
        total = self.own[t].astype(jnp.float32) + arrived[slot].astype(jnp.float32)
        self.own[t] = total.astype(jnp.bfloat16)

    def step(self, t):
        self.exchange(t).wait_recv()
        self.add(t, self.pair, t)

        def forward():
            @pl.when(self.chip > 0)
            def _():
                self.onward(t, t, self.me + 2).wait_recv()
                self.add(t, self.chain, t)

            self.onward(t, t, self.me + 2).start()

        def backward():
            @pl.when(self.chip < self.chips - 1)
            def _():
                self.onward(t, t, self.me - 2).wait_recv()
                self.add(t, self.chain, t)

            slot = jnp.where(t == self.chip - 1, self.chips, t)
            self.onward(t, slot, self.me - 2).start()

        pl.when(t > self.chip)(forward)
        pl.when(t < self.chip)(backward)

    def final(self, total):
        t = self.chip
        self.exchange(t).wait_recv()
        total[...] = self.own[t].astype(jnp.float32) + self.pair[t].astype(jnp.float32)

        @pl.when(self.chip > 0)
        def _():
            self.onward(t, t, self.other).wait_recv()
            total[...] += self.chain[t].astype(jnp.float32)

        @pl.when(self.chip < self.chips - 1)
        def _():
            self.onward(t, self.chips, self.other).wait_recv()
            total[...] += self.chain[self.chips].astype(jnp.float32)

    def drain(self):
        for t in range(self.chips):
            self.exchange(t).wait_send()

            @pl.when(self.chip != t)
            def _():
                self.onward(t, t, self.other).wait_send()


class PlaneTerms:
    def __init__(self, view, terms, sent, landed):
        self.view, self.terms, self.sent, self.landed = view, terms, sent, landed
        self.me = lax.axis_index("fsdp")

    def to(self, ahead):
        i = lax.rem(self.me + ahead, 4)
        return remote(
            self.view(i), self.terms.at[self.me], self.sent.at[ahead], self.landed.at[self.me], "fsdp", i
        )

    def keep(self):
        return pltpu.make_async_copy(
            self.view(self.me), self.terms.at[self.me], self.landed.at[self.me]
        )

    def start(self):
        self.keep().start()
        for ahead in (3, 1, 2):
            self.to(ahead).start()

    def arrive(self):
        self.keep().wait()
        for ahead in range(1, 4):
            i = lax.rem(self.me + ahead, 4)
            remote(
                self.view(i), self.terms.at[i], self.sent.at[ahead], self.landed.at[i], "fsdp", i
            ).wait_recv()

    def drain(self):
        for ahead in range(1, 4):
            self.to(ahead).wait_send()


def backward_attend(
    head, start, first, count, tile, qkv_ref, attn_ref, grad_ref, lse_ref, ids_col, ids_row, out_ref
):
    span = attn_ref.shape[1]
    scale = HEAD_DIM**-0.5
    rows, keys = pl.ds(start, tile), pl.ds(first, count)
    query = only_head(qkv_ref[rows, :span], head)
    key = qkv_ref[keys, span : 2 * span]
    grad = only_head(grad_ref[rows, :], head)
    delta = jnp.sum(
        grad.astype(jnp.float32) * attn_ref[rows, :].astype(jnp.float32), axis=1, keepdims=True
    )
    scores = contract_last(query, key) * scale
    q_pos = start + lax.broadcasted_iota(jnp.int32, (tile, count), 0)
    k_pos = first + lax.broadcasted_iota(jnp.int32, (tile, count), 1)
    allowed = (k_pos <= q_pos) & (ids_col[rows, :1] == ids_row[:1, keys])
    lane = lax.broadcasted_iota(jnp.int32, (tile, lse_ref.shape[1]), 1)
    lse = jnp.sum(jnp.where(lane == head, lse_ref[rows, :], 0.0), axis=1, keepdims=True)
    probs = jnp.where(allowed, jnp.exp(scores - lse), 0.0)
    prob_grad = contract_last(grad, qkv_ref[keys, 2 * span :])
    score_grad = (probs * (prob_grad - delta)).astype(jnp.bfloat16)
    out_ref[rows, :span] += scale * jnp.dot(
        score_grad, only_head(key, head), preferred_element_type=jnp.float32
    )
    out_ref[keys, span : 2 * span] += scale * contract_first(score_grad, query)
    out_ref[keys, 2 * span :] += contract_first(probs.astype(jnp.bfloat16), grad)


def backward_kernel(
    reach,
    x_ref,
    cot_ref,
    vec_ref,
    bias_ref,
    w_attn_ref,
    attn_ref,
    fc_ref,
    proj_ref,
    h1_ref,
    qkv_ref,
    w_qkv_ref,
    lse_ref,
    attn_own_ref,
    ids_col_ref,
    ids_row_ref,
    result_ref,
    input_grad_ref,
    fc_terms,
    proj_terms,
    attn_terms,
    nat_blocks,
    vec_out,
    qkv_terms,
    attn_v,
    own1,
    away1,
    pair1,
    chain1,
    own2,
    away2,
    pair2,
    chain2,
    dr_all,
    resid_own,
    dresid_own,
    total,
    wide,
    fc_stage,
    proj_stage,
    vec_v,
    bias_v,
    bias_sum,
    gv,
    vec_send,
    vec_land,
    plane_send,
    plane_land,
    pair_sent,
    pair_landed,
    chain_sent,
    chain_landed,
    dr_sent,
    dr_landed,
    terms_sent,
    terms_landed,
    nat_sent,
    nat_landed,
    vec_sent,
    vec_landed,
    plane_sent,
    plane_landed,
    load_sem,
):
    row, plane, chips = 8, 4, 4
    seq, fsdp = lax.axis_index("seq"), lax.axis_index("fsdp")
    chip, core = seq // 2, seq % 2
    ends = (chip == 0) | (chip == chips - 1)
    length, width = x_ref.shape
    own_rows = length // row
    pair_rows = 2 * own_rows
    units = fc_ref.shape[1]
    span = attn_own_ref.shape[1]
    depth = width // plane
    groups = -(-width // span)
    group = group_of(seq)
    columns = qkv_columns(width, row)
    bf, f32 = jnp.bfloat16, jnp.float32
    tiles = [(0, 512), (512, 1024), (1024, width)]

    def load(source, target, slot):
        copy = pltpu.make_async_copy(source, target, load_sem.at[slot])
        copy.start()
        return copy

    def pair_at(t):
        return pl.ds(pl.multiple_of(t * pair_rows, pair_rows), pair_rows)

    own_at = pl.ds(pl.multiple_of(seq * own_rows, own_rows), own_rows)
    half_at = pl.ds(pl.multiple_of(core * own_rows, own_rows), own_rows)
    hidden_sum = RowSum(
        own1, away1, pair1, chain1, pair_sent.at[0], pair_landed.at[0], chain_sent.at[0], chain_landed.at[0]
    )
    out_sum = RowSum(
        own2, away2, pair2, chain2, pair_sent.at[1], pair_landed.at[1], chain_sent.at[1], chain_landed.at[1]
    )
    dr_line = RowGather(
        None,
        lambda i, c: dr_all.at[pl.ds(pl.multiple_of(i * own_rows, own_rows), own_rows)],
        dr_sent,
        dr_landed,
        row,
    )
    fc_plane = PlaneTerms(lambda i: fc_stage.at[i], fc_terms, terms_sent.at[0], terms_landed.at[0])
    proj_plane = PlaneTerms(lambda i: proj_stage.at[i], proj_terms, terms_sent.at[1], terms_landed.at[1])

    def feed_forward(w_attn, x_v, cot_v, fc_v, proj_v, h2_v, act_v, dpre_v, pre_v, dact_v):
        first = chip_order(chip, 0)
        loads = [
            load(attn_ref, attn_v, 0),
            load(w_attn_ref.at[pl.ds(0, width)], w_attn, 1),
            load(x_ref.at[pair_at(first)], x_v, 2),
            load(vec_ref, vec_v, 3),
            load(fc_ref, fc_v, 4),
            load(cot_ref, cot_v, 5),
            load(proj_ref, proj_v, 6),
            load(bias_ref, bias_v, 7),
        ]
        bias_sum[...] = jnp.zeros_like(bias_sum)
        gv[...] = jnp.zeros_like(gv)
        greet(row, plane)
        for copy in loads[:4]:
            copy.wait()

        def back_through(rows, values, weights):
            for low, high in tiles:
                terms = jnp.dot(
                    values[0, rows, :], weights[0, :, low:high], preferred_element_type=f32
                )
                for f in range(1, plane):
                    terms += jnp.dot(
                        values[f, rows, :], weights[f, :, low:high], preferred_element_type=f32
                    )
                wide[:, low:high] = terms

        def chunk(p, carry):
            t = chip_order(chip, p)
            rows = pair_at(t)
            for low, high in tiles:
                wide[:, low:high] = jnp.dot(
                    attn_v[rows, :width], w_attn[:, low:high], preferred_element_type=f32
                )

            @pl.when(p > 0)
            def _():
                pltpu.make_async_copy(x_ref.at[rows], x_v, load_sem.at[2]).wait()

            def second_norm(i):
                part = pl.ds(i, norm_part)
                resid = wide[part, :] + x_v[part, :].astype(f32) + vec_v[4:5, :width]
                wide[part, :] = resid
                hidden = norm_rows(resid, vec_v[5:6, :width], vec_v[6:7, :width])
                h2_v[pl.ds(pl.multiple_of(t * pair_rows + i, norm_part), norm_part), :] = hidden.astype(bf)

            row_tiles(pair_rows, norm_part, second_norm)

            @pl.when(p < chips - 1)
            def _():
                load(x_ref.at[pair_at(chip_order(chip, p + 1))], x_v, 2)

            @pl.when(t == chip)
            def _():
                resid_own[...] = wide[half_at, :]

            def unit_block(f, carry):
                pre_v[...] = contract_last(h2_v[rows, :], fc_v[f])
                dact_v[...] = contract_last(cot_v[rows, :], proj_v[f])
                shift = bias_v[pl.ds(f, 1), :units]

                def gelu(i):
                    part = pl.ds(i, 32)
                    gelu_value, gelu_slope = gelu_parts(pre_v[part, :] + shift)
                    dpre = dact_v[part, :] * gelu_slope
                    place = pl.ds(pl.multiple_of(t * pair_rows + i, 32), 32)
                    act_v[f, place, :] = gelu_value.astype(bf)
                    dpre_v[f, place, :] = dpre.astype(bf)
                    bias_sum[pl.ds(f, 1), :units] += jnp.sum(dpre, axis=0, keepdims=True)

                row_tiles(pair_rows, 32, gelu)
                return carry

            @pl.when(p == 0)
            def _():
                for copy in loads[4:]:
                    copy.wait()

            lax.fori_loop(0, plane, unit_block, 0)

            back_through(rows, dpre_v, fc_v)
            hidden_sum.put(t, wide)

            @pl.when(ends & (p < chips - 1))
            def _():
                hidden_sum.step(t)

            @pl.when(jnp.logical_not(ends) & (p > 0) & (p < chips - 1))
            def _():
                hidden_sum.step(chip_order(chip, p - 1))

            return carry

        lax.fori_loop(0, chips, chunk, 0)

        @pl.when(jnp.logical_not(ends))
        def _():
            hidden_sum.step(chip_order(chip, 2))

        hidden_sum.final(total)

        def second_norm_back(i):
            part = pl.ds(i, norm_part)
            resid = resid_own[part, :]
            centred = resid - jnp.mean(resid, axis=-1, keepdims=True)
            inverse = lax.rsqrt(jnp.mean(centred * centred, axis=-1, keepdims=True) + norm_eps)
            normed = centred * inverse
            grad_hidden = total[part, :]
            scaled = grad_hidden * vec_v[5:6, :width]
            back = inverse * (
                scaled
                - jnp.mean(scaled, axis=-1, keepdims=True)
                - normed * jnp.mean(scaled * normed, axis=-1, keepdims=True)
            )
            place = pl.ds(pl.multiple_of(seq * own_rows + i, norm_part), norm_part)
            cot = cot_v[place, :].astype(f32)
            grad_resid = cot + back
            dresid_own[part, :] = grad_resid
            dr_all[place, :] = grad_resid.astype(bf)
            for at, values in ((4, grad_resid), (5, grad_hidden * normed), (6, grad_hidden), (7, cot)):
                gv[at : at + 1, :width] += jnp.sum(values, axis=0, keepdims=True)

        row_tiles(own_rows, norm_part, second_norm_back)
        dr_line.start()

        def out_chunk(p, carry):
            t = chip_order(chip, p)
            back_through(pair_at(t), act_v, proj_v)
            out_sum.put(t, wide)

            @pl.when(ends & (p < chips - 1))
            def _():
                out_sum.step(t)

            return carry

        def weight_terms(values, others, stage):
            def unit_block(f, carry):
                for low, high in tiles:
                    stage[f, :, low:high] = contract_first(values[f], others[:, low:high]).astype(bf)
                return carry

            lax.fori_loop(0, plane, unit_block, 0)

        weight_terms(act_v, cot_v, proj_stage)
        proj_plane.start()
        weight_terms(dpre_v, h2_v, fc_stage)
        fc_plane.start()
        dr_line.pass_on(1)
        lax.fori_loop(0, chips, out_chunk, 0)
        dr_line.pass_on(2)

    pl.run_scoped(
        feed_forward,
        pltpu.VMEM((width, width), bf),
        pltpu.VMEM((pair_rows, width), bf),
        pltpu.VMEM((length, width), bf),
        pltpu.VMEM((plane, units, width), bf),
        pltpu.VMEM((plane, units, width), bf),
        pltpu.VMEM((length, width), bf),
        pltpu.VMEM((plane, length, units), bf),
        pltpu.VMEM((plane, length, units), bf),
        pltpu.VMEM((pair_rows, units), f32),
        pltpu.VMEM((pair_rows, units), f32),
    )

    def attention_back(w_rows, h1_v, qkv_v, w_qkv, lse_v, attn_own, col_v, row_v, da_v, dqkv, dqkv16, ga, gq, gqt, own_x):
        loads = [
            load(w_attn_ref.at[pl.ds(pl.multiple_of(group * span, span), span)], w_rows, 0),
            load(qkv_ref, qkv_v, 1),
            load(lse_ref, lse_v, 2),
            load(attn_own_ref, attn_own, 3),
            load(ids_col_ref, col_v, 4),
            load(ids_row_ref, row_v, 5),
            load(h1_ref, h1_v, 6),
            load(w_qkv_ref, w_qkv, 7),
            load(x_ref.at[own_at], own_x, 8),
        ]
        dqkv[...] = jnp.zeros_like(dqkv)
        dr_line.pass_on(3)
        dr_line.from_other_core()
        for copy in loads[:6]:
            copy.wait()

        inside = lax.broadcasted_iota(jnp.int32, w_rows.shape, 0) < width - group * span
        w_rows[...] = jnp.where(inside, w_rows[...], jnp.zeros_like(w_rows))

        def into_heads(i):
            rows = pl.ds(i, pair_rows)
            da_v[rows, :] = contract_last(dr_all[rows, :], w_rows[...]).astype(bf)

        row_tiles(length, pair_rows, into_heads)

        @pl.when(jnp.logical_not(ends))
        def _():
            out_sum.step(chip_order(chip, 0))

        def heads(h, carry):
            for start, first, count in tile_pairs(length, 256, reach):
                backward_attend(
                    h, start, first, count, 256, qkv_v, attn_own, da_v, lse_v, col_v, row_v, dqkv
                )
            return carry

        lax.fori_loop(0, 2, heads, 0)

        @pl.when(jnp.logical_not(ends))
        def _():
            out_sum.step(chip_order(chip, 1))

        lax.fori_loop(2, 4, heads, 0)

        @pl.when(jnp.logical_not(ends))
        def _():
            out_sum.step(chip_order(chip, 2))

        lanes = pl.ds(pl.multiple_of(group * span, span), span)
        gv[2:3, lanes] = jnp.sum(dqkv[:, :span], axis=0, keepdims=True)
        gv[3:4, lanes] = jnp.sum(dqkv[:, 2 * span :], axis=0, keepdims=True)
        dqkv16[...] = dqkv[...].astype(bf)

        for copy in loads[6:]:
            copy.wait()
        for low in range(0, width, span):
            high = min(low + span, width)
            gq[low:high, :] = contract_first(h1_v[:, low:high], dqkv16[...]).astype(bf)
        qkv_plane = PlaneTerms(
            lambda i: gq.at[pl.ds(pl.multiple_of(i * depth, 16), depth)],
            qkv_terms,
            terms_sent.at[2],
            terms_landed.at[2],
        )
        qkv_plane.start()

        hidden_sum.drain()

        def chunk(p, carry):
            t = chip_order(chip, p)
            for low, high in tiles:
                wide[:, low:high] = contract_last(dqkv16[pair_at(t), :], w_qkv[low:high, :])
            hidden_sum.put(t, wide)

            @pl.when(ends & (p < chips - 1))
            def _():
                hidden_sum.step(t)

            return carry

        lax.fori_loop(0, chips, chunk, 0)

        share = width // row
        place = lax.broadcasted_iota(jnp.int32, (width, span), 0)
        lane = lax.broadcasted_iota(jnp.int32, (width, span), 1)
        chosen = ((place == seq * share + lane) & (lane < share)).astype(f32).astype(bf)

        def own_columns(i):
            rows = pl.ds(i, pair_rows)
            da_v[rows, :] = jnp.dot(dr_all[rows, :], chosen, preferred_element_type=f32).astype(bf)

        row_tiles(length, pair_rows, own_columns)
        for low in range(0, width, span):
            high = min(low + span, width)
            ga[low:high, :] = contract_first(attn_v[:, low:high], da_v[...]).astype(bf)
        attn_plane = PlaneTerms(
            lambda i: ga.at[pl.ds(pl.multiple_of(i * depth, 16), depth)],
            attn_terms,
            terms_sent.at[3],
            terms_landed.at[3],
        )
        attn_plane.start()

        @pl.when(jnp.logical_not(ends))
        def _():
            for p in range(chips - 1):
                hidden_sum.step(chip_order(chip, p))

        out_sum.final(total)
        for low, high in tiles:
            result_ref[:, low:high] = (
                resid_own[:, low:high] + total[:, low:high] + vec_v[7:8, low:high]
            )

        qkv_plane.arrive()
        load(qkv_terms, gqt, 0).wait()
        qkv_plane.drain()
        for kind in range(3):
            part = gqt[0, :, kind * span : (kind + 1) * span].astype(f32)
            for f in range(1, plane):
                part += gqt[f, :, kind * span : (kind + 1) * span].astype(f32)
            gq[kind * depth : (kind + 1) * depth, :span] = part.astype(bf)

        def nat(kind, late):
            begins = kind * width + group * span
            last = begins + jnp.minimum(span, width - group * span) - 1
            before, after = begins // columns, last // columns
            target = after if late else before
            slot = kind * groups + group - own_blocks(target, columns, width, span)[0]
            there = (group < groups) & (before != after) if late else group < groups
            return there, target, slot

        def nat_copy(kind, late, target, slot):
            return remote(
                gq.at[pl.ds(kind * depth, depth), pl.ds(0, span)],
                nat_blocks.at[slot],
                nat_sent.at[kind, late],
                nat_landed.at[slot],
                "seq",
                target,
            )

        for kind in range(3):
            for late in range(2):
                there, target, slot = nat(kind, late)

                @pl.when(there & (target != seq))
                def _():
                    nat_copy(kind, late, target, slot).start()

                @pl.when(there & (target == seq))
                def _():
                    pltpu.make_async_copy(
                        gq.at[pl.ds(kind * depth, depth), pl.ds(0, span)],
                        nat_blocks.at[slot],
                        nat_landed.at[slot],
                    ).start()

        hidden_sum.final(total)

        def first_norm_back(i):
            part = pl.ds(i, norm_part)
            values = own_x[part, :].astype(f32)
            centred = values - jnp.mean(values, axis=-1, keepdims=True)
            inverse = lax.rsqrt(jnp.mean(centred * centred, axis=-1, keepdims=True) + norm_eps)
            normed = centred * inverse
            grad_hidden = total[part, :]
            scaled = grad_hidden * vec_v[0:1, :width]
            back = inverse * (
                scaled
                - jnp.mean(scaled, axis=-1, keepdims=True)
                - normed * jnp.mean(scaled * normed, axis=-1, keepdims=True)
            )
            input_grad_ref[part, :] = dresid_own[part, :] + back
            for at, summed in ((0, grad_hidden * normed), (1, grad_hidden)):
                gv[at : at + 1, :width] += jnp.sum(summed, axis=0, keepdims=True)

        row_tiles(own_rows, norm_part, first_norm_back)

        vec_send[...] = jnp.zeros_like(vec_send)
        plane_send[...] = jnp.zeros_like(plane_send)
        for i in range(row):
            vec_send[i, :, :share] = gv[:, share * i : share * (i + 1)]

        def vec_to(ahead):
            i = lax.rem(seq + ahead, row)
            return remote(
                vec_send.at[i], vec_land.at[seq], vec_sent.at[ahead], vec_landed.at[seq], "seq", i
            )

        keep = pltpu.make_async_copy(vec_send.at[seq], vec_land.at[seq], vec_landed.at[seq])
        keep.start()
        for ahead in range(1, row):
            vec_to(ahead).start()
        for i in range(row):
            pltpu.make_async_copy(vec_send.at[i], vec_land.at[i], vec_landed.at[i]).wait()
        summed = vec_land[0]
        for i in range(1, row):
            summed += vec_land[i]
        for i in range(plane):
            plane_send[i, 0:2, :] = summed[2 * i : 2 * i + 2, :]
            plane_send[i, 2:3, :] = bias_sum[i : i + 1, :]
        vec_plane = PlaneTerms(lambda i: plane_send.at[i], plane_land, plane_sent, plane_landed)
        vec_plane.start()
        first_block, last_block = own_blocks(seq, columns, width, span)
        for k in range(4):

            @pl.when(first_block + k <= last_block)
            def _():
                pltpu.make_async_copy(
                    gq.at[pl.ds(0, depth), pl.ds(0, span)], nat_blocks.at[k], nat_landed.at[k]
                ).wait()

        vec_plane.arrive()
        vec_out[...] = plane_land[0] + plane_land[1] + plane_land[2] + plane_land[3]
        vec_plane.drain()
        for ahead in range(1, row):
            vec_to(ahead).wait_send()
        for kind in range(3):
            for late in range(2):
                there, target, slot = nat(kind, late)

                @pl.when(there & (target != seq))
                def _():
                    nat_copy(kind, late, target, slot).wait_send()

        attn_plane.drain()
        attn_plane.arrive()

    pl.run_scoped(
        attention_back,
        pltpu.VMEM((span, width), bf),
        pltpu.VMEM((length, width), bf),
        pltpu.VMEM((length, 3 * span), bf),
        pltpu.VMEM((width, 3 * span), bf),
        pltpu.VMEM((length, 128), f32),
        pltpu.VMEM((length, span), bf),
        pltpu.VMEM((length, 128), f32),
        pltpu.VMEM((8, length), f32),
        pltpu.VMEM((length, span), bf),
        pltpu.VMEM((length, 3 * span), f32),
        pltpu.VMEM((length, 3 * span), bf),
        pltpu.VMEM((width, span), bf),
        pltpu.VMEM((width, 3 * span), bf),
        pltpu.VMEM((plane, depth, 3 * span), bf),
        pltpu.VMEM((own_rows, width), bf),
    )
    for summing in (hidden_sum, out_sum):
        summing.drain()
    dr_line.drain()
    for terms in (fc_plane, proj_plane):
        terms.drain()
        terms.arrive()


def backward_phase(
    x_all, cot_all, vec, bias, w_attn, attn_all, w_fc, w_proj, h1_all, qkv, w_qkv, lse, attn_own, ids_col, ids_row, reach
):
    length, width = x_all.shape
    row, plane, chips, span = 8, 4, 4, attn_own.shape[1]
    own_rows, units, depth = length // row, w_fc.shape[1], width // plane
    bf, f32 = jnp.bfloat16, jnp.float32
    anywhere = pl.BlockSpec(memory_space=pl.ANY)
    in_vmem = pl.BlockSpec(memory_space=pltpu.VMEM)
    dma = pltpu.SemaphoreType.DMA

    def shaped(*shape, dtype=bf):
        return jax.ShapeDtypeStruct(shape, dtype)

    block = (own_rows, width)
    return pl.pallas_call(
        lambda *refs: backward_kernel(reach, *refs),
        out_shape=[
            shaped(*block, dtype=f32),
            shaped(*block, dtype=f32),
            shaped(plane, units, width),
            shaped(plane, units, width),
            shaped(plane, depth, span),
            shaped(4, depth, span),
            shaped(8, span, dtype=f32),
            shaped(plane, depth, 3 * span),
        ],
        in_specs=[anywhere] * 15,
        out_specs=[in_vmem] * 2 + [anywhere] * 4 + [in_vmem] + [anywhere],
        scratch_shapes=[
            pltpu.VMEM(attn_all.shape, bf),
            pltpu.VMEM((chips,) + block, bf),
            pltpu.VMEM((chips,) + block, bf),
            pltpu.VMEM((chips,) + block, bf),
            pltpu.VMEM((chips + 1,) + block, bf),
            pltpu.VMEM((chips,) + block, bf),
            pltpu.VMEM((chips,) + block, bf),
            pltpu.VMEM((chips,) + block, bf),
            pltpu.VMEM((chips + 1,) + block, bf),
            pltpu.VMEM((length, width), bf),
            pltpu.VMEM(block, f32),
            pltpu.VMEM(block, f32),
            pltpu.VMEM(block, f32),
            pltpu.VMEM((2 * own_rows, width), f32),
            pltpu.VMEM((plane, units, width), bf),
            pltpu.VMEM((plane, units, width), bf),
            pltpu.VMEM((8, 8 * span), f32),
            pltpu.VMEM((8, span), f32),
            pltpu.VMEM((8, span), f32),
            pltpu.VMEM((8, 8 * span), f32),
            pltpu.VMEM((row, 8, span), f32),
            pltpu.VMEM((row, 8, span), f32),
            pltpu.VMEM((plane, 8, span), f32),
            pltpu.VMEM((plane, 8, span), f32),
            dma((2, chips)),
            dma((2, chips)),
            dma((2, chips)),
            dma((2, chips + 1)),
            dma((row, 1, 3)),
            dma((row, 1)),
            dma((4, 4)),
            dma((4, 4)),
            dma((3, 2)),
            dma((4,)),
            dma((row,)),
            dma((row,)),
            dma((4,)),
            dma((4,)),
            dma((9,)),
        ],
        compiler_params=pltpu.CompilerParams(
            collective_id=1, has_side_effects=True, vmem_limit_bytes=62 * 1024 * 1024
        ),
    )(x_all, cot_all, vec, bias, w_attn, attn_all, w_fc, w_proj, h1_all, qkv, w_qkv, lse, attn_own, ids_col, ids_row)


def block_places(own, columns, width, span):
    groups = -(-width // span)
    first, last = own_blocks(own, columns, width, span)
    place = lax.iota(jnp.int32, 4 * span)
    block, lane = first + place // span, place % span
    at = (block % groups) * span + lane
    source = (block // groups) * width + at - own * columns
    there = (block <= last) & (at < width) & (source >= 0) & (source < columns)
    return jnp.where(there, source, -1)


def joined_blocks(blocks, own, columns, width):
    span = blocks.shape[2]
    source = block_places(own, columns, width, span)
    chosen = lax.broadcasted_iota(jnp.int32, (4 * span, columns), 1) == source[:, None]
    lanes = blocks.transpose(1, 0, 2).reshape(-1, 4 * span)
    lanes = jnp.where(source[None, :] >= 0, lanes, jnp.zeros_like(lanes))
    return jnp.dot(lanes, chosen.astype(jnp.bfloat16), preferred_element_type=jnp.float32)


def column_blocks(shard, own, width, span):
    columns = shard.shape[1]
    source = block_places(own, columns, width, span)
    chosen = lax.broadcasted_iota(jnp.int32, (columns, 4 * span), 0) == source[None, :]
    cut = jnp.dot(shard, chosen.astype(jnp.bfloat16), preferred_element_type=jnp.float32)
    return cut.astype(jnp.bfloat16).reshape(-1, 4, span).transpose(1, 0, 2)


def token_plan(
    tokens,
    segment_ids,
    cotangent,
    qkv_weight,
    attn_out_weight,
    fc_weight,
    proj_weight,
    vectors,
    fc_bias,
):
    own_rows, width = tokens.shape[1], tokens.shape[2]
    parts = lax.axis_size("seq")
    own = lax.axis_index("seq")
    length = own_rows * parts
    reach = length // 2
    span = 4 * HEAD_DIM
    share = vectors.shape[1]
    units = proj_weight.shape[0]
    extra = -units % 16
    group = group_of(own)

    lines = [vectors.astype(jnp.float32), fc_bias.astype(jnp.float32)[None]]
    lines = [jnp.pad(line, ((0, 0), (0, span - share))) for line in lines]
    lines.append(jnp.pad(segment_ids.astype(jnp.float32), ((0, 4), (0, span - own_rows))))
    small = jnp.concatenate(lines)
    blocks = column_blocks(qkv_weight, own, width, span)
    fc_own = jnp.pad(fc_weight.T, ((0, extra), (0, 0)))
    proj_own = jnp.pad(proj_weight, ((0, extra), (0, 0)))

    x_all, cot_all, small_all, vec, ids_col, ids_row, h1, qkv, w_qkv, lse, attn_own, attn_all, w_fc, w_proj, w_attn = (
        attention_phase(tokens[0], cotangent[0], small, blocks, attn_out_weight, fc_own, proj_own, reach)
    )
    own_small = lax.dynamic_index_in_dim(small_all, own, 1, keepdims=False)
    bias = jnp.pad(own_small[:, 2], ((0, 4), (0, 0)))
    result, input_grad, fc_terms, proj_terms, attn_terms, nat_blocks, vec_sums, _ = backward_phase(
        x_all, cot_all, vec, bias, w_attn, attn_all, w_fc, w_proj, h1, qkv, w_qkv, lse, attn_own, ids_col, ids_row, reach
    )

    def added(terms):
        return jnp.sum(terms.astype(jnp.float32), axis=0)

    own_qkv = joined_blocks(nat_blocks, own, qkv_weight.shape[1], width)
    own_attn = added(attn_terms)[:, : attn_out_weight.shape[1]]
    own_fc = added(fc_terms)[:units].T
    own_proj = added(proj_terms)[:units]
    own_vec = vec_sums[:2, :share]
    own_bias = vec_sums[2, :units]
    return (result[None], input_grad[None], own_qkv, own_attn, own_fc, own_proj, own_vec, own_bias)


def solution(mesh):
    in_specs = (
        P("fsdp", "seq", None),
        P("fsdp", "seq"),
        P("fsdp", "seq", None),
        P("fsdp", "seq"),
        P("fsdp", "seq"),
        P(None, ("fsdp", "seq")),
        P(("fsdp", "seq"), None),
        P("fsdp", "seq"),
        P(("fsdp", "seq")),
    )
    out_specs = (
        P("fsdp", "seq", None),
        P("fsdp", "seq", None),
        P("fsdp", "seq"),
        P("fsdp", "seq"),
        P(None, ("fsdp", "seq")),
        P(("fsdp", "seq"), None),
        P("fsdp", "seq"),
        P(("fsdp", "seq")),
    )

    def per_device(tokens, *rest):
        length = tokens.shape[1] * mesh.shape["seq"]
        fits = length * tokens.shape[2] <= resident_most
        square = mesh.shape["fsdp"] == 4 and mesh.shape["seq"] == 8
        plan = token_plan if fits and square else gathered_weights
        return plan(tokens, *rest)

    return jax.shard_map(
        per_device, mesh=mesh, in_specs=in_specs, out_specs=out_specs, check_vma=False
    )
```

```python
import functools
import math

import jax
import jax.numpy as jnp
from jax import lax
from jax.experimental import pallas as pl
from jax.experimental.pallas import tpu as pltpu
from jax.sharding import PartitionSpec as P

HEADS = 25
HEAD_DIM = 64


norm_eps = 1e-05
tanh_coeff = math.sqrt(2.0 / math.pi)
cubic_coeff = 0.044715
masked_score = -1e30


def layer_norm(values, gain, shift):
    centred = values - jnp.mean(values, axis=-1, keepdims=True)
    inverse = lax.rsqrt(jnp.mean(centred * centred, axis=-1, keepdims=True) + norm_eps)
    normed = centred * inverse
    return (normed, inverse, normed * gain + shift)


def norm_back(grad_out, normed, inverse, gain):
    scaled = grad_out * gain
    grad_in = inverse * (
        scaled
        - jnp.mean(scaled, axis=-1, keepdims=True)
        - normed * jnp.mean(scaled * normed, axis=-1, keepdims=True)
    )
    return (grad_in, jnp.sum(grad_out * normed, axis=0), jnp.sum(grad_out, axis=0))


def gelu_parts(preact):
    inner = tanh_coeff * (preact + cubic_coeff * preact * preact * preact)
    tangent = jnp.tanh(inner)
    gelu_value = 0.5 * preact * (1.0 + tangent)
    gelu_slope = 0.5 * (1.0 + tangent) + 0.5 * preact * (1.0 - tangent * tangent) * tanh_coeff * (
        1.0 + 3.0 * cubic_coeff * preact * preact
    )
    return (gelu_value, gelu_slope)


def block_rows():
    return 512


def gather_owned(matrix_qkv, matrix_attn, matrix_fc, matrix_proj, vector_part, bias_part):
    return (
        lax.all_gather(matrix_qkv, "fsdp", axis=0, tiled=True),
        lax.all_gather(matrix_attn, "fsdp", axis=0, tiled=True),
        lax.all_gather(matrix_fc, "fsdp", axis=1, tiled=True),
        lax.all_gather(matrix_proj, "fsdp", axis=0, tiled=True),
        lax.all_gather(vector_part, "fsdp", axis=0, tiled=True),
        lax.all_gather(bias_part, "fsdp", axis=0, tiled=True),
    )


def gather_attention(matrix_qkv, matrix_attn, vector_part, id_part):
    return (
        lax.all_gather(matrix_qkv, "seq", axis=1, tiled=True),
        lax.all_gather(matrix_attn, "seq", axis=1, tiled=True),
        lax.all_gather(vector_part, "seq", axis=1, tiled=True),
        lax.all_gather(id_part, "seq", axis=0, tiled=True),
    )


def gathered_weights(
    tokens,
    segment_ids,
    cotangent,
    qkv_weight,
    attn_out_weight,
    fc_weight,
    proj_weight,
    vectors,
    fc_bias,
):
    width = tokens.shape[2]
    local_rows = tokens.shape[1]
    heads = HEADS
    head_width = HEAD_DIM
    score_scale = head_width ** (-0.5)
    own_index = lax.axis_index("seq")
    inputs_bf = tokens[0]
    inputs = inputs_bf.astype(jnp.float32)
    doc_ids = segment_ids[0].astype(jnp.bfloat16)
    grad_out_bf = cotangent[0]
    owned = gather_owned(qkv_weight, attn_out_weight, fc_weight, proj_weight, vectors, fc_bias)
    w_qkv, w_attn, vector_bf, ids_all = gather_attention(owned[0], owned[1], owned[4], doc_ids)

    def gather_feedforward(matrix_fc, matrix_proj, bias_part):
        return (
            lax.all_gather(matrix_fc, "seq", axis=1, tiled=True),
            lax.all_gather(matrix_proj, "seq", axis=0, tiled=True),
            lax.all_gather(bias_part, "seq", axis=0, tiled=True),
        )

    w_fc, w_proj, bias_units = gather_feedforward(owned[2], owned[3], owned[5])
    vector_rows = vector_bf.astype(jnp.float32)
    fc_shift = bias_units.astype(jnp.float32)
    normed1, inverse1, shifted1 = layer_norm(inputs, vector_rows[0], vector_rows[1])
    hidden1 = shifted1.astype(jnp.bfloat16)
    projected = jnp.dot(hidden1, w_qkv, preferred_element_type=jnp.float32)
    queries = (projected[:, :width] + vector_rows[2]).astype(jnp.bfloat16)
    keys_own = projected[:, width : 2 * width].astype(jnp.bfloat16)
    values_own = (projected[:, 2 * width :] + vector_rows[3]).astype(jnp.bfloat16)
    query_heads = queries.reshape(local_rows, heads, head_width)
    positions = own_index * local_rows + lax.iota(jnp.int32, local_rows)

    def scores_for(key_block, ids_block, pos_block):
        scores = (
            jnp.einsum("qhd,khd->hqk", query_heads, key_block, preferred_element_type=jnp.float32)
            * score_scale
        )
        allowed = (
            (pos_block[None, :] <= positions[:, None])
            & (pos_block[None, :] >= 0)
            & (ids_block[None, :] == doc_ids[:, None])
        )
        return (scores, allowed)

    def stat_step(running, block_items):
        running_max, running_sum = running
        key_block, value_block, ids_block, pos_block = block_items
        scores, allowed = scores_for(key_block, ids_block, pos_block)
        masked = jnp.where(allowed[None], scores, masked_score)
        new_max = jnp.maximum(running_max, jnp.max(masked, axis=2))
        fading = jnp.exp(running_max - new_max)
        weights = jnp.where(allowed[None], jnp.exp(masked - new_max[:, :, None]), 0.0)
        running_sum = running_sum * fading + jnp.sum(weights, axis=2)
        return ((new_max, running_sum), None)

    initial = (
        jnp.full((heads, local_rows), masked_score, jnp.float32),
        jnp.zeros((heads, local_rows), jnp.float32),
    )
    keys_all, values_all = (
        lax.all_gather(keys_own, "seq", axis=0, tiled=True),
        lax.all_gather(values_own, "seq", axis=0, tiled=True),
    )
    key_count = keys_all.shape[0]
    step_rows = block_rows()
    blocks = key_count // step_rows
    key_items = (
        keys_all.reshape(blocks, step_rows, heads, head_width),
        values_all.reshape(blocks, step_rows, heads, head_width),
        ids_all.reshape(blocks, step_rows),
        lax.iota(jnp.int32, key_count).reshape(blocks, step_rows),
    )
    running, _ = lax.scan(stat_step, initial, key_items)
    final_max, final_sum = running
    log_total = final_max + jnp.log(final_sum)

    def weigh_step(total, block_items):
        key_block, value_block, ids_block, pos_block = block_items
        scores, allowed = scores_for(key_block, ids_block, pos_block)
        probs_bf = jnp.where(allowed[None], jnp.exp(scores - log_total[:, :, None]), 0.0).astype(
            jnp.bfloat16
        )
        return (
            total
            + jnp.einsum("hqk,khd->hqd", probs_bf, value_block, preferred_element_type=jnp.float32),
            None,
        )

    final_acc, _ = lax.scan(
        weigh_step, jnp.zeros((heads, local_rows, head_width), jnp.float32), key_items
    )
    attn_bf = final_acc.astype(jnp.bfloat16).transpose(1, 0, 2).reshape(local_rows, width)
    resid = inputs + jnp.dot(attn_bf, w_attn, preferred_element_type=jnp.float32) + vector_rows[4]
    normed2, inverse2, shifted2 = layer_norm(resid, vector_rows[5], vector_rows[6])
    hidden2 = shifted2.astype(jnp.bfloat16)
    preact = jnp.dot(hidden2, w_fc, preferred_element_type=jnp.float32) + fc_shift
    gelu_value, gelu_slope = gelu_parts(preact)
    act_bf = gelu_value.astype(jnp.bfloat16)
    mlp_out = jnp.dot(act_bf, w_proj, preferred_element_type=jnp.float32)
    result = resid + mlp_out + vector_rows[7]
    fenced = lax.optimization_barrier(
        (qkv_weight, attn_out_weight, fc_weight, proj_weight, vectors, fc_bias, doc_ids, result)
    )
    owned_again = gather_owned(fenced[0], fenced[1], fenced[2], fenced[3], fenced[4], fenced[5])
    back_qkv, back_attn, back_vec_bf, ids_again = gather_attention(
        owned_again[0], owned_again[1], owned_again[4], fenced[6]
    )
    back_fc, back_proj, bias_again = gather_feedforward(
        owned_again[2], owned_again[3], owned_again[5]
    )
    back_vec = back_vec_bf.astype(jnp.float32)
    grad_out = grad_out_bf.astype(jnp.float32)
    grad_proj_full = jnp.einsum(
        "tf,td->fd", act_bf, grad_out_bf, preferred_element_type=jnp.float32
    )
    grad_act = jnp.einsum("td,fd->tf", grad_out_bf, back_proj, preferred_element_type=jnp.float32)
    grad_pre = grad_act * gelu_slope
    grad_pre_bf = grad_pre.astype(jnp.bfloat16)
    grad_fc_full = jnp.einsum("td,tf->df", hidden2, grad_pre_bf, preferred_element_type=jnp.float32)
    grad_hidden2 = jnp.einsum("tf,df->td", grad_pre_bf, back_fc, preferred_element_type=jnp.float32)
    bias_full = jnp.sum(grad_pre, axis=0)
    part_fc, part_proj, part_bias = (
        lax.psum_scatter(
            grad_fc_full.astype(jnp.bfloat16), "seq", scatter_dimension=1, tiled=True
        ).astype(jnp.float32),
        lax.psum_scatter(
            grad_proj_full.astype(jnp.bfloat16), "seq", scatter_dimension=0, tiled=True
        ).astype(jnp.float32),
        lax.psum_scatter(
            bias_full.astype(jnp.bfloat16), "seq", scatter_dimension=0, tiled=True
        ).astype(jnp.float32),
    )
    grad_resid_norm, gain2_grad, shift2_grad = norm_back(
        grad_hidden2, normed2, inverse2, back_vec[5]
    )
    grad_resid = grad_out + grad_resid_norm
    grad_resid_bf = grad_resid.astype(jnp.bfloat16)
    grad_attn_out_full = jnp.einsum(
        "tc,td->cd", attn_bf, grad_resid_bf, preferred_element_type=jnp.float32
    )
    grad_attn_bf = jnp.einsum(
        "td,cd->tc", grad_resid_bf, back_attn, preferred_element_type=jnp.float32
    ).astype(jnp.bfloat16)
    grad_heads = grad_attn_bf.reshape(local_rows, heads, head_width)
    attn_heads = attn_bf.reshape(local_rows, heads, head_width)
    delta = jnp.sum(grad_heads.astype(jnp.float32) * attn_heads.astype(jnp.float32), axis=2).T

    def back_step(grad_query, block_items):
        key_block, value_block, ids_block, pos_block = block_items
        scores, allowed = scores_for(key_block, ids_block, pos_block)
        probs = jnp.where(allowed[None], jnp.exp(scores - log_total[:, :, None]), 0.0)
        probs_bf = probs.astype(jnp.bfloat16)
        value_grad = jnp.einsum(
            "hqk,qhd->khd", probs_bf, grad_heads, preferred_element_type=jnp.float32
        )
        prob_grad = jnp.einsum(
            "qhd,khd->hqk", grad_heads, value_block, preferred_element_type=jnp.float32
        )
        score_grad = (probs * (prob_grad - delta[:, :, None])).astype(jnp.bfloat16)
        grad_query = grad_query + score_scale * jnp.einsum(
            "hqk,khd->qhd", score_grad, key_block, preferred_element_type=jnp.float32
        )
        key_grad = score_scale * jnp.einsum(
            "hqk,qhd->khd", score_grad, query_heads, preferred_element_type=jnp.float32
        )
        return (grad_query, (key_grad, value_grad))

    query_zero = jnp.zeros((local_rows, heads, head_width), jnp.float32)
    grad_query, stacked_grads = lax.scan(back_step, query_zero, key_items)
    key_terms = stacked_grads[0].reshape(key_count, width)
    value_terms = stacked_grads[1].reshape(key_count, width)
    key_own_grad, value_own_grad = (
        lax.psum_scatter(
            key_terms.astype(jnp.bfloat16), "seq", scatter_dimension=0, tiled=True
        ).astype(jnp.float32),
        lax.psum_scatter(
            value_terms.astype(jnp.bfloat16), "seq", scatter_dimension=0, tiled=True
        ).astype(jnp.float32),
    )
    query_grad = grad_query.reshape(local_rows, width)
    grad_qkv_bf = jnp.concatenate([query_grad, key_own_grad, value_own_grad], axis=1).astype(
        jnp.bfloat16
    )
    grad_qkv_full = jnp.einsum(
        "td,te->de", hidden1, grad_qkv_bf, preferred_element_type=jnp.float32
    )
    grad_hidden1 = jnp.einsum(
        "te,de->td", grad_qkv_bf, back_qkv, preferred_element_type=jnp.float32
    )
    grad_input_norm, gain1_grad, shift1_grad = norm_back(
        grad_hidden1, normed1, inverse1, back_vec[0]
    )
    input_grad = grad_resid + grad_input_norm
    vector_grad = jnp.stack(
        [
            gain1_grad,
            shift1_grad,
            jnp.sum(query_grad, axis=0),
            jnp.sum(value_own_grad, axis=0),
            jnp.sum(grad_resid, axis=0),
            gain2_grad,
            shift2_grad,
            jnp.sum(grad_out, axis=0),
        ]
    )
    part_qkv, part_attn, part_vec = (
        lax.psum_scatter(
            grad_qkv_full.astype(jnp.bfloat16), "seq", scatter_dimension=1, tiled=True
        ).astype(jnp.float32),
        lax.psum_scatter(
            grad_attn_out_full.astype(jnp.bfloat16), "seq", scatter_dimension=1, tiled=True
        ).astype(jnp.float32),
        lax.psum_scatter(
            vector_grad.astype(jnp.bfloat16), "seq", scatter_dimension=1, tiled=True
        ).astype(jnp.float32),
    )
    own_qkv, own_attn, own_fc, own_proj, own_vec, own_bias = (
        lax.psum_scatter(
            part_qkv.astype(jnp.bfloat16), "fsdp", scatter_dimension=0, tiled=True
        ).astype(jnp.float32),
        lax.psum_scatter(
            part_attn.astype(jnp.bfloat16), "fsdp", scatter_dimension=0, tiled=True
        ).astype(jnp.float32),
        lax.psum_scatter(
            part_fc.astype(jnp.bfloat16), "fsdp", scatter_dimension=1, tiled=True
        ).astype(jnp.float32),
        lax.psum_scatter(
            part_proj.astype(jnp.bfloat16), "fsdp", scatter_dimension=0, tiled=True
        ).astype(jnp.float32),
        lax.psum_scatter(
            part_vec.astype(jnp.bfloat16), "fsdp", scatter_dimension=0, tiled=True
        ).astype(jnp.float32),
        lax.psum_scatter(
            part_bias.astype(jnp.bfloat16), "fsdp", scatter_dimension=0, tiled=True
        ).astype(jnp.float32),
    )
    return (result[None], input_grad[None], own_qkv, own_attn, own_fc, own_proj, own_vec, own_bias)


resident_most = 2 * 1024 * 1024


def contract_last(left, right):
    return lax.dot_general(left, right, (((1,), (1,)), ((), ())), preferred_element_type=jnp.float32)


def contract_first(left, right):
    return lax.dot_general(left, right, (((0,), (0,)), ((), ())), preferred_element_type=jnp.float32)


def head_lanes(head, shape):
    lane = lax.broadcasted_iota(jnp.int32, shape, 1)
    return (lane >= head * HEAD_DIM) & (lane < (head + 1) * HEAD_DIM)


def only_head(values, head):
    return jnp.where(head_lanes(head, values.shape), values, jnp.zeros_like(values))


def tile_pairs(length, tile, reach):
    for start in range(0, length, tile):
        first = max(0, (start - reach) // tile * tile)
        yield start, first, start + tile - first


norm_part = 32


def row_tiles(count, size, body):
    def step(i, carry):
        body(pl.multiple_of(i * size, size))
        return carry

    lax.fori_loop(0, count // size, step, 0)


MESH = pl.DeviceIdType.MESH


def remote(source, target, sent, landed, axis, index):
    return pltpu.make_async_remote_copy(
        src_ref=source,
        dst_ref=target,
        send_sem=sent,
        recv_sem=landed,
        device_id={axis: index},
        device_id_type=MESH,
    )


def greet(row, plane):
    barrier = pltpu.get_barrier_semaphore()
    for axis, size in (("seq", row), ("fsdp", plane)):
        own = lax.axis_index(axis)
        for ahead in range(1, size):
            pl.semaphore_signal(
                barrier,
                inc=1,
                device_id={axis: lax.rem(own + ahead, size)},
                device_id_type=MESH,
            )
    pl.semaphore_wait(barrier, row + plane - 2)


class RowGather:
    def __init__(self, own, view, sent, landed, row, chunks=1, has=None):
        self.own, self.view, self.sent, self.landed = own, view, sent, landed
        self.row, self.chips, self.chunks = row, row // 2, chunks
        self.has = has or (lambda i, c: None)
        self.me = lax.axis_index("seq")
        self.chip, self.core = self.me // 2, self.me % 2
        self.other = self.me + 1 - 2 * self.core

    def hop(self, i, c, way, source=None):
        place = self.view(i, c)
        target = (self.me + 2, self.me - 2, self.other)[way]
        return remote(
            place if source is None else source,
            place,
            self.sent.at[i, c, way],
            self.landed.at[i, c],
            "seq",
            target,
        )

    def when(self, i, c, condition, action):
        has = self.has(i, c)
        if has is not None:
            condition = has if condition is None else has & condition
        if condition is None:
            action()
        else:
            pl.when(condition)(action)

    def spread(self, i, c, forward, backward, source=None):
        self.when(i, c, forward, lambda: self.hop(i, c, 0, source).start())
        self.when(i, c, backward, lambda: self.hop(i, c, 1, source).start())
        self.when(i, c, None, lambda: self.hop(i, c, 2, source).start())

    def start(self, chunks=None):
        for c in chunks or range(self.chunks):
            self.spread(
                self.me, c, self.chip < self.chips - 1, self.chip > 0, self.own(c) if self.own else None
            )

    def pass_on(self, distance, chunks=None):
        chunks = chunks or range(self.chunks)

        def from_before():
            i = self.me - 2 * distance
            for c in chunks:
                self.when(i, c, None, lambda: self.hop(i, c, 2).wait_recv())
                self.when(i, c, self.chip < self.chips - 1, lambda: self.hop(i, c, 0).start())
                self.when(i, c, None, lambda: self.hop(i, c, 2).start())

        def from_after():
            i = self.me + 2 * distance
            for c in chunks:
                self.when(i, c, None, lambda: self.hop(i, c, 2).wait_recv())
                self.when(i, c, self.chip > 0, lambda: self.hop(i, c, 1).start())
                self.when(i, c, None, lambda: self.hop(i, c, 2).start())

        pl.when(self.chip >= distance)(from_before)
        pl.when(self.chip + distance < self.chips)(from_after)

    def wait_other(self, i):
        for c in range(self.chunks):
            self.when(i, c, None, lambda: self.hop(i, c, 2).wait_recv())

    def from_other_core(self):
        for k in range(self.chips):
            self.wait_other(2 * k + 1 - self.core)

    def drain(self):
        for k in range(self.chips):
            i = 2 * k + self.core
            for c in range(self.chunks):
                forward = (self.chip >= k) & (self.chip < self.chips - 1)
                backward = (self.chip <= k) & (self.chip > 0)
                self.when(i, c, forward, lambda: self.hop(i, c, 0).wait_send())
                self.when(i, c, backward, lambda: self.hop(i, c, 1).wait_send())
                self.when(i, c, None, lambda: self.hop(i, c, 2).wait_send())


class PlaneGather:
    def __init__(self, own, view, parts, sent, landed):
        self.own, self.view, self.parts, self.sent, self.landed = own, view, parts, sent, landed
        me = lax.axis_index("fsdp")
        self.me = me
        self.beside = me + 1 - 2 * (me % 2)
        self.above = lax.rem(me + 2, 4)
        self.corner = lax.rem(self.beside + 2, 4)

    def whole(self, i, slot, target, source=None):
        place = self.view(i, None)
        return remote(
            place if source is None else source,
            place,
            self.sent.at[slot],
            self.landed.at[slot],
            "fsdp",
            target,
        )

    def part(self, i, slot, target):
        place = self.view(i, self.parts[slot - 2])
        return remote(place, place, self.sent.at[slot], self.landed.at[slot], "fsdp", target)

    def start(self):
        self.whole(self.me, 0, self.beside, self.own).start()
        self.whole(self.me, 1, self.above, self.own).start()

    def pass_on(self):
        self.whole(self.beside, 0, self.beside).wait_recv()
        self.part(self.beside, 2, self.above).start()
        self.whole(self.above, 1, self.above).wait_recv()
        self.part(self.above, 3, self.beside).start()

    def finish(self):
        self.part(self.corner, 2, self.above).wait_recv()
        self.part(self.corner, 3, self.beside).wait_recv()

    def drain(self):
        self.whole(self.me, 0, self.beside).wait_send()
        self.whole(self.me, 1, self.above).wait_send()
        self.part(self.beside, 2, self.above).wait_send()
        self.part(self.above, 3, self.beside).wait_send()


def group_of(device):
    third = (device + 5) // 8 - (device + 4) // 8
    fifth = (device + 3) // 8 - (device + 2) // 8
    return device - (device + 4) // 8 - (device + 2) // 8 + 3 * third + 3 * fifth


def device_of(group):
    return group + (group + 5) // 8 + (group + 4) // 8 - 5 * ((group + 2) // 8)


def own_blocks(device, columns, width, span):
    groups = -(-width // span)

    def block_at(column):
        return groups * (column // width) + (column % width) // span

    return block_at(device * columns), block_at(device * columns + columns - 1)


def norm_rows(values, gain, shift):
    centred = values - jnp.mean(values, axis=-1, keepdims=True)
    inverse = lax.rsqrt(jnp.mean(centred * centred, axis=-1, keepdims=True) + norm_eps)
    return (centred * inverse) * gain + shift


def attend(head, pair, start, first, count, tile, qkv_ref, ids_col, ids_row, out_ref, lse_ref):
    span = out_ref.shape[1]
    rows, keys = pl.ds(start, tile), pl.ds(first, count)

    def lanes(kind):
        return pl.ds(kind * span + pair * 128, 128)

    query = only_head(qkv_ref[rows, lanes(0)], head)
    scores = contract_last(query, qkv_ref[keys, lanes(1)]) * (HEAD_DIM**-0.5)
    q_pos = start + lax.broadcasted_iota(jnp.int32, (tile, count), 0)
    k_pos = first + lax.broadcasted_iota(jnp.int32, (tile, count), 1)
    allowed = (k_pos <= q_pos) & (ids_col[rows, :1] == ids_row[:1, keys])
    masked = jnp.where(allowed, scores, masked_score)
    top = jnp.max(masked, axis=1, keepdims=True)
    weights = jnp.exp(masked - top)
    total = jnp.sum(weights, axis=1, keepdims=True)
    probs = (weights * (1.0 / total)).astype(jnp.bfloat16)
    value = only_head(qkv_ref[keys, lanes(2)], head)
    mixed = jnp.dot(probs, value, preferred_element_type=jnp.float32)
    out_ref[rows, lanes(0)] += mixed.astype(jnp.bfloat16)
    lane = lax.broadcasted_iota(jnp.int32, (tile, lse_ref.shape[1]), 1)
    lse_ref[rows, :] = jnp.where(lane == 2 * pair + head, top + jnp.log(total), lse_ref[rows, :])


def pick(index, values):
    chosen = values[-1]
    for k in range(len(values) - 1):
        chosen = jnp.where(index == k, values[k], chosen)
    return chosen


def chip_order(chip, step):
    rows = ((3, 3, 0, 0), (2, 0, 3, 1), (1, 2, 1, 2), (0, 1, 2, 3))
    return pick(step, [pick(chip, row) for row in rows])


class RowSum:
    def __init__(self, own, away, pair, chain, pair_sent, pair_landed, chain_sent, chain_landed):
        self.own, self.away, self.pair, self.chain = own, away, pair, chain
        self.pair_sent, self.pair_landed = pair_sent, pair_landed
        self.chain_sent, self.chain_landed = chain_sent, chain_landed
        self.me = lax.axis_index("seq")
        self.chips = 4
        self.chip, self.core = self.me // 2, self.me % 2
        self.other = self.me + 1 - 2 * self.core

    def exchange(self, t):
        return remote(
            self.away.at[t],
            self.pair.at[t],
            self.pair_sent.at[t],
            self.pair_landed.at[t],
            "seq",
            self.other,
        )

    def onward(self, t, slot, target):
        return remote(
            self.own.at[t],
            self.chain.at[slot],
            self.chain_sent.at[t],
            self.chain_landed.at[slot],
            "seq",
            target,
        )

    def put(self, t, terms):
        rows = self.own.shape[1]
        self.away[t] = terms[pl.ds(pl.multiple_of((1 - self.core) * rows, rows), rows), :].astype(
            jnp.bfloat16
        )
        self.exchange(t).start()
        self.own[t] = terms[pl.ds(pl.multiple_of(self.core * rows, rows), rows), :].astype(jnp.bfloat16)

    def add(self, t, arrived, slot):
        total = self.own[t].astype(jnp.float32) + arrived[slot].astype(jnp.float32)
        self.own[t] = total.astype(jnp.bfloat16)

    def step(self, t):
        self.exchange(t).wait_recv()
        self.add(t, self.pair, t)

        def forward():
            @pl.when(self.chip > 0)
            def _():
                self.onward(t, t, self.me + 2).wait_recv()
                self.add(t, self.chain, t)

            self.onward(t, t, self.me + 2).start()

        def backward():
            @pl.when(self.chip < self.chips - 1)
            def _():
                self.onward(t, t, self.me - 2).wait_recv()
                self.add(t, self.chain, t)

            slot = jnp.where(t == self.chip - 1, self.chips, t)
            self.onward(t, slot, self.me - 2).start()

        pl.when(t > self.chip)(forward)
        pl.when(t < self.chip)(backward)

    def final(self, total):
        t = self.chip
        self.exchange(t).wait_recv()
        total[...] = self.own[t].astype(jnp.float32) + self.pair[t].astype(jnp.float32)

        @pl.when(self.chip > 0)
        def _():
            self.onward(t, t, self.other).wait_recv()
            total[...] += self.chain[t].astype(jnp.float32)

        @pl.when(self.chip < self.chips - 1)
        def _():
            self.onward(t, self.chips, self.other).wait_recv()
            total[...] += self.chain[self.chips].astype(jnp.float32)

    def drain(self):
        for t in range(self.chips):
            self.exchange(t).wait_send()

            @pl.when(self.chip != t)
            def _():
                self.onward(t, t, self.other).wait_send()


class PlaneTerms:
    def __init__(self, view, terms, sent, landed):
        self.view, self.terms, self.sent, self.landed = view, terms, sent, landed
        self.me = lax.axis_index("fsdp")

    def to(self, ahead):
        i = lax.rem(self.me + ahead, 4)
        return remote(
            self.view(i), self.terms.at[self.me], self.sent.at[ahead], self.landed.at[self.me], "fsdp", i
        )

    def keep(self):
        return pltpu.make_async_copy(
            self.view(self.me), self.terms.at[self.me], self.landed.at[self.me]
        )

    def start(self):
        self.keep().start()
        for ahead in (3, 1, 2):
            self.to(ahead).start()

    def arrive(self):
        self.keep().wait()
        for ahead in range(1, 4):
            i = lax.rem(self.me + ahead, 4)
            remote(
                self.view(i), self.terms.at[i], self.sent.at[ahead], self.landed.at[i], "fsdp", i
            ).wait_recv()

    def drain(self):
        for ahead in range(1, 4):
            self.to(ahead).wait_send()


def backward_attend(
    head, start, first, count, tile, qkv_ref, attn_ref, grad_ref, lse_ref, ids_col, ids_row, out_ref
):
    span = attn_ref.shape[1]
    scale = HEAD_DIM**-0.5
    rows, keys = pl.ds(start, tile), pl.ds(first, count)
    query = only_head(qkv_ref[rows, :span], head)
    key = qkv_ref[keys, span : 2 * span]
    grad = only_head(grad_ref[rows, :], head)
    delta = jnp.sum(
        grad.astype(jnp.float32) * attn_ref[rows, :].astype(jnp.float32), axis=1, keepdims=True
    )
    scores = contract_last(query, key) * scale
    q_pos = start + lax.broadcasted_iota(jnp.int32, (tile, count), 0)
    k_pos = first + lax.broadcasted_iota(jnp.int32, (tile, count), 1)
    allowed = (k_pos <= q_pos) & (ids_col[rows, :1] == ids_row[:1, keys])
    lane = lax.broadcasted_iota(jnp.int32, (tile, lse_ref.shape[1]), 1)
    lse = jnp.sum(jnp.where(lane == head, lse_ref[rows, :], 0.0), axis=1, keepdims=True)
    probs = jnp.where(allowed, jnp.exp(scores - lse), 0.0)
    prob_grad = contract_last(grad, qkv_ref[keys, 2 * span :])
    score_grad = (probs * (prob_grad - delta)).astype(jnp.bfloat16)
    out_ref[rows, :span] += scale * jnp.dot(
        score_grad, only_head(key, head), preferred_element_type=jnp.float32
    )
    out_ref[keys, span : 2 * span] += scale * contract_first(score_grad, query)
    out_ref[keys, 2 * span :] += contract_first(probs.astype(jnp.bfloat16), grad)


def block_kernel(
    reach,
    x_ref,
    cot_ref,
    small_ref,
    blocks_ref,
    wo_ref,
    fc_ref,
    proj_ref,
    result_ref,
    input_grad_ref,
    fc_terms,
    proj_terms,
    attn_terms,
    nat_blocks,
    vec_out,
    qkv_terms,
    cot_all,
    h1_all,
    wo_all,
    wo_z,
    x_v,
    small_v,
    vec_v,
    ids_col,
    ids_row,
    pieces,
    w_v,
    qkv_v,
    attn_o,
    lse_v,
    attn_v,
    fc_v,
    proj_v,
    own1,
    away1,
    pair1,
    chain1,
    own2,
    away2,
    pair2,
    chain2,
    dr_all,
    resid_own,
    dresid_own,
    total,
    wide,
    bias_sum,
    gv,
    vec_send,
    vec_land,
    plane_send,
    plane_land,
    small_sent,
    small_landed,
    first_sent,
    first_landed,
    piece_sent,
    piece_landed,
    w_sent,
    w_landed,
    x_sent,
    x_landed,
    cot_sent,
    cot_landed,
    attn_sent,
    attn_landed,
    fc_sent,
    fc_landed,
    proj_sent,
    proj_landed,
    wo_sent,
    wo_landed,
    wo_plane_sent,
    wo_plane_landed,
    wo_pair_sent,
    wo_pair_landed,
    local_sem,
    pair_sent,
    pair_landed,
    chain_sent,
    chain_landed,
    dr_sent,
    dr_landed,
    terms_sent,
    terms_landed,
    nat_sent,
    nat_landed,
    vec_sent,
    vec_landed,
    plane_sent,
    plane_landed,
    load_sem,
):
    row, plane, chips = 8, 4, 4
    seq, fsdp = lax.axis_index("seq"), lax.axis_index("fsdp")
    chip, core = seq // 2, seq % 2
    ends = (chip == 0) | (chip == chips - 1)
    own_rows, width = x_ref.shape
    length = own_rows * row
    pair_rows = 2 * own_rows
    units = fc_ref.shape[0]
    span = attn_o.shape[1]
    share = width // row
    depth = width // plane
    groups = -(-width // span)
    group = group_of(seq)
    columns = qkv_columns(width, row)
    bf, f32 = jnp.bfloat16, jnp.float32
    tiles = [(0, 512), (512, 1024), (1024, width)]

    def load(source, target, slot):
        copy = pltpu.make_async_copy(source, target, load_sem.at[slot])
        copy.start()
        return copy

    def pair_at(t):
        return pl.ds(pl.multiple_of(t * pair_rows, pair_rows), pair_rows)

    own_at = pl.ds(pl.multiple_of(seq * own_rows, own_rows), own_rows)
    half_at = pl.ds(pl.multiple_of(core * own_rows, own_rows), own_rows)
    hidden_sum = RowSum(
        own1, away1, pair1, chain1, pair_sent.at[0], pair_landed.at[0], chain_sent.at[0], chain_landed.at[0]
    )
    out_sum = RowSum(
        own2, away2, pair2, chain2, pair_sent.at[1], pair_landed.at[1], chain_sent.at[1], chain_landed.at[1]
    )
    dr_line = RowGather(
        None,
        lambda i, c: dr_all.at[pl.ds(pl.multiple_of(i * own_rows, own_rows), own_rows)],
        dr_sent,
        dr_landed,
        row,
    )
    fc_back = PlaneTerms(lambda i: fc_v.at[i], fc_terms, terms_sent.at[0], terms_landed.at[0])
    proj_back = PlaneTerms(lambda i: proj_v.at[i], proj_terms, terms_sent.at[1], terms_landed.at[1])

    used = []

    def keep(source, target):
        copy = pltpu.make_async_copy(source, target, local_sem.at[len(used)])
        copy.start()
        used.append(copy)

    vec = vec_v
    vec[...] = jnp.zeros_like(vec)
    w_v[...] = jnp.zeros_like(w_v)
    bias_sum[...] = jnp.zeros_like(bias_sum)
    gv[...] = jnp.zeros_like(gv)
    attn_o[...] = jnp.zeros_like(attn_o)
    lse_v[...] = jnp.zeros_like(lse_v)
    greet(row, plane)
    own_small = pltpu.make_async_copy(small_ref, small_v.at[fsdp, seq], small_landed.at[seq])
    own_small.start()

    def small_to(target, slot):
        return remote(
            small_ref, small_v.at[fsdp, seq], small_sent.at[slot], small_landed.at[seq], "seq", target
        )

    for ahead in range(1, row):
        small_to(lax.rem(seq + ahead, row), ahead - 1).start()

    first_block, last_block = own_blocks(seq, qkv_columns(width, row), width, span)

    def piece(k):
        block = first_block + k
        kind, at = block // groups, block % groups
        begins = kind * width + at * span
        later = (seq * qkv_columns(width, row) + width * 3 - begins - 1) // (width * 3)
        target = device_of(at)
        place = pieces.at[kind, later]
        return block <= last_block, target, place, piece_landed.at[kind, later]

    for k in range(4):
        there, target, place, landed = piece(k)

        @pl.when(there & (target == seq))
        def _():
            pltpu.make_async_copy(blocks_ref.at[k], place, landed).start()

        @pl.when(there & (target != seq))
        def _():
            remote(blocks_ref.at[k], place, piece_sent.at[k], landed, "seq", target).start()

    def block_of(target):
        return lambda i, c: target.at[pl.ds(pl.multiple_of(i * own_rows, own_rows), own_rows)]

    x_line = RowGather(lambda c: x_ref, block_of(x_v), x_sent, x_landed, row)
    own_x = pltpu.make_async_copy(x_ref, block_of(x_v)(seq, 0), local_sem.at[0])
    own_x.start()
    used.append(None)
    x_line.start()

    wo_line = RowGather(lambda c: wo_ref, lambda i, c: wo_z.at[i], wo_sent, wo_landed, row)
    keep(wo_ref, wo_z.at[seq])
    def slab(target):
        def view(i, part):
            start, count = (0, target.shape[1]) if part is None else part
            return target.at[i, pl.ds(start, count)]

        return view

    units = fc_ref.shape[0]
    cut = units // 32 * 16
    parts = ((0, cut), (cut, units - cut))
    fc_plane = PlaneGather(fc_ref, slab(fc_v), parts, fc_sent, fc_landed)
    proj_plane = PlaneGather(proj_ref, slab(proj_v), parts, proj_sent, proj_landed)
    fc_plane.start()
    keep(cot_ref, block_of(cot_all)(seq, 0))
    keep(fc_ref, fc_v.at[fsdp])
    keep(proj_ref, proj_v.at[fsdp])

    for other in range(row):
        pltpu.make_async_copy(small_ref, small_v.at[fsdp, other], small_landed.at[other]).wait()

    def small_plane(ahead):
        return remote(
            small_v.at[fsdp],
            small_v.at[fsdp],
            first_sent.at[ahead - 1],
            first_landed.at[ahead - 1],
            "fsdp",
            lax.rem(fsdp + ahead, plane),
        )

    for ahead in range(1, plane):
        small_plane(ahead).start()
    for other in range(row):
        lanes = pl.ds(other * own_rows, own_rows)
        ids = jnp.broadcast_to(small_v[fsdp, other, 3:4, :own_rows], (own_rows, own_rows))
        ids_row[:, lanes] = ids[:8]
        ids_col[lanes, :] = ids.T
    own_w = pl.ds(pl.multiple_of(fsdp * depth, 16), depth)

    @pl.when(group < groups)
    def _():
        for kind in range(3):
            begins = kind * width + group * span
            ends = begins + jnp.minimum(span, width - group * span) - 1
            cols = qkv_columns(width, row)
            straddles = ends // cols != begins // cols
            pltpu.make_async_copy(
                blocks_ref.at[0], pieces.at[kind, 0], piece_landed.at[kind, 0]
            ).wait()
            w_v[own_w, kind * span : (kind + 1) * span] = pieces[kind, 0]

            @pl.when(straddles)
            def _():
                pltpu.make_async_copy(
                    blocks_ref.at[0], pieces.at[kind, 1], piece_landed.at[kind, 1]
                ).wait()
                w_v[own_w, kind * span : (kind + 1) * span] = pieces[kind, 0] + pieces[kind, 1]

    def w_view(i, part):
        start, count = (0, depth) if part is None else part
        return w_v.at[pl.ds(pl.multiple_of(i * depth + start, 16), count)]

    half = depth // 32 * 16
    w_plane = PlaneGather(None, w_view, ((0, half), (half, depth - half)), w_sent, w_landed)
    w_plane.start()
    x_line.pass_on(1)
    for ahead in range(1, plane):
        remote(
            small_v.at[fsdp],
            small_v.at[lax.rem(fsdp + plane - ahead, plane)],
            first_sent.at[ahead - 1],
            first_landed.at[ahead - 1],
            "fsdp",
            lax.rem(fsdp + ahead, plane),
        ).wait_recv()
    for i in range(plane):
        for other in range(row):
            vec[2 * i : 2 * i + 2, share * other : share * (other + 1)] = small_v[i, other, 0:2, :share]

    wo_cut = 6 * 128
    wo_lanes = ((0, wo_cut), (wo_cut, width - wo_cut))

    def wo_view(lanes):
        def view(i, part):
            start, count = (0, depth) if part is None else part
            rows = pl.ds(pl.multiple_of(i * depth + start, 16), count)
            return wo_all.at[rows, pl.ds(*lanes)]

        return view

    wo_planes = [
        PlaneGather(
            None, wo_view(lanes), ((0, half), (half, depth - half)), wo_plane_sent, wo_plane_landed
        )
        for lanes in wo_lanes
    ]

    def wo_pair(core, ahead):
        i = lax.rem(fsdp + ahead, plane)
        place = wo_view(wo_lanes[core])(i, None)
        return remote(place, place, wo_pair_sent.at[i], wo_pair_landed.at[i], "seq", x_line.other)

    def wo_pairs(action, core):
        for ahead in range(1, plane):
            action(wo_pair(core, ahead))

    def on_own_core(action):
        for core in range(2):
            pl.when(x_line.core == core)(functools.partial(action, core))

    cot_line = RowGather(lambda c: cot_ref, block_of(cot_all), cot_sent, cot_landed, row)
    def chunk(i, c):
        return attn_v.at[:, pl.ds(pl.multiple_of(group_of(i) * span + c * 128, 128), 128)]

    attn_line = RowGather(
        lambda c: attn_o.at[:, pl.ds(c * 128, 128)],
        chunk,
        attn_sent,
        attn_landed,
        row,
        chunks=2,
        has=lambda i, c: group_of(i) < groups - c,
    )
    def own_chunk(c):
        lanes = pl.ds(pl.multiple_of(group * span + c * 128, 128), 128)
        return pltpu.make_async_copy(
            attn_o.at[:, pl.ds(c * 128, 128)], attn_v.at[:, lanes], piece_landed.at[c, 0]
        )

    def send_chunk(c):
        attn_line.start([c])
        pl.when(group < groups - c)(lambda: own_chunk(c).start())

    def attention_forward(h1_v, wo_own, wo_zv):
        def norm_block(i):
            def part(j):
                rows = pl.ds(pl.multiple_of(i * own_rows + j, norm_part), norm_part)
                hidden = norm_rows(x_v[rows, :].astype(jnp.float32), vec[0:1, :width], vec[1:2, :width])
                h1_v[rows, :] = hidden.astype(jnp.bfloat16)

            row_tiles(own_rows, norm_part, part)

        def norm_arrived(distance):
            if 0 < distance < row // 2:
                pl.when(x_line.chip >= distance)(lambda: norm_block(seq - 2 * distance))
                pl.when(x_line.chip + distance < row // 2)(lambda: norm_block(seq + 2 * distance))

            def other(i):
                x_line.wait_other(i)
                norm_block(i)

            if distance == 1:
                other(x_line.other)
            elif distance > 1:
                nearer = distance - 1
                pl.when(x_line.chip >= nearer)(lambda: other(x_line.other - 2 * nearer))
                pl.when(x_line.chip + nearer < row // 2)(lambda: other(x_line.other + 2 * nearer))

        own_x.wait()
        norm_block(seq)
        norm_arrived(1)
        w_plane.pass_on()
        fc_plane.pass_on()
        proj_plane.start()
        x_line.pass_on(2)
        norm_arrived(2)
        x_line.pass_on(3)
        wo_line.start()
        norm_arrived(3)
        norm_arrived(4)
        w_plane.finish()

        lanes = pl.ds(pl.multiple_of(group * span, span), span)
        query_shift, value_shift = vec[2:3, lanes], vec[3:4, lanes]

        def project(i):
            rows = pl.ds(i, 2 * own_rows)
            mixed = jnp.dot(h1_v[rows, :], w_v[...], preferred_element_type=jnp.float32)
            qkv_v[rows, :span] = (mixed[:, :span] + query_shift).astype(jnp.bfloat16)
            qkv_v[rows, span : 2 * span] = mixed[:, span : 2 * span].astype(jnp.bfloat16)
            qkv_v[rows, 2 * span :] = (mixed[:, 2 * span :] + value_shift).astype(jnp.bfloat16)

        wo_line.pass_on(1)
        row_tiles(length, 2 * own_rows, project)
        wo_line.pass_on(2)
        proj_plane.pass_on()
        h1_kept = pltpu.make_async_copy(h1_v, h1_all, load_sem.at[1])
        h1_kept.start()

        tile = 256

        def heads(pair):
            def head(h, carry):
                for start, first, count in tile_pairs(length, tile, reach):
                    attend(h, pair, start, first, count, tile, qkv_v, ids_col, ids_row, attn_o, lse_v)
                return carry

            lax.fori_loop(0, 2, head, 0)

        heads(0)

        send_chunk(0)
        wo_line.pass_on(3)
        wo_line.from_other_core()
        used[1].wait()
        used[1] = None
        wo_load = pltpu.make_async_copy(wo_z, wo_zv, load_sem.at[0])
        wo_load.start()
        wo_load.wait()
        for i in range(row):
            wo_own[:, share * i : share * (i + 1)] = wo_zv[i, :, :share]
        for core, lanes in enumerate(wo_lanes):
            wo_planes[core].own = wo_own.at[:, pl.ds(*lanes)]

        on_own_core(lambda core: wo_planes[core].start())
        wo_kept = pltpu.make_async_copy(wo_own, wo_view((0, width))(fsdp, None), load_sem.at[2])
        wo_kept.start()
        heads(1)
        send_chunk(1)
        cot_line.start()
        h1_kept.wait()
        wo_kept.wait()
        attn_line.pass_on(1)
        attn_line.pass_on(2)
        on_own_core(lambda core: wo_planes[core].pass_on())
        attn_line.pass_on(3)
        cot_line.pass_on(1)
        on_own_core(lambda core: wo_planes[core].drain())

    pl.run_scoped(
        attention_forward,
        pltpu.VMEM((length, width), bf),
        pltpu.VMEM((depth, width), bf),
        pltpu.VMEM(wo_z.shape, bf),
    )
    on_own_core(lambda core: wo_planes[core].finish())
    on_own_core(lambda core: wo_pairs(lambda copy: copy.start(), core))
    attn_line.from_other_core()
    for c in range(2):
        pl.when(group < groups - c)(lambda: own_chunk(c).wait())
    on_own_core(lambda core: wo_pairs(lambda copy: copy.wait_recv(), 1 - core))
    fc_plane.finish()
    for i in range(2, 5):
        used[i].wait()
        used[i] = None

    def feed_forward(w_attn, cot_v, h2_v, act_v, dpre_v, pre_v, dact_v):
        w_load = load(wo_all.at[pl.ds(0, width)], w_attn, 1)
        w_load.wait()

        def back_through(rows, values, weights):
            for low, high in tiles:
                terms = jnp.dot(
                    values[0, rows, :], weights[0, :, low:high], preferred_element_type=f32
                )
                for f in range(1, plane):
                    terms += jnp.dot(
                        values[f, rows, :], weights[f, :, low:high], preferred_element_type=f32
                    )
                wide[:, low:high] = terms

        def chunk(p, carry):
            t = chip_order(chip, p)
            rows = pair_at(t)
            for low, high in tiles:
                wide[:, low:high] = jnp.dot(
                    attn_v[rows, :width], w_attn[:, low:high], preferred_element_type=f32
                )

            def second_norm(i):
                part = pl.ds(i, norm_part)
                place = pl.ds(pl.multiple_of(t * pair_rows + i, norm_part), norm_part)
                resid = wide[part, :] + x_v[place, :].astype(f32) + vec_v[4:5, :width]
                wide[part, :] = resid
                hidden = norm_rows(resid, vec_v[5:6, :width], vec_v[6:7, :width])
                h2_v[place, :] = hidden.astype(bf)

            row_tiles(pair_rows, norm_part, second_norm)

            @pl.when(t == chip)
            def _():
                resid_own[...] = wide[half_at, :]

            def unit_block(f, carry):
                pre_v[...] = contract_last(h2_v[rows, :], fc_v[f])
                shift = small_v[f, seq, 2:3, :units]

                def gelu(i):
                    part = pl.ds(i, 32)
                    gelu_value, gelu_slope = gelu_parts(pre_v[part, :] + shift)
                    place = pl.ds(pl.multiple_of(t * pair_rows + i, 32), 32)
                    act_v[f, place, :] = gelu_value.astype(bf)
                    dpre_v[f, place, :] = gelu_slope.astype(bf)

                row_tiles(pair_rows, 32, gelu)
                return carry

            lax.fori_loop(0, plane, unit_block, 0)
            for step in range(2):
                pl.when(p == step)(functools.partial(cot_line.pass_on, step + 2))
            return carry

        lax.fori_loop(0, chips, chunk, 0)
        cot_line.from_other_core()
        cot_load = load(cot_all, cot_v, 3)
        proj_plane.finish()
        cot_load.wait()

        def back_chunk(p, carry):
            t = chip_order(chip, p)
            rows = pair_at(t)

            def unit_block(f, carry):
                dact_v[...] = contract_last(cot_v[rows, :], proj_v[f])

                def through_gelu(i):
                    place = pl.ds(pl.multiple_of(t * pair_rows + i, 32), 32)
                    dpre = dact_v[pl.ds(i, 32), :] * dpre_v[f, place, :].astype(f32)
                    dpre_v[f, place, :] = dpre.astype(bf)
                    bias_sum[pl.ds(f, 1), :units] += jnp.sum(dpre, axis=0, keepdims=True)

                row_tiles(pair_rows, 32, through_gelu)
                return carry

            lax.fori_loop(0, plane, unit_block, 0)
            back_through(rows, dpre_v, fc_v)
            hidden_sum.put(t, wide)

            @pl.when(ends & (p < chips - 1))
            def _():
                hidden_sum.step(t)

            return carry

        def weight_terms(values, others, stage):
            def unit_block(f, carry):
                for low, high in tiles:
                    stage[f, :, low:high] = contract_first(values[f], others[:, low:high]).astype(bf)
                return carry

            lax.fori_loop(0, plane, unit_block, 0)

        lax.fori_loop(0, chips, back_chunk, 0)
        fc_plane.drain()
        weight_terms(dpre_v, h2_v, fc_v)
        fc_back.start()

        @pl.when(jnp.logical_not(ends))
        def _():
            hidden_sum.step(chip_order(chip, 0))
            hidden_sum.step(chip_order(chip, 1))

        @pl.when(jnp.logical_not(ends))
        def _():
            hidden_sum.step(chip_order(chip, 2))

        hidden_sum.final(total)

        def second_norm_back(i):
            part = pl.ds(i, norm_part)
            resid = resid_own[part, :]
            centred = resid - jnp.mean(resid, axis=-1, keepdims=True)
            inverse = lax.rsqrt(jnp.mean(centred * centred, axis=-1, keepdims=True) + norm_eps)
            normed = centred * inverse
            grad_hidden = total[part, :]
            scaled = grad_hidden * vec_v[5:6, :width]
            back = inverse * (
                scaled
                - jnp.mean(scaled, axis=-1, keepdims=True)
                - normed * jnp.mean(scaled * normed, axis=-1, keepdims=True)
            )
            place = pl.ds(pl.multiple_of(seq * own_rows + i, norm_part), norm_part)
            cot = cot_v[place, :].astype(f32)
            grad_resid = cot + back
            dresid_own[part, :] = grad_resid
            dr_all[place, :] = grad_resid.astype(bf)
            for at, values in ((4, grad_resid), (5, grad_hidden * normed), (6, grad_hidden), (7, cot)):
                gv[at : at + 1, :width] += jnp.sum(values, axis=0, keepdims=True)

        row_tiles(own_rows, norm_part, second_norm_back)
        dr_line.start()

        def out_chunk(p, carry):
            t = chip_order(chip, p)
            back_through(pair_at(t), act_v, proj_v)
            out_sum.put(t, wide)

            @pl.when(ends & (p < chips - 1))
            def _():
                out_sum.step(t)

            return carry

        lax.fori_loop(0, chips, out_chunk, 0)
        proj_plane.drain()
        dr_line.pass_on(1)
        weight_terms(act_v, cot_v, proj_v)
        proj_back.start()
        dr_line.pass_on(2)

    pl.run_scoped(
        feed_forward,
        pltpu.VMEM((width, width), bf),
        pltpu.VMEM((length, width), bf),
        pltpu.VMEM((length, width), bf),
        pltpu.VMEM((plane, length, units), bf),
        pltpu.VMEM((plane, length, units), bf),
        pltpu.VMEM((pair_rows, units), f32),
        pltpu.VMEM((pair_rows, units), f32),
    )

    def attention_back(w_rows, h1_v, da_v, dqkv, dqkv16, ga, gq, gqt):
        loads = [
            load(wo_all.at[pl.ds(pl.multiple_of(group * span, span), span)], w_rows, 0),
            load(h1_all, h1_v, 1),
        ]
        dqkv[...] = jnp.zeros_like(dqkv)
        dr_line.pass_on(3)
        dr_line.from_other_core()
        loads[0].wait()

        inside = lax.broadcasted_iota(jnp.int32, w_rows.shape, 0) < width - group * span
        w_rows[...] = jnp.where(inside, w_rows[...], jnp.zeros_like(w_rows))

        def into_heads(i):
            rows = pl.ds(i, pair_rows)
            da_v[rows, :] = contract_last(dr_all[rows, :], w_rows[...]).astype(bf)

        row_tiles(length, pair_rows, into_heads)

        @pl.when(jnp.logical_not(ends))
        def _():
            out_sum.step(chip_order(chip, 0))

        def heads(h, carry):
            for start, first, count in tile_pairs(length, 256, reach):
                backward_attend(
                    h, start, first, count, 256, qkv_v, attn_o, da_v, lse_v, ids_col, ids_row, dqkv
                )
            return carry

        lax.fori_loop(0, 2, heads, 0)

        @pl.when(jnp.logical_not(ends))
        def _():
            out_sum.step(chip_order(chip, 1))

        lax.fori_loop(2, 4, heads, 0)

        @pl.when(jnp.logical_not(ends))
        def _():
            out_sum.step(chip_order(chip, 2))

        lanes = pl.ds(pl.multiple_of(group * span, span), span)
        gv[2:3, lanes] = jnp.sum(dqkv[:, :span], axis=0, keepdims=True)
        gv[3:4, lanes] = jnp.sum(dqkv[:, 2 * span :], axis=0, keepdims=True)
        dqkv16[...] = dqkv[...].astype(bf)

        loads[1].wait()

        def kind_terms(kind):
            lanes = pl.ds(kind * span, span)
            return PlaneTerms(
                lambda i: gq.at[pl.ds(pl.multiple_of(i * depth, 16), depth), lanes],
                qkv_terms.at[kind],
                terms_sent.at[2 + kind],
                terms_landed.at[2 + kind],
            )

        kinds = [kind_terms(kind) for kind in range(3)]
        for kind in range(3):
            lanes = slice(kind * span, (kind + 1) * span)
            for low in range(0, width, span):
                high = min(low + span, width)
                gq[low:high, lanes] = contract_first(h1_v[:, low:high], dqkv16[:, lanes]).astype(bf)
            kinds[kind].start()

        hidden_sum.drain()

        def chunk(p, carry):
            t = chip_order(chip, p)
            for low, high in tiles:
                wide[:, low:high] = contract_last(dqkv16[pair_at(t), :], w_v[low:high, :])
            hidden_sum.put(t, wide)

            @pl.when(ends & (p < chips - 1))
            def _():
                hidden_sum.step(t)

            return carry

        lax.fori_loop(0, chips, chunk, 0)

        place = lax.broadcasted_iota(jnp.int32, (width, span), 0)
        lane = lax.broadcasted_iota(jnp.int32, (width, span), 1)
        chosen = ((place == seq * share + lane) & (lane < share)).astype(f32).astype(bf)

        def own_columns(i):
            rows = pl.ds(i, pair_rows)
            da_v[rows, :] = jnp.dot(dr_all[rows, :], chosen, preferred_element_type=f32).astype(bf)

        row_tiles(length, pair_rows, own_columns)
        for low in range(0, width, span):
            high = min(low + span, width)
            ga[low:high, :] = contract_first(attn_v[:, low:high], da_v[...]).astype(bf)
        attn_plane = PlaneTerms(
            lambda i: ga.at[pl.ds(pl.multiple_of(i * depth, 16), depth)],
            attn_terms,
            terms_sent.at[5],
            terms_landed.at[5],
        )
        attn_plane.start()

        @pl.when(jnp.logical_not(ends))
        def _():
            for p in range(chips - 1):
                hidden_sum.step(chip_order(chip, p))

        out_sum.final(total)
        for low, high in tiles:
            resid_own[:, low:high] += total[:, low:high] + vec_v[7:8, low:high]
        result_copy = load(resid_own, result_ref, 2)

        hidden_sum.final(total)

        def first_norm_back(i):
            part = pl.ds(i, norm_part)
            values = x_v[pl.ds(pl.multiple_of(seq * own_rows + i, norm_part), norm_part), :].astype(f32)
            centred = values - jnp.mean(values, axis=-1, keepdims=True)
            inverse = lax.rsqrt(jnp.mean(centred * centred, axis=-1, keepdims=True) + norm_eps)
            normed = centred * inverse
            grad_hidden = total[part, :]
            scaled = grad_hidden * vec_v[0:1, :width]
            back = inverse * (
                scaled
                - jnp.mean(scaled, axis=-1, keepdims=True)
                - normed * jnp.mean(scaled * normed, axis=-1, keepdims=True)
            )
            dresid_own[part, :] += back
            for at, summed in ((0, grad_hidden * normed), (1, grad_hidden)):
                gv[at : at + 1, :width] += jnp.sum(summed, axis=0, keepdims=True)

        row_tiles(own_rows, norm_part, first_norm_back)

        input_copy = load(dresid_own, input_grad_ref, 3)

        vec_send[...] = jnp.zeros_like(vec_send)
        plane_send[...] = jnp.zeros_like(plane_send)
        for i in range(row):
            vec_send[i, :, :share] = gv[:, share * i : share * (i + 1)]

        def vec_to(ahead):
            i = lax.rem(seq + ahead, row)
            return remote(
                vec_send.at[i], vec_land.at[seq], vec_sent.at[ahead], vec_landed.at[seq], "seq", i
            )

        keep = pltpu.make_async_copy(vec_send.at[seq], vec_land.at[seq], vec_landed.at[seq])
        keep.start()
        for ahead in range(1, row):
            vec_to(ahead).start()

        def nat(kind, late):
            begins = kind * width + group * span
            last = begins + jnp.minimum(span, width - group * span) - 1
            before, after = begins // columns, last // columns
            target = after if late else before
            slot = kind * groups + group - own_blocks(target, columns, width, span)[0]
            there = (group < groups) & (before != after) if late else group < groups
            return there, target, slot

        def nat_copy(kind, late, target, slot):
            return remote(
                gq.at[pl.ds(kind * depth, depth), pl.ds(0, span)],
                nat_blocks.at[slot],
                nat_sent.at[kind, late],
                nat_landed.at[slot],
                "seq",
                target,
            )

        for kind in range(3):
            kinds[kind].arrive()
            load(qkv_terms.at[kind], gqt.at[kind], 0).wait()
            kinds[kind].drain()
            part = gqt[kind, 0].astype(f32)
            for f in range(1, plane):
                part += gqt[kind, f].astype(f32)
            gq[kind * depth : (kind + 1) * depth, :span] = part.astype(bf)
            for late in range(2):
                there, target, slot = nat(kind, late)

                @pl.when(there & (target != seq))
                def _():
                    nat_copy(kind, late, target, slot).start()

                @pl.when(there & (target == seq))
                def _():
                    pltpu.make_async_copy(
                        gq.at[pl.ds(kind * depth, depth), pl.ds(0, span)],
                        nat_blocks.at[slot],
                        nat_landed.at[slot],
                    ).start()

        for i in range(row):
            pltpu.make_async_copy(vec_send.at[i], vec_land.at[i], vec_landed.at[i]).wait()
        summed = vec_land[0]
        for i in range(1, row):
            summed += vec_land[i]
        for i in range(plane):
            plane_send[i, 0:2, :] = summed[2 * i : 2 * i + 2, :]
            plane_send[i, 2:3, :] = bias_sum[i : i + 1, :]
        vec_plane = PlaneTerms(lambda i: plane_send.at[i], plane_land, plane_sent, plane_landed)
        vec_plane.start()
        first_block, last_block = own_blocks(seq, columns, width, span)
        for k in range(4):

            @pl.when(first_block + k <= last_block)
            def _():
                pltpu.make_async_copy(
                    gq.at[pl.ds(0, depth), pl.ds(0, span)], nat_blocks.at[k], nat_landed.at[k]
                ).wait()

        vec_plane.arrive()
        vec_out[...] = plane_land[0] + plane_land[1] + plane_land[2] + plane_land[3]
        vec_plane.drain()
        for ahead in range(1, row):
            vec_to(ahead).wait_send()
        for kind in range(3):
            for late in range(2):
                there, target, slot = nat(kind, late)

                @pl.when(there & (target != seq))
                def _():
                    nat_copy(kind, late, target, slot).wait_send()

        attn_plane.drain()
        attn_plane.arrive()
        result_copy.wait()
        input_copy.wait()

    pl.run_scoped(
        attention_back,
        pltpu.VMEM((span, width), bf),
        pltpu.VMEM((length, width), bf),
        pltpu.VMEM((length, span), bf),
        pltpu.VMEM((length, 3 * span), f32),
        pltpu.VMEM((length, 3 * span), bf),
        pltpu.VMEM((width, span), bf),
        pltpu.VMEM((width, 3 * span), bf),
        pltpu.VMEM((3, plane, depth, span), bf),
    )
    for ahead in range(1, row):
        small_to(lax.rem(seq + ahead, row), ahead - 1).wait_send()
    for ahead in range(1, plane):
        small_plane(ahead).wait_send()
    for k in range(4):
        there, target, place, landed = piece(k)

        @pl.when(there & (target != seq))
        def _():
            remote(blocks_ref.at[k], place, piece_sent.at[k], landed, "seq", target).wait_send()

    for line in (x_line, wo_line, cot_line, attn_line, w_plane):
        line.drain()
    on_own_core(lambda core: wo_pairs(lambda copy: copy.wait_send(), core))
    for copy in used:
        if copy is not None:
            copy.wait()
    for summing in (hidden_sum, out_sum):
        summing.drain()
    dr_line.drain()
    for terms in (fc_back, proj_back):
        terms.drain()
        terms.arrive()


def qkv_columns(width, row):
    return 3 * width // row


def block_phase(x_own, cot_own, small, blocks, wo_own, fc_own, proj_own, reach):
    own_rows, width = x_own.shape
    row, plane, chips, span = 8, 4, 4, 4 * HEAD_DIM
    length, units, depth = own_rows * row, fc_own.shape[0], width // plane
    bf, f32 = jnp.bfloat16, jnp.float32
    anywhere = pl.BlockSpec(memory_space=pl.ANY)
    in_vmem = pl.BlockSpec(memory_space=pltpu.VMEM)
    dma = pltpu.SemaphoreType.DMA
    block = (own_rows, width)

    def shaped(*shape, dtype=bf):
        return jax.ShapeDtypeStruct(shape, dtype)

    return pl.pallas_call(
        lambda *refs: block_kernel(reach, *refs),
        out_shape=[
            shaped(*block, dtype=f32),
            shaped(*block, dtype=f32),
            shaped(plane, units, width),
            shaped(plane, units, width),
            shaped(plane, depth, span),
            shaped(4, depth, span),
            shaped(8, span, dtype=f32),
            shaped(3, plane, depth, span),
            shaped(length, width),
            shaped(length, width),
            shaped(8 * span, width),
            shaped(row, depth, span),
        ],
        in_specs=[anywhere] * 7,
        out_specs=[anywhere] * 6 + [in_vmem] + [anywhere] * 5,
        scratch_shapes=[
            pltpu.VMEM((length, width), bf),
            pltpu.VMEM((plane, row, 8, span), f32),
            pltpu.VMEM((8, 8 * span), f32),
            pltpu.VMEM((length, own_rows), f32),
            pltpu.VMEM((8, length), f32),
            pltpu.VMEM((3, 2, depth, span), bf),
            pltpu.VMEM((width, 3 * span), bf),
            pltpu.VMEM((length, 3 * span), bf),
            pltpu.VMEM((length, span), bf),
            pltpu.VMEM((length, 128), f32),
            pltpu.VMEM((length, 7 * span), bf),
            pltpu.VMEM((plane, units, width), bf),
            pltpu.VMEM((plane, units, width), bf),
            pltpu.VMEM((chips,) + block, bf),
            pltpu.VMEM((chips,) + block, bf),
            pltpu.VMEM((chips,) + block, bf),
            pltpu.VMEM((chips + 1,) + block, bf),
            pltpu.VMEM((chips,) + block, bf),
            pltpu.VMEM((chips,) + block, bf),
            pltpu.VMEM((chips,) + block, bf),
            pltpu.VMEM((chips + 1,) + block, bf),
            pltpu.VMEM((length, width), bf),
            pltpu.VMEM(block, f32),
            pltpu.VMEM(block, f32),
            pltpu.VMEM(block, f32),
            pltpu.VMEM((2 * own_rows, width), f32),
            pltpu.VMEM((8, span), f32),
            pltpu.VMEM((8, 8 * span), f32),
            pltpu.VMEM((row, 8, span), f32),
            pltpu.VMEM((row, 8, span), f32),
            pltpu.VMEM((plane, 8, span), f32),
            pltpu.VMEM((plane, 8, span), f32),
            dma((row - 1,)),
            dma((row,)),
            dma((plane - 1,)),
            dma((plane - 1,)),
            dma((4,)),
            dma((3, 2)),
            dma((4,)),
            dma((4,)),
            dma((row, 1, 3)),
            dma((row, 1)),
            dma((row, 1, 3)),
            dma((row, 1)),
            dma((row, 2, 3)),
            dma((row, 2)),
            dma((4,)),
            dma((4,)),
            dma((4,)),
            dma((4,)),
            dma((row, 1, 3)),
            dma((row, 1)),
            dma((4,)),
            dma((4,)),
            dma((4,)),
            dma((4,)),
            dma((8,)),
            dma((2, chips)),
            dma((2, chips)),
            dma((2, chips)),
            dma((2, chips + 1)),
            dma((row, 1, 3)),
            dma((row, 1)),
            dma((6, 4)),
            dma((6, 4)),
            dma((3, 2)),
            dma((4,)),
            dma((row,)),
            dma((row,)),
            dma((4,)),
            dma((4,)),
            dma((4,)),
        ],
        compiler_params=pltpu.CompilerParams(
            collective_id=0, has_side_effects=True, vmem_limit_bytes=63 * 1024 * 1024
        ),
    )(x_own, cot_own, small, blocks, wo_own, fc_own, proj_own)


def block_places(own, columns, width, span):
    groups = -(-width // span)
    first, last = own_blocks(own, columns, width, span)
    place = lax.iota(jnp.int32, 4 * span)
    block, lane = first + place // span, place % span
    at = (block % groups) * span + lane
    source = (block // groups) * width + at - own * columns
    there = (block <= last) & (at < width) & (source >= 0) & (source < columns)
    return jnp.where(there, source, -1)


def joined_blocks(blocks, own, columns, width):
    span = blocks.shape[2]
    source = block_places(own, columns, width, span)
    chosen = lax.broadcasted_iota(jnp.int32, (4 * span, columns), 1) == source[:, None]
    lanes = blocks.transpose(1, 0, 2).reshape(-1, 4 * span)
    lanes = jnp.where(source[None, :] >= 0, lanes, jnp.zeros_like(lanes))
    return jnp.dot(lanes, chosen.astype(jnp.bfloat16), preferred_element_type=jnp.float32)


def column_blocks(shard, own, width, span):
    columns = shard.shape[1]
    source = block_places(own, columns, width, span)
    chosen = lax.broadcasted_iota(jnp.int32, (columns, 4 * span), 0) == source[None, :]
    cut = jnp.dot(shard, chosen.astype(jnp.bfloat16), preferred_element_type=jnp.float32)
    return cut.astype(jnp.bfloat16).reshape(-1, 4, span).transpose(1, 0, 2)


def token_plan(
    tokens,
    segment_ids,
    cotangent,
    qkv_weight,
    attn_out_weight,
    fc_weight,
    proj_weight,
    vectors,
    fc_bias,
):
    own_rows, width = tokens.shape[1], tokens.shape[2]
    parts = lax.axis_size("seq")
    own = lax.axis_index("seq")
    length = own_rows * parts
    reach = length // 2
    span = 4 * HEAD_DIM
    share = vectors.shape[1]
    units = proj_weight.shape[0]
    extra = -units % 16
    group = group_of(own)

    lines = [vectors.astype(jnp.float32), fc_bias.astype(jnp.float32)[None]]
    lines = [jnp.pad(line, ((0, 0), (0, span - share))) for line in lines]
    lines.append(jnp.pad(segment_ids.astype(jnp.float32), ((0, 4), (0, span - own_rows))))
    small = jnp.concatenate(lines)
    blocks = column_blocks(qkv_weight, own, width, span)
    fc_own = jnp.pad(fc_weight.T, ((0, extra), (0, 0)))
    proj_own = jnp.pad(proj_weight, ((0, extra), (0, 0)))

    wo_own = jnp.pad(attn_out_weight, ((0, 0), (0, span - attn_out_weight.shape[1])))
    result, input_grad, fc_terms, proj_terms, attn_terms, nat_blocks, vec_sums, *_ = block_phase(
        tokens[0], cotangent[0], small, blocks, wo_own, fc_own, proj_own, reach
    )

    def added(terms):
        return jnp.sum(terms.astype(jnp.float32), axis=0)

    own_qkv = joined_blocks(nat_blocks, own, qkv_weight.shape[1], width)
    own_attn = added(attn_terms)[:, : attn_out_weight.shape[1]]
    own_fc = added(fc_terms)[:units].T
    own_proj = added(proj_terms)[:units]
    own_vec = vec_sums[:2, :share]
    own_bias = vec_sums[2, :units]
    return (result[None], input_grad[None], own_qkv, own_attn, own_fc, own_proj, own_vec, own_bias)


def solution(mesh):
    in_specs = (
        P("fsdp", "seq", None),
        P("fsdp", "seq"),
        P("fsdp", "seq", None),
        P("fsdp", "seq"),
        P("fsdp", "seq"),
        P(None, ("fsdp", "seq")),
        P(("fsdp", "seq"), None),
        P("fsdp", "seq"),
        P(("fsdp", "seq")),
    )
    out_specs = (
        P("fsdp", "seq", None),
        P("fsdp", "seq", None),
        P("fsdp", "seq"),
        P("fsdp", "seq"),
        P(None, ("fsdp", "seq")),
        P(("fsdp", "seq"), None),
        P("fsdp", "seq"),
        P(("fsdp", "seq")),
    )

    def per_device(tokens, *rest):
        length = tokens.shape[1] * mesh.shape["seq"]
        fits = length * tokens.shape[2] <= resident_most
        square = mesh.shape["fsdp"] == 4 and mesh.shape["seq"] == 8
        plan = token_plan if fits and square else gathered_weights
        return plan(tokens, *rest)

    return jax.shard_map(
        per_device, mesh=mesh, in_specs=in_specs, out_specs=out_specs, check_vma=False
    )
```

```python
import functools
import math

import jax
import jax.numpy as jnp
from jax import lax
from jax.experimental import pallas as pl
from jax.experimental.pallas import tpu as pltpu
from jax.sharding import PartitionSpec as P

HEADS = 25
HEAD_DIM = 64


norm_eps = 1e-05
tanh_coeff = math.sqrt(2.0 / math.pi)
cubic_coeff = 0.044715
masked_score = -1e30


def layer_norm(values, gain, shift):
    centred = values - jnp.mean(values, axis=-1, keepdims=True)
    inverse = lax.rsqrt(jnp.mean(centred * centred, axis=-1, keepdims=True) + norm_eps)
    normed = centred * inverse
    return (normed, inverse, normed * gain + shift)


def norm_back(grad_out, normed, inverse, gain):
    scaled = grad_out * gain
    grad_in = inverse * (
        scaled
        - jnp.mean(scaled, axis=-1, keepdims=True)
        - normed * jnp.mean(scaled * normed, axis=-1, keepdims=True)
    )
    return (grad_in, jnp.sum(grad_out * normed, axis=0), jnp.sum(grad_out, axis=0))


def gelu_parts(preact):
    inner = tanh_coeff * (preact + cubic_coeff * preact * preact * preact)
    tangent = jnp.tanh(inner)
    gelu_value = 0.5 * preact * (1.0 + tangent)
    gelu_slope = 0.5 * (1.0 + tangent) + 0.5 * preact * (1.0 - tangent * tangent) * tanh_coeff * (
        1.0 + 3.0 * cubic_coeff * preact * preact
    )
    return (gelu_value, gelu_slope)


def block_rows():
    return 512


def gather_owned(matrix_qkv, matrix_attn, matrix_fc, matrix_proj, vector_part, bias_part):
    return (
        lax.all_gather(matrix_qkv, "fsdp", axis=0, tiled=True),
        lax.all_gather(matrix_attn, "fsdp", axis=0, tiled=True),
        lax.all_gather(matrix_fc, "fsdp", axis=1, tiled=True),
        lax.all_gather(matrix_proj, "fsdp", axis=0, tiled=True),
        lax.all_gather(vector_part, "fsdp", axis=0, tiled=True),
        lax.all_gather(bias_part, "fsdp", axis=0, tiled=True),
    )


def gather_attention(matrix_qkv, matrix_attn, vector_part, id_part):
    return (
        lax.all_gather(matrix_qkv, "seq", axis=1, tiled=True),
        lax.all_gather(matrix_attn, "seq", axis=1, tiled=True),
        lax.all_gather(vector_part, "seq", axis=1, tiled=True),
        lax.all_gather(id_part, "seq", axis=0, tiled=True),
    )


def gathered_weights(
    tokens,
    segment_ids,
    cotangent,
    qkv_weight,
    attn_out_weight,
    fc_weight,
    proj_weight,
    vectors,
    fc_bias,
):
    width = tokens.shape[2]
    local_rows = tokens.shape[1]
    heads = HEADS
    head_width = HEAD_DIM
    score_scale = head_width ** (-0.5)
    own_index = lax.axis_index("seq")
    inputs_bf = tokens[0]
    inputs = inputs_bf.astype(jnp.float32)
    doc_ids = segment_ids[0].astype(jnp.bfloat16)
    grad_out_bf = cotangent[0]
    owned = gather_owned(qkv_weight, attn_out_weight, fc_weight, proj_weight, vectors, fc_bias)
    w_qkv, w_attn, vector_bf, ids_all = gather_attention(owned[0], owned[1], owned[4], doc_ids)

    def gather_feedforward(matrix_fc, matrix_proj, bias_part):
        return (
            lax.all_gather(matrix_fc, "seq", axis=1, tiled=True),
            lax.all_gather(matrix_proj, "seq", axis=0, tiled=True),
            lax.all_gather(bias_part, "seq", axis=0, tiled=True),
        )

    w_fc, w_proj, bias_units = gather_feedforward(owned[2], owned[3], owned[5])
    vector_rows = vector_bf.astype(jnp.float32)
    fc_shift = bias_units.astype(jnp.float32)
    normed1, inverse1, shifted1 = layer_norm(inputs, vector_rows[0], vector_rows[1])
    hidden1 = shifted1.astype(jnp.bfloat16)
    projected = jnp.dot(hidden1, w_qkv, preferred_element_type=jnp.float32)
    queries = (projected[:, :width] + vector_rows[2]).astype(jnp.bfloat16)
    keys_own = projected[:, width : 2 * width].astype(jnp.bfloat16)
    values_own = (projected[:, 2 * width :] + vector_rows[3]).astype(jnp.bfloat16)
    query_heads = queries.reshape(local_rows, heads, head_width)
    positions = own_index * local_rows + lax.iota(jnp.int32, local_rows)

    def scores_for(key_block, ids_block, pos_block):
        scores = (
            jnp.einsum("qhd,khd->hqk", query_heads, key_block, preferred_element_type=jnp.float32)
            * score_scale
        )
        allowed = (
            (pos_block[None, :] <= positions[:, None])
            & (pos_block[None, :] >= 0)
            & (ids_block[None, :] == doc_ids[:, None])
        )
        return (scores, allowed)

    def stat_step(running, block_items):
        running_max, running_sum = running
        key_block, value_block, ids_block, pos_block = block_items
        scores, allowed = scores_for(key_block, ids_block, pos_block)
        masked = jnp.where(allowed[None], scores, masked_score)
        new_max = jnp.maximum(running_max, jnp.max(masked, axis=2))
        fading = jnp.exp(running_max - new_max)
        weights = jnp.where(allowed[None], jnp.exp(masked - new_max[:, :, None]), 0.0)
        running_sum = running_sum * fading + jnp.sum(weights, axis=2)
        return ((new_max, running_sum), None)

    initial = (
        jnp.full((heads, local_rows), masked_score, jnp.float32),
        jnp.zeros((heads, local_rows), jnp.float32),
    )
    keys_all, values_all = (
        lax.all_gather(keys_own, "seq", axis=0, tiled=True),
        lax.all_gather(values_own, "seq", axis=0, tiled=True),
    )
    key_count = keys_all.shape[0]
    step_rows = block_rows()
    blocks = key_count // step_rows
    key_items = (
        keys_all.reshape(blocks, step_rows, heads, head_width),
        values_all.reshape(blocks, step_rows, heads, head_width),
        ids_all.reshape(blocks, step_rows),
        lax.iota(jnp.int32, key_count).reshape(blocks, step_rows),
    )
    running, _ = lax.scan(stat_step, initial, key_items)
    final_max, final_sum = running
    log_total = final_max + jnp.log(final_sum)

    def weigh_step(total, block_items):
        key_block, value_block, ids_block, pos_block = block_items
        scores, allowed = scores_for(key_block, ids_block, pos_block)
        probs_bf = jnp.where(allowed[None], jnp.exp(scores - log_total[:, :, None]), 0.0).astype(
            jnp.bfloat16
        )
        return (
            total
            + jnp.einsum("hqk,khd->hqd", probs_bf, value_block, preferred_element_type=jnp.float32),
            None,
        )

    final_acc, _ = lax.scan(
        weigh_step, jnp.zeros((heads, local_rows, head_width), jnp.float32), key_items
    )
    attn_bf = final_acc.astype(jnp.bfloat16).transpose(1, 0, 2).reshape(local_rows, width)
    resid = inputs + jnp.dot(attn_bf, w_attn, preferred_element_type=jnp.float32) + vector_rows[4]
    normed2, inverse2, shifted2 = layer_norm(resid, vector_rows[5], vector_rows[6])
    hidden2 = shifted2.astype(jnp.bfloat16)
    preact = jnp.dot(hidden2, w_fc, preferred_element_type=jnp.float32) + fc_shift
    gelu_value, gelu_slope = gelu_parts(preact)
    act_bf = gelu_value.astype(jnp.bfloat16)
    mlp_out = jnp.dot(act_bf, w_proj, preferred_element_type=jnp.float32)
    result = resid + mlp_out + vector_rows[7]
    fenced = lax.optimization_barrier(
        (qkv_weight, attn_out_weight, fc_weight, proj_weight, vectors, fc_bias, doc_ids, result)
    )
    owned_again = gather_owned(fenced[0], fenced[1], fenced[2], fenced[3], fenced[4], fenced[5])
    back_qkv, back_attn, back_vec_bf, ids_again = gather_attention(
        owned_again[0], owned_again[1], owned_again[4], fenced[6]
    )
    back_fc, back_proj, bias_again = gather_feedforward(
        owned_again[2], owned_again[3], owned_again[5]
    )
    back_vec = back_vec_bf.astype(jnp.float32)
    grad_out = grad_out_bf.astype(jnp.float32)
    grad_proj_full = jnp.einsum(
        "tf,td->fd", act_bf, grad_out_bf, preferred_element_type=jnp.float32
    )
    grad_act = jnp.einsum("td,fd->tf", grad_out_bf, back_proj, preferred_element_type=jnp.float32)
    grad_pre = grad_act * gelu_slope
    grad_pre_bf = grad_pre.astype(jnp.bfloat16)
    grad_fc_full = jnp.einsum("td,tf->df", hidden2, grad_pre_bf, preferred_element_type=jnp.float32)
    grad_hidden2 = jnp.einsum("tf,df->td", grad_pre_bf, back_fc, preferred_element_type=jnp.float32)
    bias_full = jnp.sum(grad_pre, axis=0)
    part_fc, part_proj, part_bias = (
        lax.psum_scatter(
            grad_fc_full.astype(jnp.bfloat16), "seq", scatter_dimension=1, tiled=True
        ).astype(jnp.float32),
        lax.psum_scatter(
            grad_proj_full.astype(jnp.bfloat16), "seq", scatter_dimension=0, tiled=True
        ).astype(jnp.float32),
        lax.psum_scatter(
            bias_full.astype(jnp.bfloat16), "seq", scatter_dimension=0, tiled=True
        ).astype(jnp.float32),
    )
    grad_resid_norm, gain2_grad, shift2_grad = norm_back(
        grad_hidden2, normed2, inverse2, back_vec[5]
    )
    grad_resid = grad_out + grad_resid_norm
    grad_resid_bf = grad_resid.astype(jnp.bfloat16)
    grad_attn_out_full = jnp.einsum(
        "tc,td->cd", attn_bf, grad_resid_bf, preferred_element_type=jnp.float32
    )
    grad_attn_bf = jnp.einsum(
        "td,cd->tc", grad_resid_bf, back_attn, preferred_element_type=jnp.float32
    ).astype(jnp.bfloat16)
    grad_heads = grad_attn_bf.reshape(local_rows, heads, head_width)
    attn_heads = attn_bf.reshape(local_rows, heads, head_width)
    delta = jnp.sum(grad_heads.astype(jnp.float32) * attn_heads.astype(jnp.float32), axis=2).T

    def back_step(grad_query, block_items):
        key_block, value_block, ids_block, pos_block = block_items
        scores, allowed = scores_for(key_block, ids_block, pos_block)
        probs = jnp.where(allowed[None], jnp.exp(scores - log_total[:, :, None]), 0.0)
        probs_bf = probs.astype(jnp.bfloat16)
        value_grad = jnp.einsum(
            "hqk,qhd->khd", probs_bf, grad_heads, preferred_element_type=jnp.float32
        )
        prob_grad = jnp.einsum(
            "qhd,khd->hqk", grad_heads, value_block, preferred_element_type=jnp.float32
        )
        score_grad = (probs * (prob_grad - delta[:, :, None])).astype(jnp.bfloat16)
        grad_query = grad_query + score_scale * jnp.einsum(
            "hqk,khd->qhd", score_grad, key_block, preferred_element_type=jnp.float32
        )
        key_grad = score_scale * jnp.einsum(
            "hqk,qhd->khd", score_grad, query_heads, preferred_element_type=jnp.float32
        )
        return (grad_query, (key_grad, value_grad))

    query_zero = jnp.zeros((local_rows, heads, head_width), jnp.float32)
    grad_query, stacked_grads = lax.scan(back_step, query_zero, key_items)
    key_terms = stacked_grads[0].reshape(key_count, width)
    value_terms = stacked_grads[1].reshape(key_count, width)
    key_own_grad, value_own_grad = (
        lax.psum_scatter(
            key_terms.astype(jnp.bfloat16), "seq", scatter_dimension=0, tiled=True
        ).astype(jnp.float32),
        lax.psum_scatter(
            value_terms.astype(jnp.bfloat16), "seq", scatter_dimension=0, tiled=True
        ).astype(jnp.float32),
    )
    query_grad = grad_query.reshape(local_rows, width)
    grad_qkv_bf = jnp.concatenate([query_grad, key_own_grad, value_own_grad], axis=1).astype(
        jnp.bfloat16
    )
    grad_qkv_full = jnp.einsum(
        "td,te->de", hidden1, grad_qkv_bf, preferred_element_type=jnp.float32
    )
    grad_hidden1 = jnp.einsum(
        "te,de->td", grad_qkv_bf, back_qkv, preferred_element_type=jnp.float32
    )
    grad_input_norm, gain1_grad, shift1_grad = norm_back(
        grad_hidden1, normed1, inverse1, back_vec[0]
    )
    input_grad = grad_resid + grad_input_norm
    vector_grad = jnp.stack(
        [
            gain1_grad,
            shift1_grad,
            jnp.sum(query_grad, axis=0),
            jnp.sum(value_own_grad, axis=0),
            jnp.sum(grad_resid, axis=0),
            gain2_grad,
            shift2_grad,
            jnp.sum(grad_out, axis=0),
        ]
    )
    part_qkv, part_attn, part_vec = (
        lax.psum_scatter(
            grad_qkv_full.astype(jnp.bfloat16), "seq", scatter_dimension=1, tiled=True
        ).astype(jnp.float32),
        lax.psum_scatter(
            grad_attn_out_full.astype(jnp.bfloat16), "seq", scatter_dimension=1, tiled=True
        ).astype(jnp.float32),
        lax.psum_scatter(
            vector_grad.astype(jnp.bfloat16), "seq", scatter_dimension=1, tiled=True
        ).astype(jnp.float32),
    )
    own_qkv, own_attn, own_fc, own_proj, own_vec, own_bias = (
        lax.psum_scatter(
            part_qkv.astype(jnp.bfloat16), "fsdp", scatter_dimension=0, tiled=True
        ).astype(jnp.float32),
        lax.psum_scatter(
            part_attn.astype(jnp.bfloat16), "fsdp", scatter_dimension=0, tiled=True
        ).astype(jnp.float32),
        lax.psum_scatter(
            part_fc.astype(jnp.bfloat16), "fsdp", scatter_dimension=1, tiled=True
        ).astype(jnp.float32),
        lax.psum_scatter(
            part_proj.astype(jnp.bfloat16), "fsdp", scatter_dimension=0, tiled=True
        ).astype(jnp.float32),
        lax.psum_scatter(
            part_vec.astype(jnp.bfloat16), "fsdp", scatter_dimension=0, tiled=True
        ).astype(jnp.float32),
        lax.psum_scatter(
            part_bias.astype(jnp.bfloat16), "fsdp", scatter_dimension=0, tiled=True
        ).astype(jnp.float32),
    )
    return (result[None], input_grad[None], own_qkv, own_attn, own_fc, own_proj, own_vec, own_bias)


resident_most = 2 * 1024 * 1024


def contract_last(left, right):
    return lax.dot_general(left, right, (((1,), (1,)), ((), ())), preferred_element_type=jnp.float32)


def contract_first(left, right):
    return lax.dot_general(left, right, (((0,), (0,)), ((), ())), preferred_element_type=jnp.float32)


def head_lanes(head, shape):
    lane = lax.broadcasted_iota(jnp.int32, shape, 1)
    return (lane >= head * HEAD_DIM) & (lane < (head + 1) * HEAD_DIM)


def only_head(values, head):
    return jnp.where(head_lanes(head, values.shape), values, jnp.zeros_like(values))


def tile_pairs(length, tile, reach):
    for start in range(0, length, tile):
        first = max(0, (start - reach) // tile * tile)
        yield start, first, start + tile - first


norm_part = 64


def row_tiles(count, size, body):
    def step(i, carry):
        body(pl.multiple_of(i * size, size))
        return carry

    lax.fori_loop(0, count // size, step, 0)


MESH = pl.DeviceIdType.MESH


def remote(source, target, sent, landed, axis, index):
    return pltpu.make_async_remote_copy(
        src_ref=source,
        dst_ref=target,
        send_sem=sent,
        recv_sem=landed,
        device_id={axis: index},
        device_id_type=MESH,
    )


def greet(row, plane):
    barrier = pltpu.get_barrier_semaphore()
    for axis, size in (("seq", row), ("fsdp", plane)):
        own = lax.axis_index(axis)
        for ahead in range(1, size):
            pl.semaphore_signal(
                barrier,
                inc=1,
                device_id={axis: lax.rem(own + ahead, size)},
                device_id_type=MESH,
            )
    pl.semaphore_wait(barrier, row + plane - 2)


class RowGather:
    def __init__(self, own, view, sent, landed, row, chunks=1, has=None):
        self.own, self.view, self.sent, self.landed = own, view, sent, landed
        self.row, self.chips, self.chunks = row, row // 2, chunks
        self.has = has or (lambda i, c: None)
        self.me = lax.axis_index("seq")
        self.chip, self.core = self.me // 2, self.me % 2
        self.other = self.me + 1 - 2 * self.core

    def hop(self, i, c, way, source=None):
        place = self.view(i, c)
        target = (self.me + 2, self.me - 2, self.other)[way]
        return remote(
            place if source is None else source,
            place,
            self.sent.at[i, c, way],
            self.landed.at[i, c],
            "seq",
            target,
        )

    def when(self, i, c, condition, action):
        has = self.has(i, c)
        if has is not None:
            condition = has if condition is None else has & condition
        if condition is None:
            action()
        else:
            pl.when(condition)(action)

    def spread(self, i, c, forward, backward, source=None):
        self.when(i, c, forward, lambda: self.hop(i, c, 0, source).start())
        self.when(i, c, backward, lambda: self.hop(i, c, 1, source).start())
        self.when(i, c, None, lambda: self.hop(i, c, 2, source).start())

    def start(self, chunks=None):
        for c in chunks or range(self.chunks):
            self.spread(
                self.me, c, self.chip < self.chips - 1, self.chip > 0, self.own(c) if self.own else None
            )

    def pass_on(self, distance, chunks=None):
        chunks = chunks or range(self.chunks)

        def from_before():
            i = self.me - 2 * distance
            for c in chunks:
                self.when(i, c, None, lambda: self.hop(i, c, 2).wait_recv())
                self.when(i, c, self.chip < self.chips - 1, lambda: self.hop(i, c, 0).start())
                self.when(i, c, None, lambda: self.hop(i, c, 2).start())

        def from_after():
            i = self.me + 2 * distance
            for c in chunks:
                self.when(i, c, None, lambda: self.hop(i, c, 2).wait_recv())
                self.when(i, c, self.chip > 0, lambda: self.hop(i, c, 1).start())
                self.when(i, c, None, lambda: self.hop(i, c, 2).start())

        pl.when(self.chip >= distance)(from_before)
        pl.when(self.chip + distance < self.chips)(from_after)

    def wait_other(self, i):
        for c in range(self.chunks):
            self.when(i, c, None, lambda: self.hop(i, c, 2).wait_recv())

    def from_other_core(self):
        for k in range(self.chips):
            self.wait_other(2 * k + 1 - self.core)

    def drain(self):
        for k in range(self.chips):
            i = 2 * k + self.core
            for c in range(self.chunks):
                forward = (self.chip >= k) & (self.chip < self.chips - 1)
                backward = (self.chip <= k) & (self.chip > 0)
                self.when(i, c, forward, lambda: self.hop(i, c, 0).wait_send())
                self.when(i, c, backward, lambda: self.hop(i, c, 1).wait_send())
                self.when(i, c, None, lambda: self.hop(i, c, 2).wait_send())


class PlaneGather:
    def __init__(self, own, view, parts, sent, landed):
        self.own, self.view, self.parts, self.sent, self.landed = own, view, parts, sent, landed
        me = lax.axis_index("fsdp")
        self.me = me
        self.beside = me + 1 - 2 * (me % 2)
        self.above = lax.rem(me + 2, 4)
        self.corner = lax.rem(self.beside + 2, 4)

    def whole(self, i, slot, target, source=None):
        place = self.view(i, None)
        return remote(
            place if source is None else source,
            place,
            self.sent.at[slot],
            self.landed.at[slot],
            "fsdp",
            target,
        )

    def part(self, i, slot, target):
        place = self.view(i, self.parts[slot - 2])
        return remote(place, place, self.sent.at[slot], self.landed.at[slot], "fsdp", target)

    def start(self):
        self.whole(self.me, 0, self.beside, self.own).start()
        self.whole(self.me, 1, self.above, self.own).start()

    def pass_on(self):
        self.whole(self.beside, 0, self.beside).wait_recv()
        self.part(self.beside, 2, self.above).start()
        self.whole(self.above, 1, self.above).wait_recv()
        self.part(self.above, 3, self.beside).start()

    def finish(self):
        self.part(self.corner, 2, self.above).wait_recv()
        self.part(self.corner, 3, self.beside).wait_recv()

    def drain(self):
        self.whole(self.me, 0, self.beside).wait_send()
        self.whole(self.me, 1, self.above).wait_send()
        self.part(self.beside, 2, self.above).wait_send()
        self.part(self.above, 3, self.beside).wait_send()


def group_of(device):
    third = (device + 5) // 8 - (device + 4) // 8
    fifth = (device + 3) // 8 - (device + 2) // 8
    return device - (device + 4) // 8 - (device + 2) // 8 + 3 * third + 3 * fifth


def device_of(group):
    return group + (group + 5) // 8 + (group + 4) // 8 - 5 * ((group + 2) // 8)


def own_blocks(device, columns, width, span):
    groups = -(-width // span)

    def block_at(column):
        return groups * (column // width) + (column % width) // span

    return block_at(device * columns), block_at(device * columns + columns - 1)


def norm_rows(values, gain, shift):
    centred = values - jnp.mean(values, axis=-1, keepdims=True)
    inverse = lax.rsqrt(jnp.mean(centred * centred, axis=-1, keepdims=True) + norm_eps)
    return (centred * inverse) * gain + shift


def attend(head, pair, start, first, count, tile, qkv_ref, ids_col, ids_row, out_ref, lse_ref):
    span = out_ref.shape[1]
    rows, keys = pl.ds(start, tile), pl.ds(first, count)

    def lanes(kind):
        return pl.ds(kind * span + pair * 128, 128)

    query = only_head(qkv_ref[rows, lanes(0)], head)
    scores = contract_last(query, qkv_ref[keys, lanes(1)]) * (HEAD_DIM**-0.5)
    q_pos = start + lax.broadcasted_iota(jnp.int32, (tile, count), 0)
    k_pos = first + lax.broadcasted_iota(jnp.int32, (tile, count), 1)
    allowed = (k_pos <= q_pos) & (ids_col[rows, :1] == ids_row[:1, keys])
    masked = jnp.where(allowed, scores, masked_score)
    top = jnp.max(masked, axis=1, keepdims=True)
    weights = jnp.exp(masked - top)
    total = jnp.sum(weights, axis=1, keepdims=True)
    probs = (weights * (1.0 / total)).astype(jnp.bfloat16)
    value = only_head(qkv_ref[keys, lanes(2)], head)
    mixed = jnp.dot(probs, value, preferred_element_type=jnp.float32)
    out_ref[rows, lanes(0)] += mixed.astype(jnp.bfloat16)
    lane = lax.broadcasted_iota(jnp.int32, (tile, lse_ref.shape[1]), 1)
    lse_ref[rows, :] = jnp.where(lane == 2 * pair + head, top + jnp.log(total), lse_ref[rows, :])


def pick(index, values):
    chosen = values[-1]
    for k in range(len(values) - 1):
        chosen = jnp.where(index == k, values[k], chosen)
    return chosen


def chip_order(chip, step):
    rows = ((3, 3, 0, 0), (2, 0, 3, 1), (1, 2, 1, 2), (0, 1, 2, 3))
    return pick(step, [pick(chip, row) for row in rows])


class RowSum:
    def __init__(self, own, away, pair, chain, pair_sent, pair_landed, chain_sent, chain_landed):
        self.own, self.away, self.pair, self.chain = own, away, pair, chain
        self.pair_sent, self.pair_landed = pair_sent, pair_landed
        self.chain_sent, self.chain_landed = chain_sent, chain_landed
        self.me = lax.axis_index("seq")
        self.chips = 4
        self.chip, self.core = self.me // 2, self.me % 2
        self.other = self.me + 1 - 2 * self.core

    def exchange(self, t):
        return remote(
            self.away.at[t],
            self.pair.at[t],
            self.pair_sent.at[t],
            self.pair_landed.at[t],
            "seq",
            self.other,
        )

    def onward(self, t, slot, target):
        return remote(
            self.own.at[t],
            self.chain.at[slot],
            self.chain_sent.at[t],
            self.chain_landed.at[slot],
            "seq",
            target,
        )

    def put(self, t, terms):
        rows = self.own.shape[1]
        self.away[t] = terms[pl.ds(pl.multiple_of((1 - self.core) * rows, rows), rows), :].astype(
            jnp.bfloat16
        )
        self.exchange(t).start()
        self.own[t] = terms[pl.ds(pl.multiple_of(self.core * rows, rows), rows), :].astype(jnp.bfloat16)

    def add(self, t, arrived, slot):
        total = self.own[t].astype(jnp.float32) + arrived[slot].astype(jnp.float32)
        self.own[t] = total.astype(jnp.bfloat16)

    def step(self, t):
        self.exchange(t).wait_recv()
        self.add(t, self.pair, t)

        def forward():
            @pl.when(self.chip > 0)
            def _():
                self.onward(t, t, self.me + 2).wait_recv()
                self.add(t, self.chain, t)

            self.onward(t, t, self.me + 2).start()

        def backward():
            @pl.when(self.chip < self.chips - 1)
            def _():
                self.onward(t, t, self.me - 2).wait_recv()
                self.add(t, self.chain, t)

            slot = jnp.where(t == self.chip - 1, self.chips, t)
            self.onward(t, slot, self.me - 2).start()

        pl.when(t > self.chip)(forward)
        pl.when(t < self.chip)(backward)

    def final(self, total):
        t = self.chip
        self.exchange(t).wait_recv()
        total[...] = self.own[t].astype(jnp.float32) + self.pair[t].astype(jnp.float32)

        @pl.when(self.chip > 0)
        def _():
            self.onward(t, t, self.other).wait_recv()
            total[...] += self.chain[t].astype(jnp.float32)

        @pl.when(self.chip < self.chips - 1)
        def _():
            self.onward(t, self.chips, self.other).wait_recv()
            total[...] += self.chain[self.chips].astype(jnp.float32)

    def drain(self):
        for t in range(self.chips):
            self.exchange(t).wait_send()

            @pl.when(self.chip != t)
            def _():
                self.onward(t, t, self.other).wait_send()


class PlaneTerms:
    def __init__(self, view, terms, sent, landed):
        self.view, self.terms, self.sent, self.landed = view, terms, sent, landed
        self.me = lax.axis_index("fsdp")

    def to(self, ahead):
        i = lax.rem(self.me + ahead, 4)
        return remote(
            self.view(i), self.terms.at[self.me], self.sent.at[ahead], self.landed.at[self.me], "fsdp", i
        )

    def keep(self):
        return pltpu.make_async_copy(
            self.view(self.me), self.terms.at[self.me], self.landed.at[self.me]
        )

    def start(self):
        self.keep().start()
        for ahead in (3, 1, 2):
            self.to(ahead).start()

    def arrive(self):
        self.keep().wait()
        for ahead in range(1, 4):
            i = lax.rem(self.me + ahead, 4)
            remote(
                self.view(i), self.terms.at[i], self.sent.at[ahead], self.landed.at[i], "fsdp", i
            ).wait_recv()

    def drain(self):
        for ahead in range(1, 4):
            self.to(ahead).wait_send()


def backward_attend(
    head, start, first, count, tile, qkv_ref, attn_ref, grad_ref, lse_ref, ids_col, ids_row, out_ref
):
    span = attn_ref.shape[1]
    scale = HEAD_DIM**-0.5
    rows, keys = pl.ds(start, tile), pl.ds(first, count)
    query = only_head(qkv_ref[rows, :span], head)
    key = qkv_ref[keys, span : 2 * span]
    grad = only_head(grad_ref[rows, :], head)
    delta = jnp.sum(
        grad.astype(jnp.float32) * attn_ref[rows, :].astype(jnp.float32), axis=1, keepdims=True
    )
    scores = contract_last(query, key) * scale
    q_pos = start + lax.broadcasted_iota(jnp.int32, (tile, count), 0)
    k_pos = first + lax.broadcasted_iota(jnp.int32, (tile, count), 1)
    allowed = (k_pos <= q_pos) & (ids_col[rows, :1] == ids_row[:1, keys])
    lane = lax.broadcasted_iota(jnp.int32, (tile, lse_ref.shape[1]), 1)
    lse = jnp.sum(jnp.where(lane == head, lse_ref[rows, :], 0.0), axis=1, keepdims=True)
    probs = jnp.where(allowed, jnp.exp(scores - lse), 0.0)
    prob_grad = contract_last(grad, qkv_ref[keys, 2 * span :])
    score_grad = (probs * (prob_grad - delta)).astype(jnp.bfloat16)
    out_ref[rows, :span] += scale * jnp.dot(
        score_grad, only_head(key, head), preferred_element_type=jnp.float32
    )
    out_ref[keys, span : 2 * span] += scale * contract_first(score_grad, query)
    out_ref[keys, 2 * span :] += contract_first(probs.astype(jnp.bfloat16), grad)


def block_kernel(
    reach,
    x_ref,
    cot_ref,
    small_ref,
    blocks_ref,
    wo_ref,
    fc_ref,
    proj_ref,
    result_ref,
    input_grad_ref,
    fc_terms,
    proj_terms,
    attn_terms,
    nat_blocks,
    vec_out,
    qkv_terms,
    cot_all,
    h1_all,
    wo_all,
    wo_z,
    turn,
    cot_own,
    x_v,
    small_v,
    vec_v,
    ids_col,
    ids_row,
    pieces,
    w_v,
    qkv_v,
    attn_o,
    lse_v,
    attn_v,
    fc_v,
    proj_v,
    own1,
    away1,
    pair1,
    chain1,
    own2,
    away2,
    pair2,
    chain2,
    dr_all,
    resid_own,
    dresid_own,
    total,
    wide,
    bias_sum,
    gv,
    vec_send,
    vec_land,
    plane_send,
    plane_land,
    small_sent,
    small_landed,
    first_sent,
    first_landed,
    piece_sent,
    piece_landed,
    w_sent,
    w_landed,
    x_sent,
    x_landed,
    cot_sent,
    cot_landed,
    attn_sent,
    attn_landed,
    fc_sent,
    fc_landed,
    proj_sent,
    proj_landed,
    wo_sent,
    wo_landed,
    wo_plane_sent,
    wo_plane_landed,
    wo_pair_sent,
    wo_pair_landed,
    local_sem,
    pair_sent,
    pair_landed,
    chain_sent,
    chain_landed,
    dr_sent,
    dr_landed,
    terms_sent,
    terms_landed,
    nat_sent,
    nat_landed,
    vec_sent,
    vec_landed,
    plane_sent,
    plane_landed,
    load_sem,
):
    row, plane, chips = 8, 4, 4
    seq, fsdp = lax.axis_index("seq"), lax.axis_index("fsdp")
    chip, core = seq // 2, seq % 2
    ends = (chip == 0) | (chip == chips - 1)
    width, own_rows = x_ref.shape
    length = own_rows * row
    pair_rows = 2 * own_rows
    units = fc_ref.shape[0]
    span = attn_o.shape[1]
    share = width // row
    depth = width // plane
    groups = -(-width // span)
    group = group_of(seq)
    columns = qkv_columns(width, row)
    bf, f32 = jnp.bfloat16, jnp.float32
    tiles = [(0, 512), (512, 1024), (1024, width)]

    def load(source, target, slot):
        copy = pltpu.make_async_copy(source, target, load_sem.at[slot])
        copy.start()
        return copy

    def pair_at(t):
        return pl.ds(pl.multiple_of(t * pair_rows, pair_rows), pair_rows)

    own_at = pl.ds(pl.multiple_of(seq * own_rows, own_rows), own_rows)
    half_at = pl.ds(pl.multiple_of(core * own_rows, own_rows), own_rows)
    hidden_sum = RowSum(
        own1, away1, pair1, chain1, pair_sent.at[0], pair_landed.at[0], chain_sent.at[0], chain_landed.at[0]
    )
    out_sum = RowSum(
        own2, away2, pair2, chain2, pair_sent.at[1], pair_landed.at[1], chain_sent.at[1], chain_landed.at[1]
    )
    dr_line = RowGather(
        None,
        lambda i, c: dr_all.at[pl.ds(pl.multiple_of(i * own_rows, own_rows), own_rows)],
        dr_sent,
        dr_landed,
        row,
    )
    fc_back = PlaneTerms(lambda i: fc_v.at[i], fc_terms, terms_sent.at[0], terms_landed.at[0])
    proj_back = PlaneTerms(lambda i: proj_v.at[i], proj_terms, terms_sent.at[1], terms_landed.at[1])

    used = []

    def keep(source, target):
        copy = pltpu.make_async_copy(source, target, local_sem.at[len(used)])
        copy.start()
        used.append(copy)

    vec = vec_v
    vec[...] = jnp.zeros_like(vec)
    w_v[...] = jnp.zeros_like(w_v)
    bias_sum[...] = jnp.zeros_like(bias_sum)
    gv[...] = jnp.zeros_like(gv)
    attn_o[...] = jnp.zeros_like(attn_o)
    lse_v[...] = jnp.zeros_like(lse_v)
    def turned(source):
        turning = pltpu.make_async_copy(source, turn, load_sem.at[0])
        turning.start()
        turning.wait()
        return turn[...].astype(f32).T.astype(bf)

    x_v[own_at, :] = turned(x_ref)
    greet(row, plane)
    own_small = pltpu.make_async_copy(small_ref, small_v.at[fsdp, seq], small_landed.at[seq])
    own_small.start()

    def small_to(target, slot):
        return remote(
            small_ref, small_v.at[fsdp, seq], small_sent.at[slot], small_landed.at[seq], "seq", target
        )

    for ahead in range(1, row):
        small_to(lax.rem(seq + ahead, row), ahead - 1).start()

    first_block, last_block = own_blocks(seq, qkv_columns(width, row), width, span)

    def piece(k):
        block = first_block + k
        kind, at = block // groups, block % groups
        begins = kind * width + at * span
        later = (seq * qkv_columns(width, row) + width * 3 - begins - 1) // (width * 3)
        target = device_of(at)
        place = pieces.at[kind, later]
        return block <= last_block, target, place, piece_landed.at[kind, later]

    for k in range(4):
        there, target, place, landed = piece(k)

        @pl.when(there & (target == seq))
        def _():
            pltpu.make_async_copy(blocks_ref.at[k], place, landed).start()

        @pl.when(there & (target != seq))
        def _():
            remote(blocks_ref.at[k], place, piece_sent.at[k], landed, "seq", target).start()

    def block_of(target):
        return lambda i, c: target.at[pl.ds(pl.multiple_of(i * own_rows, own_rows), own_rows)]

    x_line = RowGather(None, block_of(x_v), x_sent, x_landed, row)
    used.append(None)
    x_line.start()

    wo_line = RowGather(lambda c: wo_ref, lambda i, c: wo_z.at[i], wo_sent, wo_landed, row)
    keep(wo_ref, wo_z.at[seq])
    def slab(target):
        def view(i, part):
            start, count = (0, target.shape[1]) if part is None else part
            return target.at[i, pl.ds(start, count)]

        return view

    units = fc_ref.shape[0]
    cut = units // 32 * 16
    parts = ((0, cut), (cut, units - cut))
    fc_plane = PlaneGather(fc_ref, slab(fc_v), parts, fc_sent, fc_landed)
    proj_plane = PlaneGather(proj_ref, slab(proj_v), parts, proj_sent, proj_landed)
    fc_plane.start()
    cot_own[...] = turned(cot_ref)
    keep(cot_own, block_of(cot_all)(seq, 0))
    keep(fc_ref, fc_v.at[fsdp])
    keep(proj_ref, proj_v.at[fsdp])

    for other in range(row):
        pltpu.make_async_copy(small_ref, small_v.at[fsdp, other], small_landed.at[other]).wait()

    def small_plane(ahead):
        return remote(
            small_v.at[fsdp],
            small_v.at[fsdp],
            first_sent.at[ahead - 1],
            first_landed.at[ahead - 1],
            "fsdp",
            lax.rem(fsdp + ahead, plane),
        )

    for ahead in range(1, plane):
        small_plane(ahead).start()
    for other in range(row):
        lanes = pl.ds(other * own_rows, own_rows)
        ids = jnp.broadcast_to(small_v[fsdp, other, 3:4, :own_rows], (own_rows, own_rows))
        ids_row[:, lanes] = ids[:8]
        ids_col[lanes, :] = ids.T
    own_w = pl.ds(pl.multiple_of(fsdp * depth, 16), depth)

    @pl.when(group < groups)
    def _():
        for kind in range(3):
            begins = kind * width + group * span
            ends = begins + jnp.minimum(span, width - group * span) - 1
            cols = qkv_columns(width, row)
            straddles = ends // cols != begins // cols
            pltpu.make_async_copy(
                blocks_ref.at[0], pieces.at[kind, 0], piece_landed.at[kind, 0]
            ).wait()
            w_v[own_w, kind * span : (kind + 1) * span] = pieces[kind, 0]

            @pl.when(straddles)
            def _():
                pltpu.make_async_copy(
                    blocks_ref.at[0], pieces.at[kind, 1], piece_landed.at[kind, 1]
                ).wait()
                w_v[own_w, kind * span : (kind + 1) * span] = pieces[kind, 0] + pieces[kind, 1]

    def w_view(i, part):
        start, count = (0, depth) if part is None else part
        return w_v.at[pl.ds(pl.multiple_of(i * depth + start, 16), count)]

    half = depth // 32 * 16
    w_plane = PlaneGather(None, w_view, ((0, half), (half, depth - half)), w_sent, w_landed)
    w_plane.start()
    x_line.pass_on(1)
    for ahead in range(1, plane):
        remote(
            small_v.at[fsdp],
            small_v.at[lax.rem(fsdp + plane - ahead, plane)],
            first_sent.at[ahead - 1],
            first_landed.at[ahead - 1],
            "fsdp",
            lax.rem(fsdp + ahead, plane),
        ).wait_recv()
    for i in range(plane):
        for other in range(row):
            vec[2 * i : 2 * i + 2, share * other : share * (other + 1)] = small_v[i, other, 0:2, :share]

    wo_cut = 6 * 128
    wo_lanes = ((0, wo_cut), (wo_cut, width - wo_cut))

    def wo_view(lanes):
        def view(i, part):
            start, count = (0, depth) if part is None else part
            rows = pl.ds(pl.multiple_of(i * depth + start, 16), count)
            return wo_all.at[rows, pl.ds(*lanes)]

        return view

    wo_planes = [
        PlaneGather(
            None, wo_view(lanes), ((0, half), (half, depth - half)), wo_plane_sent, wo_plane_landed
        )
        for lanes in wo_lanes
    ]

    def wo_pair(core, ahead):
        i = lax.rem(fsdp + ahead, plane)
        place = wo_view(wo_lanes[core])(i, None)
        return remote(place, place, wo_pair_sent.at[i], wo_pair_landed.at[i], "seq", x_line.other)

    def wo_pairs(action, core):
        for ahead in range(1, plane):
            action(wo_pair(core, ahead))

    def on_own_core(action):
        for core in range(2):
            pl.when(x_line.core == core)(functools.partial(action, core))

    cot_line = RowGather(lambda c: cot_own, block_of(cot_all), cot_sent, cot_landed, row)
    def chunk(i, c):
        return attn_v.at[:, pl.ds(pl.multiple_of(group_of(i) * span + c * 128, 128), 128)]

    attn_line = RowGather(
        lambda c: attn_o.at[:, pl.ds(c * 128, 128)],
        chunk,
        attn_sent,
        attn_landed,
        row,
        chunks=2,
        has=lambda i, c: group_of(i) < groups - c,
    )
    def own_chunk(c):
        lanes = pl.ds(pl.multiple_of(group * span + c * 128, 128), 128)
        return pltpu.make_async_copy(
            attn_o.at[:, pl.ds(c * 128, 128)], attn_v.at[:, lanes], piece_landed.at[c, 0]
        )

    def send_chunk(c):
        attn_line.start([c])
        pl.when(group < groups - c)(lambda: own_chunk(c).start())

    def attention_forward(h1_v, wo_own, wo_zv):
        def norm_block(i):
            def part(j):
                rows = pl.ds(pl.multiple_of(i * own_rows + j, norm_part), norm_part)
                hidden = norm_rows(x_v[rows, :].astype(jnp.float32), vec[0:1, :width], vec[1:2, :width])
                h1_v[rows, :] = hidden.astype(jnp.bfloat16)

            row_tiles(own_rows, norm_part, part)

        def norm_arrived(distance):
            if 0 < distance < row // 2:
                pl.when(x_line.chip >= distance)(lambda: norm_block(seq - 2 * distance))
                pl.when(x_line.chip + distance < row // 2)(lambda: norm_block(seq + 2 * distance))

            def other(i):
                x_line.wait_other(i)
                norm_block(i)

            if distance == 1:
                other(x_line.other)
            elif distance > 1:
                nearer = distance - 1
                pl.when(x_line.chip >= nearer)(lambda: other(x_line.other - 2 * nearer))
                pl.when(x_line.chip + nearer < row // 2)(lambda: other(x_line.other + 2 * nearer))

        norm_block(seq)
        norm_arrived(1)
        w_plane.pass_on()
        fc_plane.pass_on()
        proj_plane.start()
        x_line.pass_on(2)
        norm_arrived(2)
        x_line.pass_on(3)
        wo_line.start()
        norm_arrived(3)
        norm_arrived(4)
        w_plane.finish()

        lanes = pl.ds(pl.multiple_of(group * span, span), span)
        query_shift, value_shift = vec[2:3, lanes], vec[3:4, lanes]

        def project(i):
            rows = pl.ds(i, 2 * own_rows)
            mixed = jnp.dot(h1_v[rows, :], w_v[...], preferred_element_type=jnp.float32)
            qkv_v[rows, :span] = (mixed[:, :span] + query_shift).astype(jnp.bfloat16)
            qkv_v[rows, span : 2 * span] = mixed[:, span : 2 * span].astype(jnp.bfloat16)
            qkv_v[rows, 2 * span :] = (mixed[:, 2 * span :] + value_shift).astype(jnp.bfloat16)

        wo_line.pass_on(1)
        row_tiles(length, 2 * own_rows, project)
        wo_line.pass_on(2)
        proj_plane.pass_on()
        h1_kept = pltpu.make_async_copy(h1_v, h1_all, load_sem.at[1])
        h1_kept.start()

        tile = 256

        def heads(pair):
            def head(h, carry):
                for start, first, count in tile_pairs(length, tile, reach):
                    attend(h, pair, start, first, count, tile, qkv_v, ids_col, ids_row, attn_o, lse_v)
                return carry

            lax.fori_loop(0, 2, head, 0)

        heads(0)

        send_chunk(0)
        wo_line.pass_on(3)
        wo_line.from_other_core()
        used[1].wait()
        used[1] = None
        wo_load = pltpu.make_async_copy(wo_z, wo_zv, load_sem.at[0])
        wo_load.start()
        wo_load.wait()
        for i in range(row):
            wo_own[:, share * i : share * (i + 1)] = wo_zv[i, :, :share]
        for core, lanes in enumerate(wo_lanes):
            wo_planes[core].own = wo_own.at[:, pl.ds(*lanes)]

        on_own_core(lambda core: wo_planes[core].start())
        wo_kept = pltpu.make_async_copy(wo_own, wo_view((0, width))(fsdp, None), load_sem.at[2])
        wo_kept.start()
        heads(1)
        send_chunk(1)
        cot_line.start()
        h1_kept.wait()
        wo_kept.wait()
        attn_line.pass_on(1)
        attn_line.pass_on(2)
        on_own_core(lambda core: wo_planes[core].pass_on())
        attn_line.pass_on(3)
        cot_line.pass_on(1)
        on_own_core(lambda core: wo_planes[core].drain())

    pl.run_scoped(
        attention_forward,
        pltpu.VMEM((length, width), bf),
        pltpu.VMEM((depth, width), bf),
        pltpu.VMEM(wo_z.shape, bf),
    )
    on_own_core(lambda core: wo_planes[core].finish())
    on_own_core(lambda core: wo_pairs(lambda copy: copy.start(), core))
    attn_line.from_other_core()
    for c in range(2):
        pl.when(group < groups - c)(lambda: own_chunk(c).wait())
    on_own_core(lambda core: wo_pairs(lambda copy: copy.wait_recv(), 1 - core))
    fc_plane.finish()
    for i in range(2, 5):
        used[i].wait()
        used[i] = None

    def feed_forward(w_attn, cot_v, h2_v, act_v, dpre_v, pre_v, dact_v):
        w_load = load(wo_all.at[pl.ds(0, width)], w_attn, 1)
        w_load.wait()

        def back_through(rows, values, weights):
            for low, high in tiles:
                terms = jnp.dot(
                    values[0, rows, :], weights[0, :, low:high], preferred_element_type=f32
                )
                for f in range(1, plane):
                    terms += jnp.dot(
                        values[f, rows, :], weights[f, :, low:high], preferred_element_type=f32
                    )
                wide[:, low:high] = terms

        def chunk(p, carry):
            t = chip_order(chip, p)
            rows = pair_at(t)
            for low, high in tiles:
                wide[:, low:high] = jnp.dot(
                    attn_v[rows, :width], w_attn[:, low:high], preferred_element_type=f32
                )

            def second_norm(i):
                part = pl.ds(i, norm_part)
                place = pl.ds(pl.multiple_of(t * pair_rows + i, norm_part), norm_part)
                resid = wide[part, :] + x_v[place, :].astype(f32) + vec_v[4:5, :width]
                wide[part, :] = resid
                hidden = norm_rows(resid, vec_v[5:6, :width], vec_v[6:7, :width])
                h2_v[place, :] = hidden.astype(bf)

            row_tiles(pair_rows, norm_part, second_norm)

            @pl.when(t == chip)
            def _():
                resid_own[...] = wide[half_at, :]

            def unit_block(f, carry):
                pre_v[...] = contract_last(h2_v[rows, :], fc_v[f])
                shift = small_v[f, seq, 2:3, :units]

                def gelu(i):
                    part = pl.ds(i, 32)
                    gelu_value, gelu_slope = gelu_parts(pre_v[part, :] + shift)
                    place = pl.ds(pl.multiple_of(t * pair_rows + i, 32), 32)
                    act_v[f, place, :] = gelu_value.astype(bf)
                    dpre_v[f, place, :] = gelu_slope.astype(bf)

                row_tiles(pair_rows, 32, gelu)
                return carry

            lax.fori_loop(0, plane, unit_block, 0)
            for step in range(2):
                pl.when(p == step)(functools.partial(cot_line.pass_on, step + 2))
            return carry

        lax.fori_loop(0, chips, chunk, 0)
        cot_line.from_other_core()
        cot_load = load(cot_all, cot_v, 3)
        proj_plane.finish()
        cot_load.wait()

        def back_chunk(p, carry):
            t = chip_order(chip, p)
            rows = pair_at(t)

            def unit_block(f, carry):
                dact_v[...] = contract_last(cot_v[rows, :], proj_v[f])

                def through_gelu(i):
                    place = pl.ds(pl.multiple_of(t * pair_rows + i, 32), 32)
                    dpre = dact_v[pl.ds(i, 32), :] * dpre_v[f, place, :].astype(f32)
                    dpre_v[f, place, :] = dpre.astype(bf)
                    bias_sum[pl.ds(f, 1), :units] += jnp.sum(dpre, axis=0, keepdims=True)

                row_tiles(pair_rows, 32, through_gelu)
                return carry

            lax.fori_loop(0, plane, unit_block, 0)
            back_through(rows, dpre_v, fc_v)
            hidden_sum.put(t, wide)

            @pl.when(ends & (p < chips - 1))
            def _():
                hidden_sum.step(t)

            return carry

        def weight_terms(values, others, stage):
            def unit_block(f, carry):
                for low, high in tiles:
                    stage[f, :, low:high] = contract_first(values[f], others[:, low:high]).astype(bf)
                return carry

            lax.fori_loop(0, plane, unit_block, 0)

        lax.fori_loop(0, chips, back_chunk, 0)
        fc_plane.drain()
        weight_terms(dpre_v, h2_v, fc_v)
        fc_back.start()

        @pl.when(jnp.logical_not(ends))
        def _():
            hidden_sum.step(chip_order(chip, 0))
            hidden_sum.step(chip_order(chip, 1))

        @pl.when(jnp.logical_not(ends))
        def _():
            hidden_sum.step(chip_order(chip, 2))

        hidden_sum.final(total)

        def second_norm_back(i):
            part = pl.ds(i, norm_part)
            resid = resid_own[part, :]
            centred = resid - jnp.mean(resid, axis=-1, keepdims=True)
            inverse = lax.rsqrt(jnp.mean(centred * centred, axis=-1, keepdims=True) + norm_eps)
            normed = centred * inverse
            grad_hidden = total[part, :]
            scaled = grad_hidden * vec_v[5:6, :width]
            back = inverse * (
                scaled
                - jnp.mean(scaled, axis=-1, keepdims=True)
                - normed * jnp.mean(scaled * normed, axis=-1, keepdims=True)
            )
            place = pl.ds(pl.multiple_of(seq * own_rows + i, norm_part), norm_part)
            cot = cot_v[place, :].astype(f32)
            grad_resid = cot + back
            dresid_own[part, :] = grad_resid
            dr_all[place, :] = grad_resid.astype(bf)
            for at, values in ((4, grad_resid), (5, grad_hidden * normed), (6, grad_hidden), (7, cot)):
                gv[at : at + 1, :width] += jnp.sum(values, axis=0, keepdims=True)

        row_tiles(own_rows, norm_part, second_norm_back)
        dr_line.start()

        def out_chunk(p, carry):
            t = chip_order(chip, p)
            back_through(pair_at(t), act_v, proj_v)
            out_sum.put(t, wide)

            @pl.when(ends & (p < chips - 1))
            def _():
                out_sum.step(t)

            return carry

        lax.fori_loop(0, chips, out_chunk, 0)
        proj_plane.drain()
        dr_line.pass_on(1)
        weight_terms(act_v, cot_v, proj_v)
        proj_back.start()
        dr_line.pass_on(2)

    pl.run_scoped(
        feed_forward,
        pltpu.VMEM((width, width), bf),
        pltpu.VMEM((length, width), bf),
        pltpu.VMEM((length, width), bf),
        pltpu.VMEM((plane, length, units), bf),
        pltpu.VMEM((plane, length, units), bf),
        pltpu.VMEM((pair_rows, units), f32),
        pltpu.VMEM((pair_rows, units), f32),
    )

    def attention_back(w_rows, h1_v, da_v, dqkv, dqkv16, ga, gq, gqt):
        loads = [
            load(wo_all.at[pl.ds(pl.multiple_of(group * span, span), span)], w_rows, 0),
            load(h1_all, h1_v, 1),
        ]
        dqkv[...] = jnp.zeros_like(dqkv)
        dr_line.pass_on(3)
        dr_line.from_other_core()
        loads[0].wait()

        inside = lax.broadcasted_iota(jnp.int32, w_rows.shape, 0) < width - group * span
        w_rows[...] = jnp.where(inside, w_rows[...], jnp.zeros_like(w_rows))

        def into_heads(i):
            rows = pl.ds(i, pair_rows)
            da_v[rows, :] = contract_last(dr_all[rows, :], w_rows[...]).astype(bf)

        row_tiles(length, pair_rows, into_heads)

        @pl.when(jnp.logical_not(ends))
        def _():
            out_sum.step(chip_order(chip, 0))

        def heads(h, carry):
            for start, first, count in tile_pairs(length, 256, reach):
                backward_attend(
                    h, start, first, count, 256, qkv_v, attn_o, da_v, lse_v, ids_col, ids_row, dqkv
                )
            return carry

        lax.fori_loop(0, 2, heads, 0)

        @pl.when(jnp.logical_not(ends))
        def _():
            out_sum.step(chip_order(chip, 1))

        lax.fori_loop(2, 4, heads, 0)

        @pl.when(jnp.logical_not(ends))
        def _():
            out_sum.step(chip_order(chip, 2))

        lanes = pl.ds(pl.multiple_of(group * span, span), span)
        gv[2:3, lanes] = jnp.sum(dqkv[:, :span], axis=0, keepdims=True)
        gv[3:4, lanes] = jnp.sum(dqkv[:, 2 * span :], axis=0, keepdims=True)
        dqkv16[...] = dqkv[...].astype(bf)

        loads[1].wait()

        def kind_terms(kind):
            lanes = pl.ds(kind * span, span)
            return PlaneTerms(
                lambda i: gq.at[pl.ds(pl.multiple_of(i * depth, 16), depth), lanes],
                qkv_terms.at[kind],
                terms_sent.at[2 + kind],
                terms_landed.at[2 + kind],
            )

        kinds = [kind_terms(kind) for kind in range(3)]
        for kind in range(3):
            lanes = slice(kind * span, (kind + 1) * span)
            for low in range(0, width, span):
                high = min(low + span, width)
                gq[low:high, lanes] = contract_first(h1_v[:, low:high], dqkv16[:, lanes]).astype(bf)
            kinds[kind].start()

        hidden_sum.drain()

        def chunk(p, carry):
            t = chip_order(chip, p)
            for low, high in tiles:
                wide[:, low:high] = contract_last(dqkv16[pair_at(t), :], w_v[low:high, :])
            hidden_sum.put(t, wide)

            @pl.when(ends & (p < chips - 1))
            def _():
                hidden_sum.step(t)

            return carry

        lax.fori_loop(0, chips, chunk, 0)

        place = lax.broadcasted_iota(jnp.int32, (width, span), 0)
        lane = lax.broadcasted_iota(jnp.int32, (width, span), 1)
        chosen = ((place == seq * share + lane) & (lane < share)).astype(f32).astype(bf)

        def own_columns(i):
            rows = pl.ds(i, pair_rows)
            da_v[rows, :] = jnp.dot(dr_all[rows, :], chosen, preferred_element_type=f32).astype(bf)

        row_tiles(length, pair_rows, own_columns)
        for low in range(0, width, span):
            high = min(low + span, width)
            ga[low:high, :] = contract_first(attn_v[:, low:high], da_v[...]).astype(bf)
        attn_plane = PlaneTerms(
            lambda i: ga.at[pl.ds(pl.multiple_of(i * depth, 16), depth)],
            attn_terms,
            terms_sent.at[5],
            terms_landed.at[5],
        )
        attn_plane.start()

        @pl.when(jnp.logical_not(ends))
        def _():
            for p in range(chips - 1):
                hidden_sum.step(chip_order(chip, p))

        out_sum.final(total)
        for low, high in tiles:
            resid_own[:, low:high] += total[:, low:high] + vec_v[7:8, low:high]
        result_copy = load(resid_own, result_ref, 2)

        hidden_sum.final(total)

        def first_norm_back(i):
            part = pl.ds(i, norm_part)
            values = x_v[pl.ds(pl.multiple_of(seq * own_rows + i, norm_part), norm_part), :].astype(f32)
            centred = values - jnp.mean(values, axis=-1, keepdims=True)
            inverse = lax.rsqrt(jnp.mean(centred * centred, axis=-1, keepdims=True) + norm_eps)
            normed = centred * inverse
            grad_hidden = total[part, :]
            scaled = grad_hidden * vec_v[0:1, :width]
            back = inverse * (
                scaled
                - jnp.mean(scaled, axis=-1, keepdims=True)
                - normed * jnp.mean(scaled * normed, axis=-1, keepdims=True)
            )
            dresid_own[part, :] += back
            for at, summed in ((0, grad_hidden * normed), (1, grad_hidden)):
                gv[at : at + 1, :width] += jnp.sum(summed, axis=0, keepdims=True)

        row_tiles(own_rows, norm_part, first_norm_back)

        input_copy = load(dresid_own, input_grad_ref, 3)

        vec_send[...] = jnp.zeros_like(vec_send)
        plane_send[...] = jnp.zeros_like(plane_send)
        for i in range(row):
            vec_send[i, :, :share] = gv[:, share * i : share * (i + 1)]

        def vec_to(ahead):
            i = lax.rem(seq + ahead, row)
            return remote(
                vec_send.at[i], vec_land.at[seq], vec_sent.at[ahead], vec_landed.at[seq], "seq", i
            )

        keep = pltpu.make_async_copy(vec_send.at[seq], vec_land.at[seq], vec_landed.at[seq])
        keep.start()
        for ahead in range(1, row):
            vec_to(ahead).start()

        def nat(kind, late):
            begins = kind * width + group * span
            last = begins + jnp.minimum(span, width - group * span) - 1
            before, after = begins // columns, last // columns
            target = after if late else before
            slot = kind * groups + group - own_blocks(target, columns, width, span)[0]
            there = (group < groups) & (before != after) if late else group < groups
            return there, target, slot

        def nat_copy(kind, late, target, slot):
            return remote(
                gq.at[pl.ds(kind * depth, depth), pl.ds(0, span)],
                nat_blocks.at[slot],
                nat_sent.at[kind, late],
                nat_landed.at[slot],
                "seq",
                target,
            )

        for kind in range(3):
            kinds[kind].arrive()
            load(qkv_terms.at[kind], gqt.at[kind], 0).wait()
            kinds[kind].drain()
            part = gqt[kind, 0].astype(f32)
            for f in range(1, plane):
                part += gqt[kind, f].astype(f32)
            gq[kind * depth : (kind + 1) * depth, :span] = part.astype(bf)
            for late in range(2):
                there, target, slot = nat(kind, late)

                @pl.when(there & (target != seq))
                def _():
                    nat_copy(kind, late, target, slot).start()

                @pl.when(there & (target == seq))
                def _():
                    pltpu.make_async_copy(
                        gq.at[pl.ds(kind * depth, depth), pl.ds(0, span)],
                        nat_blocks.at[slot],
                        nat_landed.at[slot],
                    ).start()

        for i in range(row):
            pltpu.make_async_copy(vec_send.at[i], vec_land.at[i], vec_landed.at[i]).wait()
        summed = vec_land[0]
        for i in range(1, row):
            summed += vec_land[i]
        for i in range(plane):
            plane_send[i, 0:2, :] = summed[2 * i : 2 * i + 2, :]
            plane_send[i, 2:3, :] = bias_sum[i : i + 1, :]
        vec_plane = PlaneTerms(lambda i: plane_send.at[i], plane_land, plane_sent, plane_landed)
        vec_plane.start()
        first_block, last_block = own_blocks(seq, columns, width, span)
        for k in range(4):

            @pl.when(first_block + k <= last_block)
            def _():
                pltpu.make_async_copy(
                    gq.at[pl.ds(0, depth), pl.ds(0, span)], nat_blocks.at[k], nat_landed.at[k]
                ).wait()

        vec_plane.arrive()
        vec_out[...] = plane_land[0] + plane_land[1] + plane_land[2] + plane_land[3]
        vec_plane.drain()
        for ahead in range(1, row):
            vec_to(ahead).wait_send()
        for kind in range(3):
            for late in range(2):
                there, target, slot = nat(kind, late)

                @pl.when(there & (target != seq))
                def _():
                    nat_copy(kind, late, target, slot).wait_send()

        attn_plane.drain()
        attn_plane.arrive()
        result_copy.wait()
        input_copy.wait()

    pl.run_scoped(
        attention_back,
        pltpu.VMEM((span, width), bf),
        pltpu.VMEM((length, width), bf),
        pltpu.VMEM((length, span), bf),
        pltpu.VMEM((length, 3 * span), f32),
        pltpu.VMEM((length, 3 * span), bf),
        pltpu.VMEM((width, span), bf),
        pltpu.VMEM((width, 3 * span), bf),
        pltpu.VMEM((3, plane, depth, span), bf),
    )
    for ahead in range(1, row):
        small_to(lax.rem(seq + ahead, row), ahead - 1).wait_send()
    for ahead in range(1, plane):
        small_plane(ahead).wait_send()
    for k in range(4):
        there, target, place, landed = piece(k)

        @pl.when(there & (target != seq))
        def _():
            remote(blocks_ref.at[k], place, piece_sent.at[k], landed, "seq", target).wait_send()

    for line in (x_line, wo_line, cot_line, attn_line, w_plane):
        line.drain()
    on_own_core(lambda core: wo_pairs(lambda copy: copy.wait_send(), core))
    for copy in used:
        if copy is not None:
            copy.wait()
    for summing in (hidden_sum, out_sum):
        summing.drain()
    dr_line.drain()
    for terms in (fc_back, proj_back):
        terms.drain()
        terms.arrive()


def qkv_columns(width, row):
    return 3 * width // row


def block_phase(x_own, cot_own, small, blocks, wo_own, fc_own, proj_own, reach):
    width, own_rows = x_own.shape
    row, plane, chips, span = 8, 4, 4, 4 * HEAD_DIM
    length, units, depth = own_rows * row, fc_own.shape[0], width // plane
    bf, f32 = jnp.bfloat16, jnp.float32
    anywhere = pl.BlockSpec(memory_space=pl.ANY)
    in_vmem = pl.BlockSpec(memory_space=pltpu.VMEM)
    dma = pltpu.SemaphoreType.DMA
    block = (own_rows, width)

    def shaped(*shape, dtype=bf):
        return jax.ShapeDtypeStruct(shape, dtype)

    return pl.pallas_call(
        lambda *refs: block_kernel(reach, *refs),
        out_shape=[
            shaped(*block, dtype=f32),
            shaped(*block, dtype=f32),
            shaped(plane, units, width),
            shaped(plane, units, width),
            shaped(plane, depth, span),
            shaped(4, depth, span),
            shaped(8, span, dtype=f32),
            shaped(3, plane, depth, span),
            shaped(length, width),
            shaped(length, width),
            shaped(8 * span, width),
            shaped(row, depth, span),
        ],
        in_specs=[anywhere] * 7,
        out_specs=[anywhere] * 6 + [in_vmem] + [anywhere] * 5,
        scratch_shapes=[
            pltpu.VMEM((width, own_rows), bf),
            pltpu.VMEM(block, bf),
            pltpu.VMEM((length, width), bf),
            pltpu.VMEM((plane, row, 8, span), f32),
            pltpu.VMEM((8, 8 * span), f32),
            pltpu.VMEM((length, own_rows), f32),
            pltpu.VMEM((8, length), f32),
            pltpu.VMEM((3, 2, depth, span), bf),
            pltpu.VMEM((width, 3 * span), bf),
            pltpu.VMEM((length, 3 * span), bf),
            pltpu.VMEM((length, span), bf),
            pltpu.VMEM((length, 128), f32),
            pltpu.VMEM((length, 7 * span), bf),
            pltpu.VMEM((plane, units, width), bf),
            pltpu.VMEM((plane, units, width), bf),
            pltpu.VMEM((chips,) + block, bf),
            pltpu.VMEM((chips,) + block, bf),
            pltpu.VMEM((chips,) + block, bf),
            pltpu.VMEM((chips + 1,) + block, bf),
            pltpu.VMEM((chips,) + block, bf),
            pltpu.VMEM((chips,) + block, bf),
            pltpu.VMEM((chips,) + block, bf),
            pltpu.VMEM((chips + 1,) + block, bf),
            pltpu.VMEM((length, width), bf),
            pltpu.VMEM(block, f32),
            pltpu.VMEM(block, f32),
            pltpu.VMEM(block, f32),
            pltpu.VMEM((2 * own_rows, width), f32),
            pltpu.VMEM((8, span), f32),
            pltpu.VMEM((8, 8 * span), f32),
            pltpu.VMEM((row, 8, span), f32),
            pltpu.VMEM((row, 8, span), f32),
            pltpu.VMEM((plane, 8, span), f32),
            pltpu.VMEM((plane, 8, span), f32),
            dma((row - 1,)),
            dma((row,)),
            dma((plane - 1,)),
            dma((plane - 1,)),
            dma((4,)),
            dma((3, 2)),
            dma((4,)),
            dma((4,)),
            dma((row, 1, 3)),
            dma((row, 1)),
            dma((row, 1, 3)),
            dma((row, 1)),
            dma((row, 2, 3)),
            dma((row, 2)),
            dma((4,)),
            dma((4,)),
            dma((4,)),
            dma((4,)),
            dma((row, 1, 3)),
            dma((row, 1)),
            dma((4,)),
            dma((4,)),
            dma((4,)),
            dma((4,)),
            dma((8,)),
            dma((2, chips)),
            dma((2, chips)),
            dma((2, chips)),
            dma((2, chips + 1)),
            dma((row, 1, 3)),
            dma((row, 1)),
            dma((6, 4)),
            dma((6, 4)),
            dma((3, 2)),
            dma((4,)),
            dma((row,)),
            dma((row,)),
            dma((4,)),
            dma((4,)),
            dma((4,)),
        ],
        compiler_params=pltpu.CompilerParams(
            collective_id=0, has_side_effects=True, vmem_limit_bytes=63 * 1024 * 1024
        ),
    )(x_own, cot_own, small, blocks, wo_own, fc_own, proj_own)


def block_places(own, columns, width, span):
    groups = -(-width // span)
    first, last = own_blocks(own, columns, width, span)
    place = lax.iota(jnp.int32, 4 * span)
    block, lane = first + place // span, place % span
    at = (block % groups) * span + lane
    source = (block // groups) * width + at - own * columns
    there = (block <= last) & (at < width) & (source >= 0) & (source < columns)
    return jnp.where(there, source, -1)


def joined_blocks(blocks, own, columns, width):
    span = blocks.shape[2]
    source = block_places(own, columns, width, span)
    chosen = lax.broadcasted_iota(jnp.int32, (4 * span, columns), 1) == source[:, None]
    lanes = blocks.transpose(1, 0, 2).reshape(-1, 4 * span)
    lanes = jnp.where(source[None, :] >= 0, lanes, jnp.zeros_like(lanes))
    return jnp.dot(lanes, chosen.astype(jnp.bfloat16), preferred_element_type=jnp.float32)


def column_blocks(shard, own, width, span):
    columns = shard.shape[1]
    source = block_places(own, columns, width, span)
    chosen = lax.broadcasted_iota(jnp.int32, (columns, 4 * span), 0) == source[None, :]
    cut = jnp.dot(shard, chosen.astype(jnp.bfloat16), preferred_element_type=jnp.float32)
    return cut.astype(jnp.bfloat16).reshape(-1, 4, span).transpose(1, 0, 2)


def token_plan(
    tokens,
    segment_ids,
    cotangent,
    qkv_weight,
    attn_out_weight,
    fc_weight,
    proj_weight,
    vectors,
    fc_bias,
):
    own_rows, width = tokens.shape[1], tokens.shape[2]
    parts = lax.axis_size("seq")
    own = lax.axis_index("seq")
    length = own_rows * parts
    reach = length // 2
    span = 4 * HEAD_DIM
    share = vectors.shape[1]
    units = proj_weight.shape[0]
    extra = -units % 16
    group = group_of(own)

    lines = [vectors.astype(jnp.float32), fc_bias.astype(jnp.float32)[None]]
    lines = [jnp.pad(line, ((0, 0), (0, span - share))) for line in lines]
    lines.append(jnp.pad(segment_ids.astype(jnp.float32), ((0, 4), (0, span - own_rows))))
    small = jnp.concatenate(lines)
    blocks = column_blocks(qkv_weight, own, width, span)
    fc_own = jnp.pad(fc_weight.T, ((0, extra), (0, 0)))
    proj_own = jnp.pad(proj_weight, ((0, extra), (0, 0)))

    wo_own = jnp.pad(attn_out_weight, ((0, 0), (0, span - attn_out_weight.shape[1])))
    result, input_grad, fc_terms, proj_terms, attn_terms, nat_blocks, vec_sums, *_ = block_phase(
        tokens[0].T, cotangent[0].T, small, blocks, wo_own, fc_own, proj_own, reach
    )

    def added(terms, count):
        parts = [terms[i, :count].astype(jnp.float32) for i in range(terms.shape[0])]
        return functools.reduce(jnp.add, parts)

    own_qkv = joined_blocks(nat_blocks, own, qkv_weight.shape[1], width)
    own_attn = added(attn_terms, attn_terms.shape[1])[:, : attn_out_weight.shape[1]]
    own_fc = added(fc_terms, units).T
    own_proj = added(proj_terms, units)
    own_vec = vec_sums[:2, :share]
    own_bias = vec_sums[2, :units]
    return (result[None], input_grad[None], own_qkv, own_attn, own_fc, own_proj, own_vec, own_bias)


def solution(mesh):
    in_specs = (
        P("fsdp", "seq", None),
        P("fsdp", "seq"),
        P("fsdp", "seq", None),
        P("fsdp", "seq"),
        P("fsdp", "seq"),
        P(None, ("fsdp", "seq")),
        P(("fsdp", "seq"), None),
        P("fsdp", "seq"),
        P(("fsdp", "seq")),
    )
    out_specs = (
        P("fsdp", "seq", None),
        P("fsdp", "seq", None),
        P("fsdp", "seq"),
        P("fsdp", "seq"),
        P(None, ("fsdp", "seq")),
        P(("fsdp", "seq"), None),
        P("fsdp", "seq"),
        P(("fsdp", "seq")),
    )

    def per_device(tokens, *rest):
        length = tokens.shape[1] * mesh.shape["seq"]
        fits = length * tokens.shape[2] <= resident_most
        square = mesh.shape["fsdp"] == 4 and mesh.shape["seq"] == 8
        plan = token_plan if fits and square else gathered_weights
        return plan(tokens, *rest)

    return jax.shard_map(
        per_device, mesh=mesh, in_specs=in_specs, out_specs=out_specs, check_vma=False
    )
```
